32 devices in a mesh: dp: 8 (over z, y), seq: 4 (over x, core).
Axes of the slice: x: 2, y: 2, z: 4, core: 2. Of those that a mesh axis runs over, the one named last changes fastest.
Arguments:
- cell_tokens: bfloat16 [16, 2048, 768], P('dp', 'seq'), may hold values from -6 to 6
- first_gain: float32 [2, 768], replicated, may hold values from 0.25 to 1.75
- first_bias: float32 [2, 768], replicated, may hold values from -1.75 to 1.75
- joined_weight: bfloat16 [2, 768, 2304], replicated, may hold values from -0.21875 to 0.21875
- query_value_bias: float32 [2, 1536], replicated, may hold values from -1.75 to 1.75
- output_weight: bfloat16 [2, 768, 768], replicated, may hold values from -0.875 to 0.875
- output_bias: float32 [2, 768], replicated, may hold values from -1.75 to 1.75
- second_gain: float32 [2, 768], replicated, may hold values from 0.25 to 1.75
- second_bias: float32 [2, 768], replicated, may hold values from -1.75 to 1.75
- up_weight: bfloat16 [2, 768, 3072], replicated, may hold values from -0.21875 to 0.21875
- up_bias: float32 [2, 3072], replicated, may hold values from -1.75 to 1.75
- down_weight: bfloat16 [2, 3072, 768], replicated, may hold values from -0.109375 to 0.109375
- down_bias: float32 [2, 768], replicated, may hold values from -1.75 to 1.75
- cotangent: bfloat16 [16, 2048, 768], P('dp', 'seq'), may hold values from -6 to 6
- gene_mask: int32 [16, 2048], P('dp', 'seq'), may hold values from 0 to 1, as said below
Outputs:
- block_output: float32 [16, 2048, 768], P('dp', 'seq')
- input_gradient: float32 [16, 2048, 768], P('dp', 'seq')
- first_gain_gradient: float32 [2, 768], P(None, ('dp', 'seq'))
- first_bias_gradient: float32 [2, 768], P(None, ('dp', 'seq'))
- joined_weight_gradient: float32 [2, 768, 2304], P(None, ('dp', 'seq'))
- query_value_bias_gradient: float32 [2, 1536], P(None, ('dp', 'seq'))
- output_weight_gradient: float32 [2, 768, 768], P(None, ('dp', 'seq'))
- output_bias_gradient: float32 [2, 768], P(None, ('dp', 'seq'))
- second_gain_gradient: float32 [2, 768], P(None, ('dp', 'seq'))
- second_bias_gradient: float32 [2, 768], P(None, ('dp', 'seq'))
- up_weight_gradient: float32 [2, 768, 3072], P(None, ('dp', 'seq'))
- up_bias_gradient: float32 [2, 3072], P(None, ('dp', 'seq'))
- down_weight_gradient: float32 [2, 3072, 768], P(None, ('dp', 'seq'))
- down_bias_gradient: float32 [2, 768], P(None, ('dp', 'seq'))
The draws below stay inside these ranges and needn't reach their ends.
Inputs may be any that keep to these rules, and one draw needn't show every extreme that they name: `gene_mask`: 1 marks a masked gene, 0 a visible one; the share of masked genes differs from cell to cell.
All inputs are finite; a program needn't handle non-finite values.
Results may differ from the reference program's by a relative error of at most 0.014.
Values may be sent and summed in bfloat16 or wider, within the bound.
A program may use at most 320 MiB of HBM per device.

```python
import jax
import jax.numpy as jnp
from jax import lax

D = 768
HEADS = 12
HEAD = 64
FF = 3072
GENES = 2048
LAYERS = 2
CELLS = 16


def draw_gene_mask(key, part):
    key = jax.random.fold_in(key, 7)
    rate_key, roll_key = jax.random.split(key)
    rates = jax.random.randint(rate_key, (CELLS, 1), 5, 31)
    rolls = jax.random.randint(roll_key, (CELLS, GENES), 0, 100)
    return (rolls < rates).astype(jnp.int32)


def block_scale(stream_key, dims, cuts, least, top_value):
    level, own = 1.0, jax.random.fold_in(stream_key, 6)
    for axis_at, blocks in cuts:
        heights = jnp.exp(jax.random.uniform(jax.random.fold_in(own, axis_at), (blocks,), jnp.float32, least / len(cuts), top_value / len(cuts)))
        level = level * jnp.repeat(heights, dims[axis_at] // blocks).reshape([-1 if axis == axis_at else 1 for axis in range(len(dims))])
    return level


def normal_values(stream_key, shape, scale, reach, pieces=(), dtype=jnp.bfloat16):
    factor_of = block_scale(stream_key, shape, pieces, -0.22, 0.18) if pieces else 1.0
    values = jax.random.normal(stream_key, shape, jnp.float32) * scale * factor_of
    return jnp.minimum(jnp.maximum(values, -reach), reach).astype(dtype)


def setup_inputs(seed: int = 0) -> dict:
    keys = jax.random.split(jax.random.key(seed), 16)
    return {
        "cell_tokens": normal_values(keys[0], (CELLS, GENES, D), 1.0, 6.0, ((0, 8), (1, 4))),
        "first_gain": jnp.clip(1.0 + 0.15 * jax.random.normal(keys[1], (LAYERS, D), jnp.float32), 0.25, 1.75),
        "first_bias": normal_values(keys[2], (LAYERS, D), 0.3, 1.75, (), jnp.float32),
        "joined_weight": normal_values(keys[3], (LAYERS, D, 3 * D), D ** -0.5, 0.21875),
        "query_value_bias": normal_values(keys[4], (LAYERS, 2 * D), 0.3, 1.75, (), jnp.float32),
        "output_weight": normal_values(keys[5], (LAYERS, D, D), (D // 16) ** -0.5, 0.875),
        "output_bias": normal_values(keys[6], (LAYERS, D), 0.3, 1.75, (), jnp.float32),
        "second_gain": jnp.clip(1.0 + 0.15 * jax.random.normal(keys[7], (LAYERS, D), jnp.float32), 0.25, 1.75),
        "second_bias": normal_values(keys[8], (LAYERS, D), 0.3, 1.75, (), jnp.float32),
        "up_weight": normal_values(keys[9], (LAYERS, D, FF), D ** -0.5, 0.21875),
        "up_bias": normal_values(keys[10], (LAYERS, FF), 0.3, 1.75, (), jnp.float32),
        "down_weight": normal_values(keys[11], (LAYERS, FF, D), FF ** -0.5, 0.109375),
        "down_bias": normal_values(keys[12], (LAYERS, D), 0.3, 1.75, (), jnp.float32),
        "cotangent": normal_values(keys[13], (CELLS, GENES, D), 1.0, 6.0, ((0, 8), (1, 4))),
        "gene_mask": draw_gene_mask(jax.random.fold_in(keys[15], 71), 0),
    }


@jax.custom_vjp
def low(v):
    return lax.optimization_barrier(v.astype(jnp.bfloat16)).astype(jnp.float32)

@jax.custom_vjp
def low_back(v):
    return v

def low_keep(v):
    return (low(v), None)

def low_pass(kept, grad):
    return (grad,)

def back_keep(v):
    return (v, None)

def back_low(kept, grad):
    return (low(grad),)
low.defvjp(low_keep, low_pass)
low_back.defvjp(back_keep, back_low)

def matmul(left, right):
    return jnp.dot(left, right, precision=lax.Precision.HIGHEST, preferred_element_type=jnp.float32)

def rounded(values):
    return low_back(low(values))

def layer_norm(stream, gain_row, bias_row):
    centre = lax.optimization_barrier(jnp.mean(stream, axis=-1, keepdims=True))
    shifted = stream - centre
    spread = lax.optimization_barrier(jnp.mean(shifted * shifted, axis=-1, keepdims=True))
    return shifted * lax.rsqrt(spread + 1e-05) * gain_row + bias_row

def attention(queries, key_rows, value_rows):
    scores = jnp.einsum('qhd,khd->hqk', queries, key_rows, precision=lax.Precision.HIGHEST) * HEAD ** (-0.5)
    scores = low_back(scores)
    highest = lax.optimization_barrier(jnp.max(scores, axis=-1, keepdims=True))
    exponents = jnp.exp(scores - highest)
    softmax_out = exponents / lax.optimization_barrier(jnp.sum(exponents, axis=-1, keepdims=True))
    outcome = jnp.einsum('hqk,khd->qhd', low(softmax_out), value_rows, precision=lax.Precision.HIGHEST)
    return rounded(outcome)

def layer(stream, params, layer_index):
    gain_one, bias_one, joined_mat, qv_vector, output_mat, output_vec, gain_two, bias_two, up_mat, up_vec, down_mat, down_vec = params
    model_width = stream.shape[-1]
    length = stream.shape[0]
    normed = low(layer_norm(stream, gain_one[layer_index], bias_one[layer_index]))
    qv_row = qv_vector[layer_index]
    joined_bias = jnp.concatenate([qv_row[:model_width], jnp.zeros((model_width,), jnp.float32), qv_row[model_width:]])
    joined_rows = rounded(matmul(normed, joined_mat[layer_index]) + joined_bias).reshape(length, 3, HEADS, HEAD)
    attended = jax.checkpoint(attention)(joined_rows[:, 0], joined_rows[:, 1], joined_rows[:, 2]).reshape(length, model_width)
    stream = stream + low_back(matmul(attended, output_mat[layer_index]) + output_vec[layer_index])
    normed = low(layer_norm(stream, gain_two[layer_index], bias_two[layer_index]))
    hidden = low_back(matmul(normed, up_mat[layer_index]) + up_vec[layer_index])
    active = low(jax.nn.gelu(hidden, approximate=False))
    return stream + low_back(matmul(active, down_mat[layer_index]) + down_vec[layer_index])

def reference(cell_tokens, first_gain, first_bias, joined_weight, query_value_bias, output_weight, output_bias, second_gain, second_bias, up_weight, up_bias, down_weight, down_bias, cotangent, gene_mask):
    params = tuple((weight.astype(jnp.float32) for weight in (first_gain, first_bias, joined_weight, query_value_bias, output_weight, output_bias, second_gain, second_bias, up_weight, up_bias, down_weight, down_bias)))

    def forward(stream, weights):
        for layer_index in range(LAYERS):
            stream = layer(stream, weights, layer_index)
        return stream

    def per_cell(totals, inputs):
        tokens_in, seed_rows, masked = inputs
        result, pullback = jax.vjp(forward, tokens_in.astype(jnp.float32), params)
        seeded = seed_rows.astype(jnp.float32) * masked.astype(jnp.float32)[:, None]
        input_delta, weight_deltas = pullback(seeded)
        totals = tuple((summed + addend for summed, addend in zip(totals, weight_deltas)))
        return (totals, (result, input_delta))
    zeroes = tuple((jnp.zeros_like(weight) for weight in params))
    totals, (results, input_deltas) = lax.scan(per_cell, zeroes, (cell_tokens, cotangent, gene_mask))
    return (results, input_deltas, totals[0], totals[1], totals[2], totals[3], totals[4], totals[5], totals[6], totals[7], totals[8], totals[9], totals[10], totals[11])
```

```python
import functools

import jax
import jax.numpy as jnp
from jax import lax
from jax.experimental import pallas as pl
from jax.experimental.pallas import tpu as pltpu
from jax.sharding import PartitionSpec as P

HEAD = 64
LOG2E = 1.4426950408889634
BF = jnp.bfloat16
F32 = jnp.float32
NN = ((1,), (0,))
NT = ((1,), (1,))
SAFE = 80.0


def dot(a, b, dims):
    return lax.dot_general(a, b, (dims, ((), ())), preferred_element_type=F32)


def params(mib):
    return pltpu.CompilerParams(vmem_limit_bytes=mib << 20)


def row(index):
    return pl.BlockSpec((1, index[1]), lambda *_: (index[0], 0))


def normalise(x):
    n = x.shape[-1]
    centred = x - jnp.sum(x, axis=-1, keepdims=True) * (1.0 / n)
    inverse = lax.rsqrt(jnp.sum(centred * centred, axis=-1, keepdims=True) * (1.0 / n) + 1e-05)
    return centred * inverse, inverse


def norm_back(upstream, gain, unit, inverse):
    n = unit.shape[-1]
    e = upstream * gain
    mean_e = jnp.sum(e, axis=-1, keepdims=True) * (1.0 / n)
    mean_eu = jnp.sum(e * unit, axis=-1, keepdims=True) * (1.0 / n)
    return inverse * (e - mean_e - unit * mean_eu)


def column_sum(x):
    return jnp.sum(x, axis=0, keepdims=True)


def gelu_pair(x):
    a = jnp.abs(x)
    base = 1.0 + 0.23164190 * a
    t = pl.reciprocal(base, approx=True)
    t = t * (2.0 - base * t)
    poly = t * (0.127414796 + t * (-0.142248368 + t * (0.7107068705 + t * (-0.7265760135 + t * 0.5307027145))))
    u = jnp.exp2(x * x * (-0.5 * LOG2E))
    half = poly * u
    cdf = jnp.where(x >= 0, 1.0 - half, half)
    return x * cdf, cdf + x * (u * 0.3989422804014327)


def qkv_tile(x, gain, bias, weight, row_bias, normed_ref, q_ref, kv_ref):
    d = x.shape[-1]
    unit, _ = normalise(x)
    normed = (unit * gain + bias).astype(BF)
    normed_ref[...] = normed
    for part in range(3):
        cols = slice(part * d, (part + 1) * d)
        out = dot(normed, weight[:, cols], NN)
        if part != 1:
            out = out + row_bias[:, cols]
        if part == 0:
            q_ref[...] = out.astype(BF)
        else:
            kv_ref[part - 1] = out.astype(BF)


def first_kernel(x, gain, bias, weight, row_bias, normed, q, kv):
    qkv_tile(x[...].astype(F32), gain[...], bias[...], weight, row_bias, normed, q, kv)


def first_call(x, layer, gain, bias, weight, row_bias, tile):
    t, d = x.shape
    return pl.pallas_call(
        first_kernel,
        grid=(t // tile,),
        in_specs=[
            pl.BlockSpec((tile, d), lambda i: (i, 0)),
            pl.BlockSpec((None, 1, d), lambda i: (layer, 0, 0)),
            pl.BlockSpec((None, 1, d), lambda i: (layer, 0, 0)),
            pl.BlockSpec((None, d, 3 * d), lambda i: (layer, 0, 0)),
            pl.BlockSpec((None, 1, 3 * d), lambda i: (layer, 0, 0)),
        ],
        out_specs=[
            pl.BlockSpec((tile, d), lambda i: (i, 0)),
            pl.BlockSpec((tile, d), lambda i: (i, 0)),
            pl.BlockSpec((2, tile, d), lambda i: (0, i, 0)),
        ],
        out_shape=[
            jax.ShapeDtypeStruct((t, d), BF),
            jax.ShapeDtypeStruct((t, d), BF),
            jax.ShapeDtypeStruct((2, t, d), BF),
        ],
        compiler_params=params(56),
        name="norm_qkv",
    )(x, gain, bias, weight, row_bias)


def attend_kernel(q, kv, kvo, out, lse, *, chunk):
    t = q.shape[0]
    c = LOG2E * HEAD**-0.5
    lane = lax.broadcasted_iota(jnp.int32, (128, 128), 0) // HEAD
    pick = (lane == lax.broadcasted_iota(jnp.int32, (128, 128), 1)).astype(BF)

    def squares(x):
        x = x.astype(F32)
        return jnp.max(dot((x * x).astype(BF), pick, NN), axis=0, keepdims=True)

    bound = squares(q[...]) * jnp.maximum(squares(kv[0]), squares(kvo[0]))
    fast = jnp.max(bound) * (c * c * 1.05) < SAFE * SAFE

    def run(stable):
        for head in range(2):
            ls = slice(HEAD * head, HEAD * head + HEAD)
            values = []
            for ref in (kv, kvo):
                v = ref[1, :, ls].astype(F32).T.astype(BF)
                values.append(jnp.concatenate([v, jnp.ones((16, t), BF)], axis=0))

            def score(j):
                block = q[j * chunk : (j + 1) * chunk, ls]
                return [dot(ref[0, :, ls], block, NT) for ref in (kv, kvo)]

            ahead = score(0)
            for j in range(t // chunk):
                s = ahead
                if j + 1 < t // chunk:
                    ahead = score(j + 1)
                if stable:
                    shift = c * jnp.maximum(
                        jnp.max(s[0], axis=0, keepdims=True), jnp.max(s[1], axis=0, keepdims=True)
                    )
                    p = [jnp.exp2(x * c - shift).astype(BF) for x in s]
                else:
                    shift = 0.0
                    p = [jnp.exp2(x * c).astype(BF) for x in s]
                total = dot(values[0], p[0], NN) + dot(values[1], p[1], NN)
                level = total[HEAD : HEAD + 1]
                cols = slice(j * chunk, (j + 1) * chunk)
                out[cols, ls] = (total[:HEAD] / level).T.astype(BF)
                lse[0, head : head + 1, cols] = shift + jnp.log2(level)

    pl.when(fast)(lambda: run(False))
    pl.when(jnp.logical_not(fast))(lambda: run(True))


def attend_call(q, kv, kvo):
    t, d = q.shape
    pairs = d // 128
    both = pl.BlockSpec((2, t, 128), lambda h: (0, 0, h))
    one = pl.BlockSpec((t, 128), lambda h: (0, h))
    return pl.pallas_call(
        functools.partial(attend_kernel, chunk=min(256, t)),
        grid=(pairs,),
        in_specs=[one, both, both],
        out_specs=[one, pl.BlockSpec((1, 8, t), lambda h: (h, 0, 0))],
        out_shape=[jax.ShapeDtypeStruct((t, d), BF), jax.ShapeDtypeStruct((pairs, 8, t), F32)],
        compiler_params=params(56),
        name="attend",
    )(q, kv, kvo)


def attend_back_kernel(q, kv, kvo, up, out, lse, dq, dkv, dkvo, *, chunk):
    t = q.shape[0]
    scale = HEAD**-0.5
    c = LOG2E * scale
    for head in range(2):
        ls = slice(HEAD * head, HEAD * head + HEAD)
        qh = q[:, ls]
        uh = up[:, ls]
        q_t = qh.astype(F32).T.astype(BF)
        u_t = uh.astype(F32).T.astype(BF)
        level = lse[0].T[:, head : head + 1]
        inner = jnp.sum(uh.astype(F32) * out[:, ls].astype(F32), axis=1, keepdims=True)
        blocks = [
            (src, dst, slice(i * chunk, (i + 1) * chunk))
            for src, dst in ((kvo, dkvo), (kv, dkv))
            for i in range(t // chunk)
        ]

        def products(block):
            src, _, rows = block
            return dot(qh, src[0, rows, ls], NT), dot(uh, src[1, rows, ls], NT)

        total = None
        ahead = products(blocks[0])
        for at, (src, dst, rows) in enumerate(blocks):
            s, dp = ahead
            if at + 1 < len(blocks):
                ahead = products(blocks[at + 1])
            p = jnp.exp2(s * c - level)
            ds = (p * (dp - inner)).astype(BF)
            dst[1, rows, ls] = dot(u_t, p.astype(BF), NN).T.astype(BF)
            dst[0, rows, ls] = (dot(q_t, ds, NN).T * scale).astype(BF)
            part = dot(ds, src[0, rows, ls], NN)
            total = part if total is None else total + part
        dq[:, ls] = (total * scale).astype(BF)


def attend_back_call(q, kv, kvo, up, out, lse):
    t, d = q.shape
    pairs = d // 128
    both = pl.BlockSpec((2, t, 128), lambda h: (0, 0, h))
    one = pl.BlockSpec((t, 128), lambda h: (0, h))
    return pl.pallas_call(
        functools.partial(attend_back_kernel, chunk=min(256, t)),
        grid=(pairs,),
        in_specs=[one, both, both, one, one, pl.BlockSpec((1, 8, t), lambda h: (h, 0, 0))],
        out_specs=[one, both, both],
        out_shape=[
            jax.ShapeDtypeStruct((t, d), BF),
            jax.ShapeDtypeStruct((2, t, d), BF),
            jax.ShapeDtypeStruct((2, t, d), BF),
        ],
        compiler_params=params(56),
        name="attend_back",
    )(q, kv, kvo, up, out, lse)


def forward_kernel(
    att, x, wo_h, wu_h, wd_h, bo, g2, b2, bu, bd, middle_o, n2_o, act_o, slope_o, next_o, wo, wu, wd, sems, *, layer, cut
):
    first = pl.program_id(0) == 0
    copies = [
        pltpu.make_async_copy(src.at[layer], dst, sems.at[i])
        for i, (src, dst) in enumerate(((wo_h, wo), (wu_h, wu), (wd_h, wd)))
    ]

    @pl.when(first)
    def _():
        for copy in copies:
            copy.start()
        copies[0].wait()

    middle = x[...].astype(F32) + (dot(att[...], wo[...], NN) + bo[...])
    middle_o[...] = middle
    unit, _ = normalise(middle)
    n2 = (unit * g2[...] + b2[...]).astype(BF)
    n2_o[...] = n2

    @pl.when(first)
    def _():
        copies[1].wait()
        copies[2].wait()

    ff = wu.shape[1]
    count = ff // cut

    def up(j):
        cols = slice(j * cut, (j + 1) * cut)
        return dot(n2, wu[:, cols], NN) + bu[:, cols]

    ahead = up(0)
    total = None
    for j in range(count):
        hidden = ahead
        if j + 1 < count:
            ahead = up(j + 1)
        cols = slice(j * cut, (j + 1) * cut)
        act, slope = gelu_pair(hidden)
        act = act.astype(BF)
        act_o[:, cols] = act
        slope_o[:, cols] = slope.astype(BF)
        part = dot(act, wd[cols, :], NN)
        total = part if total is None else total + part
    next_o[...] = middle + (total + bd[...])


def forward_call(att, x, layer, wo, wu, wd, bo, g2, b2, bu, bd, tile):
    t, d = att.shape
    ff = wu.shape[2]
    tok = pl.BlockSpec((tile, d), lambda i: (i, 0))
    wide = pl.BlockSpec((tile, ff), lambda i: (i, 0))
    vec = pl.BlockSpec((None, 1, d), lambda i: (layer, 0, 0))
    vec_ff = pl.BlockSpec((None, 1, ff), lambda i: (layer, 0, 0))
    hbm = pl.BlockSpec(memory_space=pl.ANY)
    return pl.pallas_call(
        functools.partial(forward_kernel, layer=layer, cut=512),
        grid=(t // tile,),
        in_specs=[tok, tok, hbm, hbm, hbm, vec, vec, vec, vec_ff, vec],
        out_specs=[tok, tok, wide, wide, tok],
        out_shape=[
            jax.ShapeDtypeStruct((t, d), F32),
            jax.ShapeDtypeStruct((t, d), BF),
            jax.ShapeDtypeStruct((t, ff), BF),
            jax.ShapeDtypeStruct((t, ff), BF),
            jax.ShapeDtypeStruct((t, d), F32),
        ],
        scratch_shapes=[
            pltpu.VMEM((d, d), BF),
            pltpu.VMEM((d, ff), BF),
            pltpu.VMEM((ff, d), BF),
            pltpu.SemaphoreType.DMA((3,)),
        ],
        compiler_params=params(58),
        name="feed_forward",
    )(att, x, wo, wu, wd, bo, g2, b2, bu, bd)


def add_row(ref, at, value, first):
    ref[at : at + 1, :] = jnp.where(first, 0.0, ref[at : at + 1, :]) + value


def backward_kernel(
    g, slope, middle, wo_h, wu_h, wd_h, g2, dz_o, dh_o, dm_o, dy_o, da_o, sums, sums_ff, wo, wu, wd, sems, *, layer, cut
):
    first = pl.program_id(0) == 0
    copies = [
        pltpu.make_async_copy(src.at[layer], dst, sems.at[i])
        for i, (src, dst) in enumerate(((wd_h, wd), (wu_h, wu), (wo_h, wo)))
    ]

    @pl.when(first)
    def _():
        for copy in copies:
            copy.start()
        sums[...] = jnp.zeros_like(sums)
        sums_ff[...] = jnp.zeros_like(sums_ff)
        copies[0].wait()
        copies[1].wait()

    dz = g[...].astype(BF)
    dz_o[...] = dz
    sums[0:1, :] += column_sum(dz.astype(F32))
    ff = wu.shape[1]
    count = ff // cut

    def spread(j):
        return dot(dz, wd[j * cut : (j + 1) * cut, :], NT)

    ahead = spread(0)
    total = None
    for j in range(count):
        da = ahead
        if j + 1 < count:
            ahead = spread(j + 1)
        cols = slice(j * cut, (j + 1) * cut)
        dh = (da * slope[:, cols].astype(F32)).astype(BF)
        dh_o[:, cols] = dh
        sums_ff[0:1, cols] += column_sum(dh.astype(F32))
        part = dot(dh, wu[:, cols], NT)
        total = part if total is None else total + part
    unit, inverse = normalise(middle[...])
    sums[1:2, :] += column_sum(total * unit)
    sums[2:3, :] += column_sum(total)
    dm = g[...].astype(F32) + norm_back(total, g2[...], unit, inverse)
    dm_o[...] = dm
    dy = dm.astype(BF)
    dy_o[...] = dy
    sums[3:4, :] += column_sum(dy.astype(F32))

    @pl.when(first)
    def _():
        copies[2].wait()

    da_o[...] = dot(dy, wo[...], NT).astype(BF)


def backward_call(g, slope, middle, layer, wo, wu, wd, g2, tile):
    t, d = middle.shape
    ff = wu.shape[2]
    tok = pl.BlockSpec((tile, d), lambda i: (i, 0))
    wide = pl.BlockSpec((tile, ff), lambda i: (i, 0))
    vec = pl.BlockSpec((None, 1, d), lambda i: (layer, 0, 0))
    hbm = pl.BlockSpec(memory_space=pl.ANY)
    return pl.pallas_call(
        functools.partial(backward_kernel, layer=layer, cut=512),
        grid=(t // tile,),
        in_specs=[tok, wide, tok, hbm, hbm, hbm, vec],
        out_specs=[
            tok,
            wide,
            tok,
            tok,
            tok,
            pl.BlockSpec((8, d), lambda i: (0, 0)),
            pl.BlockSpec((8, ff), lambda i: (0, 0)),
        ],
        out_shape=[
            jax.ShapeDtypeStruct((t, d), BF),
            jax.ShapeDtypeStruct((t, ff), BF),
            jax.ShapeDtypeStruct((t, d), F32),
            jax.ShapeDtypeStruct((t, d), BF),
            jax.ShapeDtypeStruct((t, d), BF),
            jax.ShapeDtypeStruct((8, d), F32),
            jax.ShapeDtypeStruct((8, ff), F32),
        ],
        scratch_shapes=[
            pltpu.VMEM((d, d), BF),
            pltpu.VMEM((d, ff), BF),
            pltpu.VMEM((ff, d), BF),
            pltpu.SemaphoreType.DMA((3,)),
        ],
        compiler_params=params(58),
        name="feed_forward_back",
    )(g, slope, middle, wo, wu, wd, g2)


def joined_back_kernel(dq, dkv, dkv_in, x, dm, weight, gain, df_o, g_o, sums):
    d = dq.shape[-1]

    @pl.when(pl.program_id(0) == 0)
    def _():
        sums[...] = jnp.zeros_like(sums)

    parts = [dq[...]]
    for i in range(2):
        parts.append((dkv[i].astype(F32) + dkv_in[i].astype(F32)).astype(BF))
    total = None
    for i, part in enumerate(parts):
        cols = slice(i * d, (i + 1) * d)
        df_o[:, cols] = part
        piece = dot(part, weight[:, cols], NT)
        total = piece if total is None else total + piece
    sums[2:3, :] += column_sum(parts[0].astype(F32))
    sums[3:4, :] += column_sum(parts[2].astype(F32))
    unit, inverse = normalise(x[...].astype(F32))
    sums[0:1, :] += column_sum(total * unit)
    sums[1:2, :] += column_sum(total)
    g_o[...] = dm[...] + norm_back(total, gain[...], unit, inverse)


def joined_back_call(dq, dkv, dkv_in, x, dm, layer, weight, gain, tile):
    t, d = dq.shape
    tok = pl.BlockSpec((tile, d), lambda i: (i, 0))
    both = pl.BlockSpec((2, tile, d), lambda i: (0, i, 0))
    return pl.pallas_call(
        joined_back_kernel,
        grid=(t // tile,),
        in_specs=[
            tok,
            both,
            both,
            tok,
            tok,
            pl.BlockSpec((None, d, 3 * d), lambda i: (layer, 0, 0)),
            pl.BlockSpec((None, 1, d), lambda i: (layer, 0, 0)),
        ],
        out_specs=[
            pl.BlockSpec((tile, 3 * d), lambda i: (i, 0)),
            tok,
            pl.BlockSpec((8, d), lambda i: (0, 0)),
        ],
        out_shape=[
            jax.ShapeDtypeStruct((t, 3 * d), BF),
            jax.ShapeDtypeStruct((t, d), F32),
            jax.ShapeDtypeStruct((8, d), F32),
        ],
        compiler_params=params(56),
        name="joined_back",
    )(dq, dkv, dkv_in, x, dm, weight, gain)


def weight_grad_kernel(core, a, b, keep, send, turned, *, rows, fixed_a):
    def turn():
        turned[...] = a[...].astype(F32).T.astype(BF)

    if fixed_a:
        pl.when(pl.program_id(0) == 0)(turn)
    else:
        turn()
    out = dot(turned[...], b[...], NN)
    n, cols = out.shape
    even = jnp.concatenate([out[i : i + rows] for i in range(0, n, 2 * rows)], axis=0).astype(BF)
    odd = jnp.concatenate([out[i + rows : i + 2 * rows] for i in range(0, n, 2 * rows)], axis=0).astype(BF)

    @pl.when(core[0] == 0)
    def _():
        keep[...] = even
        send[...] = odd

    @pl.when(core[0] == 1)
    def _():
        keep[...] = odd
        send[...] = even


def weight_grad_call(core, a, b, chunks, block):
    t, n = a.shape
    cols = b.shape[1]
    fixed_a = n == block
    steps = cols // block if fixed_a else n // block
    half = block // 2
    if fixed_a:
        a_at, b_at, o_at = (lambda i: (0, 0)), (lambda i: (0, i)), (lambda i: (0, i))
    else:
        a_at, b_at, o_at = (lambda i: (0, i)), (lambda i: (0, 0)), (lambda i: (i, 0))
    shape = jax.ShapeDtypeStruct((n // 2, cols), BF)
    keep, send = pl.pallas_call(
        functools.partial(weight_grad_kernel, rows=n // chunks, fixed_a=fixed_a),
        grid=(steps,),
        in_specs=[
            pl.BlockSpec(memory_space=pltpu.SMEM),
            pl.BlockSpec((t, block), a_at),
            pl.BlockSpec((t, block), b_at),
        ],
        out_specs=[pl.BlockSpec((half, block), o_at)] * 2,
        out_shape=[shape, shape],
        scratch_shapes=[pltpu.VMEM((block, t), BF)],
        compiler_params=params(56),
        name="weight_grad",
    )(core, a, b)
    split = (chunks // 2, n // chunks, cols)
    return keep.reshape(split), send.reshape(split)


def flip(device_count, bit):
    return [(i, i ^ (1 << bit)) for i in range(device_count)]


class Reducer:
    def __init__(self, device_count, index):
        self.count, self.index = device_count, index
        self.bits = device_count.bit_length() - 1

    def swap(self, array, bit):
        return lax.ppermute(array, ("dp", "seq"), flip(self.count, bit))

    def begin(self, keep, send):
        return [keep, self.swap(send, 0)], list(range(self.bits - 1, 0, -1))

    def half(self, terms, bits, bit, which):
        at = bits.index(bit)
        out = []
        for term in terms:
            n = term.shape[0]
            lo = 1 << (len(bits) - 1 - at)
            view = term.reshape(n // (2 * lo), 2, lo, *term.shape[1:])
            out.append(lax.dynamic_index_in_dim(view, which, 1, keepdims=False).reshape(n // 2, *term.shape[1:]))
        return out

    def run(self, terms, bits, order, dtype):
        for bit in order:
            mine = (self.index >> bit) & 1
            total = sum(t.astype(F32) for t in self.half(terms, bits, bit, 1 - mine)).astype(dtype)
            kept = self.half(terms, bits, bit, mine)
            terms = [sum(t.astype(F32) for t in kept).astype(dtype), self.swap(total, bit)]
            bits = [b for b in bits if b != bit]
        return sum(t.astype(F32) for t in terms)[0]

    def small(self, rows):
        flat = jnp.concatenate([r.reshape(self.count, -1) for r in rows], axis=1)[:, None, :]
        width = flat.shape[2]
        pad = -width % 128
        flat = jnp.pad(flat, ((0, 0), (0, 0), (0, pad)))
        bits = list(range(self.bits - 1, -1, -1))
        return self.run([flat], bits, list(range(self.bits)), F32)[0, :width]


def on_device(
    device_count,
    cell_tokens,
    first_gain,
    first_bias,
    joined_weight,
    query_value_bias,
    output_weight,
    output_bias,
    second_gain,
    second_bias,
    up_weight,
    up_bias,
    down_weight,
    down_bias,
    cotangent,
    gene_mask,
):
    _, genes, d = cell_tokens.shape
    layers = joined_weight.shape[0]
    seq = lax.axis_index("seq")
    index = lax.axis_index("dp") * 4 + seq
    chip, core = seq // 2, seq % 2
    core_ref = core.astype(jnp.int32).reshape(1)
    across = [(0, 2), (1, 3), (2, 0), (3, 1)]
    beside = [(0, 1), (1, 0), (2, 3), (3, 2)]
    tile = genes
    reducer = Reducer(device_count, index)

    def rows(v):
        return v[:, None, :]

    def trade(pair):
        mine = lax.dynamic_index_in_dim(pair, chip, 0, keepdims=False)
        other = lax.dynamic_index_in_dim(pair, 1 - chip, 0, keepdims=False)
        return jnp.concatenate([mine, lax.ppermute(other, "seq", across)], axis=0)

    def trade_back(held):
        own = held[:genes]
        got = lax.ppermute(held[genes:].astype(BF), "seq", across).astype(F32)
        return jnp.where(chip == 0, jnp.stack([own, got]), jnp.stack([got, own]))

    g1, b1 = rows(first_gain), rows(first_bias)
    g2, b2 = rows(second_gain), rows(second_bias)
    bo, bu, bd = rows(output_bias), rows(up_bias), rows(down_bias)
    qkv_bias = rows(
        jnp.concatenate(
            [query_value_bias[:, :d], jnp.zeros((layers, d), F32), query_value_bias[:, d:]], axis=1
        )
    )

    x = trade(cell_tokens)
    seeded = cotangent * gene_mask.astype(BF)[:, :, None]
    g = trade(seeded)

    saved = []
    for layer in range(layers):
        normed, q, kv = first_call(x, layer, g1, b1, joined_weight, qkv_bias, tile)
        kvo = lax.ppermute(kv, "seq", beside)
        att, lse = attend_call(q, kv, kvo)
        middle, n2, act, slope, following = forward_call(
            att, x, layer, output_weight, up_weight, down_weight, bo, g2, b2, bu, bd, tile
        )
        saved.append((x, normed, q, kv, kvo, att, lse, middle, n2, act, slope))
        x = following
    block_output = trade_back(x)

    chunks = device_count
    grads = [None] * layers
    vectors = [None] * layers
    dp_bits = list(range(2, reducer.bits))
    for layer in reversed(range(layers)):
        x, normed, q, kv, kvo, att, lse, middle, n2, act, slope = saved[layer]
        dz, dh, dm, dy, da, sums, sums_ff = backward_call(
            g, slope, middle, layer, output_weight, up_weight, down_weight, g2, tile
        )
        w_down = reducer.begin(*weight_grad_call(core_ref, act, dz, chunks, d))
        w_up = reducer.begin(*weight_grad_call(core_ref, n2, dh, chunks, d))
        w_out = reducer.begin(*weight_grad_call(core_ref, att, dy, chunks, d))
        dq, dkv, dkvo = attend_back_call(q, kv, kvo, da, att, lse)
        dkv_in = lax.ppermute(dkvo, "seq", beside)
        df, g, sums_in = joined_back_call(dq, dkv, dkv_in, x, dm, layer, joined_weight, g1, tile)
        w_joined = reducer.begin(*weight_grad_call(core_ref, normed, df, chunks, d))
        grads[layer] = [
            reducer.run(*w_joined, dp_bits + [1], BF),
            reducer.run(*w_out, dp_bits + [1], BF),
            reducer.run(*w_up, [1] + dp_bits, BF),
            reducer.run(*w_down, dp_bits + [1], BF),
        ]
        vectors[layer] = [
            sums_in[0],
            sums_in[1],
            sums_in[2],
            sums_in[3],
            sums[3],
            sums[1],
            sums[2],
            sums_ff[0],
            sums[0],
        ]
    input_gradient = trade_back(g)

    qv = [jnp.concatenate([v[2], v[3]]) for v in vectors]
    plain = [0, 1, 4, 5, 6, 8]
    rows_out = [vectors[l][i] for l in range(layers) for i in plain]
    rows_out += qv + [v[7] for v in vectors]
    summed = reducer.small(rows_out)
    piece = d // device_count
    at = 0
    small = {}
    for l in range(layers):
        for i in plain:
            small[l, i] = summed[at : at + piece]
            at += piece
    for key, width in (("qv", 2 * piece), ("up", up_bias.shape[1] // device_count)):
        for l in range(layers):
            small[l, key] = summed[at : at + width]
            at += width

    def vec(key):
        return jnp.stack([small[l, key] for l in range(layers)])

    def mat(i):
        return jnp.stack([grads[l][i] for l in range(layers)])

    return (
        block_output,
        input_gradient,
        vec(0),
        vec(1),
        mat(0),
        vec("qv"),
        mat(1),
        vec(4),
        vec(5),
        vec(6),
        mat(2),
        vec("up"),
        mat(3),
        vec(8),
    )


def solution(mesh):
    split = P(None, ("dp", "seq"))
    split_rows = P(None, ("dp", "seq"), None)
    tokens = P("dp", "seq", None)
    return jax.shard_map(
        functools.partial(on_device, mesh.size),
        mesh=mesh,
        in_specs=(tokens,) + (P(),) * 12 + (tokens, P("dp", "seq")),
        out_specs=(
            tokens,
            tokens,
            split,
            split,
            split_rows,
            split,
            split_rows,
            split,
            split,
            split,
            split_rows,
            split,
            split_rows,
            split,
        ),
        check_vma=False,
    )
```

```python
import functools

import jax
import jax.numpy as jnp
from jax import lax
from jax.experimental import pallas as pl
from jax.experimental.pallas import tpu as pltpu
from jax.sharding import PartitionSpec as P

HEAD = 64
LOG2E = 1.4426950408889634
BF = jnp.bfloat16
F32 = jnp.float32
NN = ((1,), (0,))
NT = ((1,), (1,))
SAFE = 80.0


def dot(a, b, dims):
    return lax.dot_general(a, b, (dims, ((), ())), preferred_element_type=F32)


def params(mib):
    return pltpu.CompilerParams(vmem_limit_bytes=mib << 20)


def cost(products, nbytes=0):
    return pl.CostEstimate(flops=int(2 * products), bytes_accessed=int(nbytes), transcendentals=0)


def normalise(x):
    n = x.shape[-1]
    centred = x - jnp.sum(x, axis=-1, keepdims=True) * (1.0 / n)
    inverse = lax.rsqrt(jnp.sum(centred * centred, axis=-1, keepdims=True) * (1.0 / n) + 1e-05)
    return centred * inverse, inverse


def norm_back(upstream, gain, unit, inverse):
    n = unit.shape[-1]
    e = upstream * gain
    mean_e = jnp.sum(e, axis=-1, keepdims=True) * (1.0 / n)
    mean_eu = jnp.sum(e * unit, axis=-1, keepdims=True) * (1.0 / n)
    return inverse * (e - mean_e - unit * mean_eu)


def column_sum(x):
    return jnp.sum(x, axis=0, keepdims=True)


def gelu_pair(x):
    a = jnp.abs(x)
    base = 1.0 + 0.23164190 * a
    t = pl.reciprocal(base, approx=True)
    t = t * (2.0 - base * t)
    poly = t * (0.127414796 + t * (-0.142248368 + t * (0.7107068705 + t * (-0.7265760135 + t * 0.5307027145))))
    u = jnp.exp2(x * x * (-0.5 * LOG2E))
    half = poly * u
    cdf = jnp.where(x >= 0, 1.0 - half, half)
    return x * cdf, cdf + x * (u * 0.3989422804014327)


def kernel_call(kernel, ins, in_specs, after=(), **kwargs):
    n = len(ins)
    extra = [pl.BlockSpec(memory_space=pl.ANY)] * len(after)

    def body(*refs):
        kernel(*refs[:n], *refs[n + len(after) :])

    return pl.pallas_call(body, in_specs=list(in_specs) + extra, **kwargs)(*ins, *after)


def qkv_tile(x, gain, bias, weight, row_bias, normed_ref, q_ref, kv_ref):
    d = x.shape[-1]
    unit, _ = normalise(x)
    normed = (unit * gain + bias).astype(BF)
    normed_ref[...] = normed
    for part in range(3):
        cols = slice(part * d, (part + 1) * d)
        out = dot(normed, weight[:, cols], NN)
        if part != 1:
            out = out + row_bias[:, cols]
        if part == 0:
            q_ref[...] = out.astype(BF)
        else:
            kv_ref[part - 1] = out.astype(BF)


def first_kernel(x, gain, bias, weight, row_bias, normed, q, kv):
    qkv_tile(x[...].astype(F32), gain[...], bias[...], weight, row_bias, normed, q, kv)


def first_call(x, layer, gain, bias, weight, row_bias, tile):
    t, d = x.shape
    return pl.pallas_call(
        first_kernel,
        grid=(t // tile,),
        in_specs=[
            pl.BlockSpec((tile, d), lambda i: (i, 0)),
            pl.BlockSpec((None, 1, d), lambda i: (layer, 0, 0)),
            pl.BlockSpec((None, 1, d), lambda i: (layer, 0, 0)),
            pl.BlockSpec((None, d, 3 * d), lambda i: (layer, 0, 0)),
            pl.BlockSpec((None, 1, 3 * d), lambda i: (layer, 0, 0)),
        ],
        out_specs=[
            pl.BlockSpec((tile, d), lambda i: (i, 0)),
            pl.BlockSpec((tile, d), lambda i: (i, 0)),
            pl.BlockSpec((2, tile, d), lambda i: (0, i, 0)),
        ],
        out_shape=[
            jax.ShapeDtypeStruct((t, d), BF),
            jax.ShapeDtypeStruct((t, d), BF),
            jax.ShapeDtypeStruct((2, t, d), BF),
        ],
        compiler_params=params(56),
        cost_estimate=cost(4.6e9),
        name="norm_qkv",
    )(x, gain, bias, weight, row_bias)


def attend_kernel(q, kv, kvo, out, lse, *, chunk):
    t = q.shape[0]
    c = LOG2E * HEAD**-0.5
    lane = lax.broadcasted_iota(jnp.int32, (128, 128), 0) // HEAD
    pick = (lane == lax.broadcasted_iota(jnp.int32, (128, 128), 1)).astype(BF)

    def squares(x):
        x = x.astype(F32)
        return jnp.max(dot((x * x).astype(BF), pick, NN), axis=0, keepdims=True)

    bound = squares(q[...]) * jnp.maximum(squares(kv[0]), squares(kvo[0]))
    fast = jnp.max(bound) * (c * c * 1.05) < SAFE * SAFE

    def run(stable):
        for head in range(2):
            ls = slice(HEAD * head, HEAD * head + HEAD)
            values = []
            for ref in (kv, kvo):
                v = ref[1, :, ls].astype(F32).T.astype(BF)
                values.append(jnp.concatenate([v, jnp.ones((16, t), BF)], axis=0))

            def score(j):
                block = q[j * chunk : (j + 1) * chunk, ls]
                return [dot(ref[0, :, ls], block, NT) for ref in (kv, kvo)]

            ahead = score(0)
            for j in range(t // chunk):
                s = ahead
                if j + 1 < t // chunk:
                    ahead = score(j + 1)
                if stable:
                    shift = c * jnp.maximum(
                        jnp.max(s[0], axis=0, keepdims=True), jnp.max(s[1], axis=0, keepdims=True)
                    )
                    p = [jnp.exp2(x * c - shift).astype(BF) for x in s]
                else:
                    shift = 0.0
                    p = [jnp.exp2(x * c).astype(BF) for x in s]
                total = dot(values[0], p[0], NN) + dot(values[1], p[1], NN)
                level = total[HEAD : HEAD + 1]
                cols = slice(j * chunk, (j + 1) * chunk)
                out[cols, ls] = (total[:HEAD] / level).T.astype(BF)
                lse[0, head : head + 1, cols] = shift + jnp.log2(level)

    pl.when(fast)(lambda: run(False))
    pl.when(jnp.logical_not(fast))(lambda: run(True))


def attend_call(q, kv, kvo):
    t, d = q.shape
    pairs = d // 128
    both = pl.BlockSpec((2, t, 128), lambda h: (0, 0, h))
    one = pl.BlockSpec((t, 128), lambda h: (0, h))
    return pl.pallas_call(
        functools.partial(attend_kernel, chunk=min(256, t)),
        grid=(pairs,),
        in_specs=[one, both, both],
        out_specs=[one, pl.BlockSpec((1, 8, t), lambda h: (h, 0, 0))],
        out_shape=[jax.ShapeDtypeStruct((t, d), BF), jax.ShapeDtypeStruct((pairs, 8, t), F32)],
        compiler_params=params(56),
        cost_estimate=cost(16e9),
        name="attend",
    )(q, kv, kvo)


class Place:
    def __init__(self, count):
        self.count = count
        self.bits = count.bit_length() - 1
        self.dp, self.seq = lax.axis_index("dp"), lax.axis_index("seq")

    def bit(self, b):
        return (self.seq // (1 << b)) % 2 if b < 2 else (self.dp // (1 << (b - 2))) % 2

    def partner(self, b):
        step = 1 - 2 * self.bit(b)
        if b < 2:
            return {"dp": self.dp, "seq": self.seq + step * (1 << b)}
        return {"dp": self.dp + step * (1 << (b - 2)), "seq": self.seq}

    def greet(self):
        barrier = pltpu.get_barrier_semaphore()
        for b in range(self.bits):
            pl.semaphore_signal(barrier, inc=1, device_id=self.partner(b), device_id_type=pl.DeviceIdType.MESH)
        pl.semaphore_wait(barrier, self.bits)


class Job:
    def __init__(self, keep, send, count, orders):
        self.lead = count.bit_length() - 2
        self.keep = keep.reshape((2,) * self.lead + keep.shape[1:])
        self.send = send.reshape((2,) * self.lead + send.shape[1:])
        self.rows, self.cols = keep.shape[1:]
        self.orders = orders
        self.wide = self.cols // len(orders)
        self.dtype = keep.dtype

    def scratch(self):
        out = []
        for _ in self.orders:
            block = (self.rows, self.wide)
            out.append(pltpu.VMEM((2,) * self.lead + block, self.dtype))
            for left in range(self.lead, -1, -1):
                out.append(pltpu.VMEM((2,) * left + block, self.dtype))
        return out

    def out_shape(self):
        return jax.ShapeDtypeStruct((self.rows, self.cols), F32)


class Part:
    def __init__(self, place, job, at, keep, send, out, scratch, sems, first_sem):
        self.place, self.job, self.keep, self.send, self.out = place, job, keep, send, out
        self.order = job.orders[at]
        self.cols = slice(at * job.wide, (at + 1) * job.wide)
        self.total, self.got = scratch[0], scratch[1:]
        self.sems, self.first = sems, first_sem

    def own(self):
        return pltpu.make_async_copy(
            self.keep.at[(slice(None),) * (self.job.lead + 1) + (self.cols,)], self.total, self.sems.at[0, self.first]
        )

    def index(self, stage, away):
        out = []
        for b in range(self.job.lead, 0, -1):
            at = self.order.index(b) + 1
            if at < stage or (at == stage and not away):
                out.append(self.place.bit(b))
            elif at == stage:
                out.append(1 - self.place.bit(b))
            else:
                out.append(slice(None))
        return tuple(out)

    def copy(self, stage):
        if stage == 0:
            bit, src = 0, self.send.at[(slice(None),) * (self.job.lead + 1) + (self.cols,)]
        else:
            bit, src = self.order[stage - 1], self.total.at[self.index(stage, True)]
        return pltpu.make_async_remote_copy(
            src_ref=src,
            dst_ref=self.got[stage],
            send_sem=self.sems.at[1, self.first + stage],
            recv_sem=self.sems.at[2, self.first + stage],
            device_id=self.place.partner(bit),
            device_id_type=pl.DeviceIdType.MESH,
        )

    def begin(self, stage):
        if stage == 0:
            self.own().start()
        self.copy(stage).start()

    def end(self, stage):
        if stage == 0:
            self.own().wait()
        self.copy(stage).wait()
        index = self.index(stage, False)
        if stage == len(self.order):
            self.out[:, self.cols] = self.total[index].astype(F32) + self.got[stage][...].astype(F32)
        elif stage == 0:
            self.total[...] = self.total[...] + self.got[0][...]
        else:
            self.total[index] = self.total[index] + self.got[stage][...]


class Sums:
    def __init__(self, jobs, count):
        self.jobs, self.count = jobs, count
        self.stages = count.bit_length() - 1

    def inputs(self):
        return [x for job in self.jobs for x in (job.keep, job.send)]

    def n_parts(self):
        return sum(len(job.orders) for job in self.jobs)

    def in_specs(self):
        return [pl.BlockSpec(memory_space=pl.ANY)] * (2 * len(self.jobs))

    def out_shapes(self):
        return [job.out_shape() for job in self.jobs]

    def out_specs(self):
        return [pl.BlockSpec((job.rows, job.cols), lambda *_: (0, 0)) for job in self.jobs]

    def scratch(self):
        out = [x for job in self.jobs for x in job.scratch()]
        return out + [pltpu.SemaphoreType.DMA((3, self.n_parts() * self.stages))]

    def parts(self, place, ins, outs, scratch):
        scratch = list(scratch)
        sems = scratch.pop()
        found = []
        for i, job in enumerate(self.jobs):
            for at in range(len(job.orders)):
                mine, scratch = scratch[: job.lead + 2], scratch[job.lead + 2 :]
                found.append(
                    Part(place, job, at, ins[2 * i], ins[2 * i + 1], outs[i], mine, sems, len(found) * self.stages)
                )
        return found

    def advance(self, parts, stage):
        for part in parts:
            if stage > 0:
                part.end(stage - 1)
            if stage < self.stages:
                part.begin(stage)


def attend_back_kernel(*refs, chunk, sums, slots):
    n_in, n_out = 6 + 2 * len(sums.jobs), 3 + len(sums.jobs)
    q, kv, kvo, up, out, lse = refs[:6]
    dq, dkv, dkvi = refs[n_in : n_in + 3]
    outbox, box_sems = refs[n_in + n_out : n_in + n_out + 2]
    place = Place(sums.count)
    parts = sums.parts(place, refs[6:n_in], refs[n_in + 3 : n_in + n_out], refs[n_in + n_out + 2 :])
    t = q.shape[0]
    scale = HEAD**-0.5
    c = LOG2E * scale
    pair, pairs = pl.program_id(0), len(slots) - 1

    def parcel(at):
        return pltpu.make_async_remote_copy(
            src_ref=outbox.at[at % 2],
            dst_ref=dkvi.at[at],
            send_sem=box_sems.at[0, at],
            recv_sem=box_sems.at[1, at],
            device_id=place.partner(0),
            device_id_type=pl.DeviceIdType.MESH,
        )

    pl.when(pair == 0)(place.greet)
    for at in range(pairs):

        @pl.when(pair == at)
        def _(at=at):
            for stage in slots[at]:
                sums.advance(parts, stage)
            if at >= 2:
                parcel(at - 2).wait_send()

    box = outbox.at[lax.rem(pair, 2)]
    for head in range(2):
        ls = slice(HEAD * head, HEAD * head + HEAD)
        qh = q[:, ls]
        uh = up[:, ls]
        q_t = qh.astype(F32).T.astype(BF)
        u_t = uh.astype(F32).T.astype(BF)
        level = lse[0].T[:, head : head + 1]
        inner = jnp.sum(uh.astype(F32) * out[:, ls].astype(F32), axis=1, keepdims=True)
        blocks = [
            (src, dst, slice(i * chunk, (i + 1) * chunk))
            for src, dst in ((kvo, box), (kv, dkv))
            for i in range(t // chunk)
        ]

        def products(block):
            src, _, rows = block
            return dot(qh, src[0, rows, ls], NT), dot(uh, src[1, rows, ls], NT)

        total = None
        ahead = products(blocks[0])
        for at, (src, dst, rows) in enumerate(blocks):
            s, dp = ahead
            if at + 1 < len(blocks):
                ahead = products(blocks[at + 1])
            p = jnp.exp2(s * c - level)
            ds = (p * (dp - inner)).astype(BF)
            dst[1, rows, ls] = dot(u_t, p.astype(BF), NN).T.astype(BF)
            dst[0, rows, ls] = (dot(q_t, ds, NN).T * scale).astype(BF)
            part = dot(ds, src[0, rows, ls], NN)
            total = part if total is None else total + part
        dq[:, ls] = (total * scale).astype(BF)

    for at in range(pairs):

        @pl.when(pair == at)
        def _(at=at):
            parcel(at).start()
            if at == pairs - 1:
                for stage in slots[pairs]:
                    sums.advance(parts, stage)
                for last in range(max(0, pairs - 2), pairs):
                    parcel(last).wait_send()
                for each in range(pairs):
                    parcel(each).wait_recv()


def attend_back_call(q, kv, kvo, up, out, lse, sums, collective_id):
    t, d = q.shape
    pairs = d // 128
    both = pl.BlockSpec((2, t, 128), lambda h: (0, 0, h))
    one = pl.BlockSpec((t, 128), lambda h: (0, h))
    slots = [[] for _ in range(pairs + 1)]
    starts = [0, 1, 3, 4, 5]
    for stage in range(sums.stages + 1):
        slots[starts[stage] if stage < min(len(starts), sums.stages) else pairs].append(stage)
    return pl.pallas_call(
        functools.partial(attend_back_kernel, chunk=min(256, t), sums=sums, slots=slots),
        grid=(pairs,),
        in_specs=[one, both, both, one, one, pl.BlockSpec((1, 8, t), lambda h: (h, 0, 0))] + sums.in_specs(),
        out_specs=[one, both, pl.BlockSpec(memory_space=pl.ANY)] + sums.out_specs(),
        out_shape=[
            jax.ShapeDtypeStruct((t, d), BF),
            jax.ShapeDtypeStruct((2, t, d), BF),
            jax.ShapeDtypeStruct((pairs, 2, t, 128), BF),
        ]
        + sums.out_shapes(),
        scratch_shapes=[pltpu.VMEM((2, 2, t, 128), BF), pltpu.SemaphoreType.DMA((2, pairs))] + sums.scratch(),
        compiler_params=pltpu.CompilerParams(
            vmem_limit_bytes=60 << 20, collective_id=collective_id, has_side_effects=True
        ),
        cost_estimate=cost(37e9),
        name="attend_back",
    )(q, kv, kvo, up, out, lse, *sums.inputs())


def sums_kernel(*refs, sums):
    n = len(sums.jobs)
    place = Place(sums.count)
    parts = sums.parts(place, refs[: 2 * n], refs[2 * n : 3 * n], refs[3 * n :])
    place.greet()
    for stage in range(sums.stages + 1):
        sums.advance(parts, stage)


def sums_call(sums, collective_id):
    return pl.pallas_call(
        functools.partial(sums_kernel, sums=sums),
        grid=(1,),
        in_specs=sums.in_specs(),
        out_specs=sums.out_specs(),
        out_shape=sums.out_shapes(),
        scratch_shapes=sums.scratch(),
        compiler_params=pltpu.CompilerParams(
            vmem_limit_bytes=60 << 20, collective_id=collective_id, has_side_effects=True
        ),
        cost_estimate=cost(15e9),
        name="sums",
    )(*sums.inputs())


def forward_kernel(
    att, x, wo_h, wu_h, wd_h, bo, g2, b2, bu, bd, middle_o, n2_o, act_o, slope_o, next_o, wo, wu, wd, sems, *, layer, cut
):
    first = pl.program_id(0) == 0
    copies = [
        pltpu.make_async_copy(src.at[layer], dst, sems.at[i])
        for i, (src, dst) in enumerate(((wo_h, wo), (wu_h, wu), (wd_h, wd)))
    ]

    @pl.when(first)
    def _():
        for copy in copies:
            copy.start()
        copies[0].wait()

    middle = x[...].astype(F32) + (dot(att[...], wo[...], NN) + bo[...])
    middle_o[...] = middle
    unit, _ = normalise(middle)
    n2 = (unit * g2[...] + b2[...]).astype(BF)
    n2_o[...] = n2

    @pl.when(first)
    def _():
        copies[1].wait()
        copies[2].wait()

    ff = wu.shape[1]
    count = ff // cut

    def up(j):
        cols = slice(j * cut, (j + 1) * cut)
        return dot(n2, wu[:, cols], NN) + bu[:, cols]

    ahead = up(0)
    total = None
    for j in range(count):
        hidden = ahead
        if j + 1 < count:
            ahead = up(j + 1)
        cols = slice(j * cut, (j + 1) * cut)
        act, slope = gelu_pair(hidden)
        act = act.astype(BF)
        act_o[:, cols] = act
        slope_o[:, cols] = slope.astype(BF)
        part = dot(act, wd[cols, :], NN)
        total = part if total is None else total + part
    next_o[...] = middle + (total + bd[...])


def forward_call(att, x, layer, wo, wu, wd, bo, g2, b2, bu, bd, tile):
    t, d = att.shape
    ff = wu.shape[2]
    tok = pl.BlockSpec((tile, d), lambda i: (i, 0))
    wide = pl.BlockSpec((tile, ff), lambda i: (i, 0))
    vec = pl.BlockSpec((None, 1, d), lambda i: (layer, 0, 0))
    vec_ff = pl.BlockSpec((None, 1, ff), lambda i: (layer, 0, 0))
    hbm = pl.BlockSpec(memory_space=pl.ANY)
    return pl.pallas_call(
        functools.partial(forward_kernel, layer=layer, cut=512),
        grid=(t // tile,),
        in_specs=[tok, tok, hbm, hbm, hbm, vec, vec, vec, vec_ff, vec],
        out_specs=[tok, tok, wide, wide, tok],
        out_shape=[
            jax.ShapeDtypeStruct((t, d), F32),
            jax.ShapeDtypeStruct((t, d), BF),
            jax.ShapeDtypeStruct((t, ff), BF),
            jax.ShapeDtypeStruct((t, ff), BF),
            jax.ShapeDtypeStruct((t, d), F32),
        ],
        scratch_shapes=[
            pltpu.VMEM((d, d), BF),
            pltpu.VMEM((d, ff), BF),
            pltpu.VMEM((ff, d), BF),
            pltpu.SemaphoreType.DMA((3,)),
        ],
        compiler_params=params(58),
        cost_estimate=cost(15e9),
        name="feed_forward",
    )(att, x, wo, wu, wd, bo, g2, b2, bu, bd)


def add_row(ref, at, value, first):
    ref[at : at + 1, :] = jnp.where(first, 0.0, ref[at : at + 1, :]) + value


def backward_kernel(
    ga, gb, slope, middle, wo_h, wu_h, wd_h, g2, dz_o, dh_o, dm_o, dy_o, da_o, sums, sums_ff, wo, wu, wd, sems, *, layer, cut
):
    first = pl.program_id(0) == 0
    copies = [
        pltpu.make_async_copy(src.at[layer], dst, sems.at[i])
        for i, (src, dst) in enumerate(((wd_h, wd), (wu_h, wu), (wo_h, wo)))
    ]

    @pl.when(first)
    def _():
        for copy in copies:
            copy.start()
        sums[...] = jnp.zeros_like(sums)
        sums_ff[...] = jnp.zeros_like(sums_ff)
        copies[0].wait()
        copies[1].wait()

    g = jnp.where(first, ga[...], gb[...])
    dz = g.astype(BF)
    dz_o[...] = dz
    sums[0:1, :] += column_sum(dz.astype(F32))
    ff = wu.shape[1]
    count = ff // cut

    def spread(j):
        return dot(dz, wd[j * cut : (j + 1) * cut, :], NT)

    ahead = spread(0)
    total = None
    for j in range(count):
        da = ahead
        if j + 1 < count:
            ahead = spread(j + 1)
        cols = slice(j * cut, (j + 1) * cut)
        dh = (da * slope[:, cols].astype(F32)).astype(BF)
        dh_o[:, cols] = dh
        sums_ff[0:1, cols] += column_sum(dh.astype(F32))
        part = dot(dh, wu[:, cols], NT)
        total = part if total is None else total + part
    unit, inverse = normalise(middle[...])
    sums[1:2, :] += column_sum(total * unit)
    sums[2:3, :] += column_sum(total)
    dm = g.astype(F32) + norm_back(total, g2[...], unit, inverse)
    dm_o[...] = dm
    dy = dm.astype(BF)
    dy_o[...] = dy
    sums[3:4, :] += column_sum(dy.astype(F32))

    @pl.when(first)
    def _():
        copies[2].wait()

    da_o[...] = dot(dy, wo[...], NT).astype(BF)


def backward_call(g, slope, middle, layer, wo, wu, wd, g2, tile, after):
    t, d = middle.shape
    ff = wu.shape[2]
    tok = pl.BlockSpec((tile, d), lambda i: (i, 0))
    wide = pl.BlockSpec((tile, ff), lambda i: (i, 0))
    vec = pl.BlockSpec((None, 1, d), lambda i: (layer, 0, 0))
    hbm = pl.BlockSpec(memory_space=pl.ANY)
    if isinstance(g, tuple):
        pieces = [pl.BlockSpec((tile, d), lambda i: (0, 0))] * 2
    else:
        g = (g, g)
        pieces = [pl.BlockSpec((tile, d), lambda i: (0, 0)), pl.BlockSpec((tile, d), lambda i: (1, 0))]
    return kernel_call(
        functools.partial(backward_kernel, layer=layer, cut=512),
        (*g, slope, middle, wo, wu, wd, g2),
        [*pieces, wide, tok, hbm, hbm, hbm, vec],
        after,
        grid=(t // tile,),
        out_specs=[
            tok,
            wide,
            tok,
            tok,
            tok,
            pl.BlockSpec((8, d), lambda i: (0, 0)),
            pl.BlockSpec((8, ff), lambda i: (0, 0)),
        ],
        out_shape=[
            jax.ShapeDtypeStruct((t, d), BF),
            jax.ShapeDtypeStruct((t, ff), BF),
            jax.ShapeDtypeStruct((t, d), F32),
            jax.ShapeDtypeStruct((t, d), BF),
            jax.ShapeDtypeStruct((t, d), BF),
            jax.ShapeDtypeStruct((8, d), F32),
            jax.ShapeDtypeStruct((8, ff), F32),
        ],
        scratch_shapes=[
            pltpu.VMEM((d, d), BF),
            pltpu.VMEM((d, ff), BF),
            pltpu.VMEM((ff, d), BF),
            pltpu.SemaphoreType.DMA((3,)),
        ],
        compiler_params=params(58),
        cost_estimate=cost(13e9),
        name="feed_forward_back",
    )


def joined_back_kernel(dq, dkv, dkvi, x, dm, weight, gain, df_o, g_o, sums):
    d = x.shape[-1]

    @pl.when(pl.program_id(0) == 0)
    def _():
        sums[...] = jnp.zeros_like(sums)

    parts = [dq[...]]
    for i in range(2):
        got = jnp.concatenate([dkvi[h, i] for h in range(d // 128)], axis=1)
        parts.append((dkv[i].astype(F32) + got.astype(F32)).astype(BF))
    total = None
    for i, part in enumerate(parts):
        cols = slice(i * d, (i + 1) * d)
        df_o[:, cols] = part
        piece = dot(part, weight[:, cols], NT)
        total = piece if total is None else total + piece
    sums[2:3, :] += column_sum(parts[0].astype(F32))
    sums[3:4, :] += column_sum(parts[2].astype(F32))
    unit, inverse = normalise(x[...].astype(F32))
    sums[0:1, :] += column_sum(total * unit)
    sums[1:2, :] += column_sum(total)
    g_o[...] = dm[...] + norm_back(total, gain[...], unit, inverse)


def joined_back_call(dq, dkv, dkvi, x, dm, layer, weight, gain, tile):
    t, d = x.shape
    tok = pl.BlockSpec((tile, d), lambda i: (i, 0))
    return pl.pallas_call(
        joined_back_kernel,
        in_specs=[
            tok,
            pl.BlockSpec((2, tile, d), lambda i: (0, i, 0)),
            pl.BlockSpec((d // 128, 2, tile, 128), lambda i: (0, 0, i, 0)),
            tok,
            tok,
            pl.BlockSpec((None, d, 3 * d), lambda i: (layer, 0, 0)),
            pl.BlockSpec((None, 1, d), lambda i: (layer, 0, 0)),
        ],
        grid=(t // tile,),
        out_specs=[
            pl.BlockSpec((tile, 3 * d), lambda i: (i, 0)),
            tok,
            pl.BlockSpec((8, d), lambda i: (0, 0)),
        ],
        out_shape=[
            jax.ShapeDtypeStruct((t, 3 * d), BF),
            jax.ShapeDtypeStruct((t, d), F32),
            jax.ShapeDtypeStruct((8, d), F32),
        ],
        compiler_params=params(56),
        cost_estimate=cost(6e9),
        name="joined_back",
    )(dq, dkv, dkvi, x, dm, weight, gain)


def weight_grad_kernel(core, a, b, keep, send, *, rows):
    out = lax.dot_general(a[...], b[...], (((0,), (0,)), ((), ())), preferred_element_type=F32)
    n, _ = out.shape
    even = jnp.concatenate([out[i : i + rows] for i in range(0, n, 2 * rows)], axis=0).astype(BF)
    odd = jnp.concatenate([out[i + rows : i + 2 * rows] for i in range(0, n, 2 * rows)], axis=0).astype(BF)

    @pl.when(core[0] == 0)
    def _():
        keep[...] = even
        send[...] = odd

    @pl.when(core[0] == 1)
    def _():
        keep[...] = odd
        send[...] = even


def weight_grad_call(core, a, b, chunks, block, after=()):
    t, n = a.shape
    cols = b.shape[1]
    fixed_a = n == block
    steps = cols // block if fixed_a else n // block
    if fixed_a:
        a_at, b_at, o_at = (lambda i: (0, 0)), (lambda i: (0, i)), (lambda i: (0, i))
    else:
        a_at, b_at, o_at = (lambda i: (0, i)), (lambda i: (0, 0)), (lambda i: (i, 0))
    shape = jax.ShapeDtypeStruct((n // 2, cols), BF)
    keep, send = kernel_call(
        functools.partial(weight_grad_kernel, rows=n // chunks),
        (core, a, b),
        [
            pl.BlockSpec(memory_space=pltpu.SMEM),
            pl.BlockSpec((t, block), a_at),
            pl.BlockSpec((t, block), b_at),
        ],
        after,
        grid=(steps,),
        out_specs=[pl.BlockSpec((block // 2, block), o_at)] * 2,
        out_shape=[shape, shape],
        compiler_params=params(56),
        cost_estimate=cost(t * n * cols * 1.7),
        name="weight_grad",
    )
    split = (chunks // 2, n // chunks, cols)
    return keep.reshape(split), send.reshape(split)


def cut_rows(rows, count):
    flat = jnp.concatenate([r.reshape(count, -1) for r in rows], axis=1)
    return jnp.pad(flat, ((0, 0), (0, -flat.shape[1] % 1024)))


def on_device(
    device_count,
    cell_tokens,
    first_gain,
    first_bias,
    joined_weight,
    query_value_bias,
    output_weight,
    output_bias,
    second_gain,
    second_bias,
    up_weight,
    up_bias,
    down_weight,
    down_bias,
    cotangent,
    gene_mask,
):
    _, genes, d = cell_tokens.shape
    layers = joined_weight.shape[0]
    seq = lax.axis_index("seq")
    index = lax.axis_index("dp") * 4 + seq
    chip, core = seq // 2, seq % 2
    core_ref = core.astype(jnp.int32).reshape(1)
    across = [(0, 2), (1, 3), (2, 0), (3, 1)]
    beside = [(0, 1), (1, 0), (2, 3), (3, 2)]
    tile = genes

    def rows(v):
        return v[:, None, :]

    def trade(pair):
        mine = lax.dynamic_index_in_dim(pair, chip, 0, keepdims=False)
        other = lax.dynamic_index_in_dim(pair, 1 - chip, 0, keepdims=False)
        return mine, lax.ppermute(other, "seq", across)

    def trade_back(held):
        own = held[:genes]
        got = lax.ppermute(held[genes:].astype(BF), "seq", across).astype(F32)
        return jnp.where(chip == 0, jnp.stack([own, got]), jnp.stack([got, own]))

    g1, b1 = rows(first_gain), rows(first_bias)
    g2, b2 = rows(second_gain), rows(second_bias)
    bo, bu, bd = rows(output_bias), rows(up_bias), rows(down_bias)
    qkv_bias = rows(
        jnp.concatenate(
            [query_value_bias[:, :d], jnp.zeros((layers, d), F32), query_value_bias[:, d:]], axis=1
        )
    )

    x = jnp.concatenate(trade(cell_tokens), axis=0)
    seeded = cotangent * gene_mask.astype(BF)[:, :, None]
    g = trade(seeded)

    saved = []
    for layer in range(layers):
        normed, q, kv = first_call(x, layer, g1, b1, joined_weight, qkv_bias, tile)
        kvo = lax.ppermute(kv, "seq", beside)
        att, lse = attend_call(q, kv, kvo)
        middle, n2, act, slope, following = forward_call(
            att, x, layer, output_weight, up_weight, down_weight, bo, g2, b2, bu, bd, tile
        )
        saved.append((x, normed, q, kv, kvo, att, lse, middle, n2, act, slope))
        x = following
    block_output = trade_back(x)

    chunks = device_count
    grads = [None] * layers
    vectors = [None] * layers
    high = list(range(device_count.bit_length() - 1, 1, -1))[1:]
    dp_bits = high[::-1]
    orders = (
        [1] + dp_bits,
        dp_bits[:1] + dp_bits[1:-1] + [1] + dp_bits[-1:],
        dp_bits[1:-1] + [1] + dp_bits[:1] + dp_bits[-1:],
    )
    waiting = []
    for layer in reversed(range(layers)):
        x, normed, q, kv, kvo, att, lse, middle, n2, act, slope = saved[layer]
        dz, dh, dm, dy, da, sums, sums_ff = backward_call(
            g, slope, middle, layer, output_weight, up_weight, down_weight, g2, tile, []
        )
        jobs = waiting + [
            Job(*weight_grad_call(core_ref, a, b, chunks, d), device_count, orders)
            for a, b in ((att, dy), (n2, dh), (act, dz))
        ]
        dq, dkv, dkvi, *done = attend_back_call(q, kv, kvo, da, att, lse, Sums(jobs, device_count), layer)
        if waiting:
            grads[layer + 1].append(done.pop(0))
        grads[layer] = done
        df, g, sums_in = joined_back_call(dq, dkv, dkvi, x, dm, layer, joined_weight, g1, tile)
        waiting = [Job(*weight_grad_call(core_ref, normed, df, chunks, d), device_count, orders)]
        vectors[layer] = [
            sums_in[0],
            sums_in[1],
            sums_in[2],
            sums_in[3],
            sums[3],
            sums[1],
            sums[2],
            sums_ff[0],
            sums[0],
        ]
    input_gradient = trade_back(g)

    qv = [jnp.concatenate([v[2], v[3]]) for v in vectors]
    plain = [0, 1, 4, 5, 6, 8]
    rows_out = [vectors[l][i] for l in range(layers) for i in plain]
    rows_out += qv + [v[7] for v in vectors]
    flat = cut_rows(rows_out, device_count).reshape(device_count // 2, 2, -1, 128)
    own = lax.dynamic_index_in_dim(flat, core, 1, keepdims=False)
    other = lax.dynamic_index_in_dim(flat, 1 - core, 1, keepdims=False)
    waiting.append(Job(own, other, device_count, orders[:1]))
    last, summed = sums_call(Sums(waiting, device_count), layers)
    grads[0].append(last)
    summed = summed.reshape(-1)
    piece = d // device_count
    at = 0
    small = {}
    for l in range(layers):
        for i in plain:
            small[l, i] = summed[at : at + piece]
            at += piece
    for key, width in (("qv", 2 * piece), ("up", up_bias.shape[1] // device_count)):
        for l in range(layers):
            small[l, key] = summed[at : at + width]
            at += width

    def vec(key):
        return jnp.stack([small[l, key] for l in range(layers)])

    def mat(i):
        return jnp.stack([grads[l][i] for l in range(layers)])

    return (
        block_output,
        input_gradient,
        vec(0),
        vec(1),
        mat(3),
        vec("qv"),
        mat(0),
        vec(4),
        vec(5),
        vec(6),
        mat(1),
        vec("up"),
        mat(2),
        vec(8),
    )


def solution(mesh):
    split = P(None, ("dp", "seq"))
    split_rows = P(None, ("dp", "seq"), None)
    tokens = P("dp", "seq", None)
    return jax.shard_map(
        functools.partial(on_device, mesh.size),
        mesh=mesh,
        in_specs=(tokens,) + (P(),) * 12 + (tokens, P("dp", "seq")),
        out_specs=(
            tokens,
            tokens,
            split,
            split,
            split_rows,
            split,
            split_rows,
            split,
            split,
            split,
            split_rows,
            split,
            split_rows,
            split,
        ),
        check_vma=False,
    )
```

```python
import functools

import jax
import jax.numpy as jnp
from jax import lax
from jax.experimental import pallas as pl
from jax.experimental.pallas import tpu as pltpu
from jax.sharding import PartitionSpec as P

HEAD = 64
LOG2E = 1.4426950408889634
BF = jnp.bfloat16
F32 = jnp.float32
NN = ((1,), (0,))
NT = ((1,), (1,))
SAFE = 80.0
BLOCK = 256
SLOTS = (0, 2, 6, 8, 10)


class _Names:
    def __getattr__(self, word):
        return word


N = _Names()


def tag(word, *numbers):
    return N._.join([word, *map(str, numbers)])


def dot(a, b, dims):
    return lax.dot_general(a, b, (dims, ((), ())), preferred_element_type=F32)


def params(mib):
    return pltpu.CompilerParams(vmem_limit_bytes=mib << 20)


def cost(products, nbytes=0):
    return pl.CostEstimate(flops=int(2 * products), bytes_accessed=int(nbytes), transcendentals=0)


def normalise(x):
    n = x.shape[-1]
    centred = x - jnp.sum(x, axis=-1, keepdims=True) * (1.0 / n)
    inverse = lax.rsqrt(jnp.sum(centred * centred, axis=-1, keepdims=True) * (1.0 / n) + 1e-05)
    return centred * inverse, inverse


def norm_back(upstream, gain, unit, inverse):
    n = unit.shape[-1]
    e = upstream * gain
    mean_e = jnp.sum(e, axis=-1, keepdims=True) * (1.0 / n)
    mean_eu = jnp.sum(e * unit, axis=-1, keepdims=True) * (1.0 / n)
    return inverse * (e - mean_e - unit * mean_eu)


def column_sum(x):
    return jnp.sum(x, axis=0, keepdims=True)


def gelu_pair(x):
    cdf = 0.5 + 0.5 * lax.erf(x * 0.7071067811865476)
    slope = jnp.exp2(x * x * (-0.5 * LOG2E)) * 0.3989422804014327
    return x * cdf, cdf + x * slope


def kernel_call(kernel, ins, in_specs, after=(), **kwargs):
    n = len(ins)
    extra = [pl.BlockSpec(memory_space=pl.ANY)] * len(after)

    def body(*refs):
        kernel(*refs[:n], *refs[n + len(after) :])

    return pl.pallas_call(body, in_specs=list(in_specs) + extra, **kwargs)(*ins, *after)


def qkv_kernel(*refs, names, layer, block, count, trading):
    r = dict(zip(names, refs))
    t, d = r[N.x_v].shape
    spans = [slice(i, i + block) for i in range(0, t, block)]
    half = len(spans) // 2
    place = Place(count)
    row = slice(layer, layer + 1)
    copies = Copies(r[N.sems])
    for k in range(3):
        cols = slice(k * d, (k + 1) * d)
        copies.add((N.weight, k), r[N.weight].at[layer, :, cols], r[N.weight_v].at[k])
    chip = place.bit(1)
    for i, at in enumerate(spans):
        if not trading:
            copies.add((N.x, i), r[N.x].at[at], r[N.x_v].at[at])
        elif i < half:
            copies.add((N.x, i), r[N.x].at[chip, at], r[N.x_v].at[at])
        if trading:
            copies.add((N.held, i), r[N.x_v].at[at], r[N.held].at[at])
        copies.add((N.normed, i), r[N.normed_v].at[at], r[N.normed].at[at])
        copies.add((N.q, i), r[N.q_v].at[at], r[N.q].at[at])
        copies.add((N.kv, i), r[N.kv_v].at[:, at], r[N.kv].at[:, at])

    def remote(src, dst, i, bit):
        return pltpu.make_async_remote_copy(
            src_ref=src,
            dst_ref=dst,
            send_sem=r[N.far_sems].at[0, i],
            recv_sem=r[N.far_sems].at[1, i],
            device_id=place.partner(bit),
            device_id_type=pl.DeviceIdType.MESH,
        )

    if trading:
        for i, cell in enumerate((chip, 1 - chip)):
            copies.add((N.seed, i), r[N.cotangent].at[cell], r[N.seed_v].at[i])
            copies.add((N.seeded, i), r[N.seed_v].at[i], r[N.seed_own if i == 0 else N.seed_send])

    def parcel(i):
        return remote(r[N.kv_v].at[:, spans[i]], r[N.kvo].at[:, spans[i]], i, 0)

    def trade():
        return remote(r[N.x].at[1 - chip], r[N.x_v].at[t // 2 :], len(spans), 1)

    for i in range(half if trading else len(spans)):
        copies.start(N.x, i)
        if i == 0:
            for k in (1, 2, 0):
                copies.start(N.weight, k)
    place.greet(2)
    if trading:
        trade().start()
        for i in range(2):
            copies.start(N.seed, i)
    waited = set()

    def weight(k):
        if k not in waited:
            copies.wait(N.weight, k)
            waited.add(k)
        return r[N.weight_v][k]

    for group in (range(half), range(half, len(spans))):
        if trading and group.start:
            masks = jnp.broadcast_to(r[N.mask][...].astype(F32)[:, None, :], (2, 8, t // 2))
            for i in range(2):
                mask = jnp.where(chip == i, masks[0], masks[1])
                copies.wait(N.seed, i)
                r[N.seed_v][i] = r[N.seed_v][i] * mask.T[:, :1].astype(BF)
                copies.start(N.seeded, i)
            trade().wait()
        for i in group:
            at = spans[i]
            if not trading or i < half:
                copies.wait(N.x, i)
            if trading:
                copies.start(N.held, i)
            unit, _ = normalise(r[N.x_v][at].astype(F32))
            normed = (unit * r[N.gain][row, :] + r[N.bias][row, :]).astype(BF)
            r[N.normed_v][at] = normed
            copies.start(N.normed, i)
            r[N.kv_v][0, at] = dot(normed, weight(1), NN).astype(BF)
            r[N.kv_v][1, at] = (dot(normed, weight(2), NN) + r[N.qv_bias][row, d:]).astype(BF)
            parcel(i).start()
            copies.start(N.kv, i)
        if trading or group.start:
            for i in group if trading else range(len(spans)):
                at = spans[i]
                r[N.q_v][at] = (dot(r[N.normed_v][at], weight(0), NN) + r[N.qv_bias][row, :d]).astype(BF)
                copies.start(N.q, i)
    if trading:
        for i in range(2):
            copies.wait(N.seeded, i)
    for i in range(len(spans)):
        for name in (N.held, N.normed, N.q, N.kv) if trading else (N.normed, N.q, N.kv):
            copies.wait(name, i)
        parcel(i).wait()


def qkv_call(x, layer, devices, gain, bias, weight, qv_bias, collective_id, seeds=()):
    trading = x.ndim == 3
    d = x.shape[-1]
    t = x.size // d
    block = min(BLOCK, t // 2)
    blocks = t // block
    ins, outs, scratch = Names(), Names(), Names()
    hbm = pl.BlockSpec(memory_space=pl.ANY)
    ins.add(N.x, hbm)
    ins.add(N.weight, hbm)
    for name in (N.gain, N.bias, N.qv_bias):
        ins.add(name, pl.BlockSpec(memory_space=pltpu.VMEM))
    if trading:
        ins.add(N.cotangent, hbm)
        ins.add(N.mask, pl.BlockSpec(memory_space=pltpu.VMEM))
        outs.add(N.held, hbm, ((t, d), x.dtype))
        for name in (N.seed_own, N.seed_send):
            outs.add(name, hbm, ((t // 2, d), BF))
        scratch.add(N.seed_v, pltpu.VMEM((2, t // 2, d), BF))
    outs.add(N.normed, hbm, ((t, d), BF))
    outs.add(N.q, hbm, ((t, d), BF))
    outs.add(N.kv, hbm, ((2, t, d), BF))
    outs.add(N.kvo, hbm, ((2, t, d), BF))
    scratch.add(N.x_v, pltpu.VMEM((t, d), x.dtype))
    scratch.add(N.normed_v, pltpu.VMEM((t, d), BF))
    scratch.add(N.q_v, pltpu.VMEM((t, d), BF))
    scratch.add(N.kv_v, pltpu.VMEM((2, t, d), BF))
    scratch.add(N.weight_v, pltpu.VMEM((3, d, d), BF))
    scratch.add(N.sems, pltpu.SemaphoreType.DMA((7 + 5 * blocks,)))
    scratch.add(N.far_sems, pltpu.SemaphoreType.DMA((2, blocks + 1)))
    found = pl.pallas_call(
        functools.partial(
            qkv_kernel,
            names=ins.names + outs.names + scratch.names,
            layer=layer,
            block=block,
            count=devices,
            trading=trading,
        ),
        grid=(1,),
        in_specs=ins.specs,
        out_specs=outs.specs,
        out_shape=[jax.ShapeDtypeStruct(*shape) for shape in outs.shapes],
        scratch_shapes=scratch.specs,
        compiler_params=pltpu.CompilerParams(
            vmem_limit_bytes=62 << 20, collective_id=collective_id, has_side_effects=True
        ),
        cost_estimate=cost(12e9 if trading else 5e9),
        name=N.norm_qkv,
    )(x, weight, gain, bias, qv_bias, *seeds)
    return dict(zip(outs.names, found))


def attend_kernel(q, kv, kvo, out, lse, *, chunk):
    t = q.shape[0]
    c = LOG2E * HEAD**-0.5
    lane = lax.broadcasted_iota(jnp.int32, (128, 128), 0) // HEAD
    pick = (lane == lax.broadcasted_iota(jnp.int32, (128, 128), 1)).astype(BF)

    def squares(x):
        x = x.astype(F32)
        return jnp.max(dot((x * x).astype(BF), pick, NN), axis=0, keepdims=True)

    bound = squares(q[...]) * jnp.maximum(squares(kv[0]), squares(kvo[0]))
    fast = jnp.max(bound) * (c * c * 1.05) < SAFE * SAFE

    def run(stable):
        for head in range(2):
            ls = slice(HEAD * head, HEAD * head + HEAD)
            values = []
            for ref in (kv, kvo):
                v = ref[1, :, ls].astype(F32).T.astype(BF)
                values.append(jnp.concatenate([v, jnp.ones((16, t), BF)], axis=0))

            def score(j):
                block = q[j * chunk : (j + 1) * chunk, ls]
                return [dot(ref[0, :, ls], block, NT) for ref in (kv, kvo)]

            ahead = score(0)
            for j in range(t // chunk):
                s = ahead
                if j + 1 < t // chunk:
                    ahead = score(j + 1)
                if stable:
                    shift = c * jnp.maximum(
                        jnp.max(s[0], axis=0, keepdims=True), jnp.max(s[1], axis=0, keepdims=True)
                    )
                    p = [jnp.exp2(x * c - shift).astype(BF) for x in s]
                else:
                    shift = 0.0
                    p = [jnp.exp2(x * c).astype(BF) for x in s]
                total = dot(values[0], p[0], NN) + dot(values[1], p[1], NN)
                level = total[HEAD : HEAD + 1]
                cols = slice(j * chunk, (j + 1) * chunk)
                out[cols, ls] = (total[:HEAD] / level).T.astype(BF)
                lse[0, head : head + 1, cols] = shift + jnp.log2(level)

    pl.when(fast)(lambda: run(False))
    pl.when(jnp.logical_not(fast))(lambda: run(True))


def attend_call(q, kv, kvo):
    t, d = q.shape
    pairs = d // 128
    both = pl.BlockSpec((2, t, 128), lambda h: (0, 0, h))
    one = pl.BlockSpec((t, 128), lambda h: (0, h))
    return pl.pallas_call(
        functools.partial(attend_kernel, chunk=min(256, t)),
        grid=(pairs,),
        in_specs=[one, both, both],
        out_specs=[one, pl.BlockSpec((1, 8, t), lambda h: (h, 0, 0))],
        out_shape=[jax.ShapeDtypeStruct((t, d), BF), jax.ShapeDtypeStruct((pairs, 8, t), F32)],
        compiler_params=params(62),
        cost_estimate=cost(16e9),
        name=N.attend,
    )(q, kv, kvo)


class Place:
    def __init__(self, count):
        self.count = count
        self.bits = count.bit_length() - 1
        self.dp, self.seq = lax.axis_index(N.dp), lax.axis_index(N.seq)

    def bit(self, b):
        return (self.seq // (1 << b)) % 2 if b < 2 else (self.dp // (1 << (b - 2))) % 2

    def partner(self, b):
        step = 1 - 2 * self.bit(b)
        if b < 2:
            return {N.dp: self.dp, N.seq: self.seq + step * (1 << b)}
        return {N.dp: self.dp + step * (1 << (b - 2)), N.seq: self.seq}

    def greet(self, bits=None):
        bits = self.bits if bits is None else bits
        barrier = pltpu.get_barrier_semaphore()
        for b in range(bits):
            pl.semaphore_signal(barrier, inc=1, device_id=self.partner(b), device_id_type=pl.DeviceIdType.MESH)
        pl.semaphore_wait(barrier, bits)


class Job:
    def __init__(self, keep, send, count, orders, shape=None):
        self.lead = count.bit_length() - 2
        self.made = keep is None
        if not self.made:
            self.keep = keep.reshape((2,) * self.lead + keep.shape[1:])
            self.send = send.reshape((2,) * self.lead + send.shape[1:])
        self.rows, self.cols = shape or keep.shape[1:]
        self.orders = orders
        self.wide = self.cols // len(orders)
        self.dtype = BF

    def scratch(self):
        out = []
        for _ in self.orders:
            block = (self.rows, self.wide)
            out.append(pltpu.VMEM((2,) * self.lead + block, self.dtype))
            if self.made:
                out.append(pltpu.VMEM((2,) * self.lead + block, self.dtype))
            for left in range(self.lead, -1, -1):
                out.append(pltpu.VMEM((2,) * left + block, self.dtype))
        return out

    def out_shape(self):
        return jax.ShapeDtypeStruct((self.rows, self.cols), F32)


class Part:
    def __init__(self, place, job, at, keep, send, out, scratch, sems, first_sem):
        self.place, self.job, self.keep, self.send, self.out = place, job, keep, send, out
        self.order = job.orders[at]
        self.cols = slice(at * job.wide, (at + 1) * job.wide)
        self.total, self.got = scratch[0], scratch[1:]
        self.sems, self.first = sems, first_sem

    def fill(self, out, rows):
        lead = self.job.lead
        for core in range(2):

            @pl.when(self.place.bit(0) == core)
            def _(core=core):
                for at in range(2 << lead):
                    index = tuple((at >> (b + 1)) & 1 for b in reversed(range(lead)))
                    into = self.total if at % 2 == core else self.send
                    into[index] = out[at * rows : (at + 1) * rows].astype(BF)

    def own(self):
        return pltpu.make_async_copy(
            self.keep.at[(slice(None),) * (self.job.lead + 1) + (self.cols,)], self.total, self.sems.at[0, self.first]
        )

    def index(self, stage, away):
        out = []
        for b in range(self.job.lead, 0, -1):
            at = self.order.index(b) + 1
            if at < stage or (at == stage and not away):
                out.append(self.place.bit(b))
            elif at == stage:
                out.append(1 - self.place.bit(b))
            else:
                out.append(slice(None))
        return tuple(out)

    def copy(self, stage):
        if stage == 0 and self.keep is None:
            bit, src = 0, self.send
        elif stage == 0:
            bit, src = 0, self.send.at[(slice(None),) * (self.job.lead + 1) + (self.cols,)]
        else:
            bit, src = self.order[stage - 1], self.total.at[self.index(stage, True)]
        return pltpu.make_async_remote_copy(
            src_ref=src,
            dst_ref=self.got[stage],
            send_sem=self.sems.at[1, self.first + stage],
            recv_sem=self.sems.at[2, self.first + stage],
            device_id=self.place.partner(bit),
            device_id_type=pl.DeviceIdType.MESH,
        )

    def begin(self, stage):
        if stage == 0 and self.keep is not None:
            self.own().start()
        self.copy(stage).start()

    def end(self, stage):
        if stage == 0 and self.keep is not None:
            self.own().wait()
        self.copy(stage).wait()
        index = self.index(stage, False)
        if stage == len(self.order):
            self.out[:, self.cols] = self.total[index].astype(F32) + self.got[stage][...].astype(F32)
        elif stage == 0:
            self.total[...] = self.total[...] + self.got[0][...]
        else:
            self.total[index] = self.total[index] + self.got[stage][...]


class Trade:
    def __init__(self, place, src, dst, sems):
        self.ends = dict(src_ref=src, dst_ref=dst, send_sem=sems.at[0], recv_sem=sems.at[1])
        self.place = place

    def copy(self):
        return pltpu.make_async_remote_copy(
            **self.ends, device_id=self.place.partner(1), device_id_type=pl.DeviceIdType.MESH
        )


class Sums:
    def __init__(self, jobs, count, trade=None, trade_at=0):
        self.jobs, self.count, self.trade, self.trade_at = jobs, count, trade, trade_at
        self.stages = count.bit_length() - 1

    def n_ins(self):
        return 2 * sum(not job.made for job in self.jobs) + (self.trade is not None)

    def n_outs(self):
        return len(self.jobs) + (self.trade is not None)

    def inputs(self):
        return [x for job in self.jobs if not job.made for x in (job.keep, job.send)] + ([] if self.trade is None else [self.trade])

    def n_parts(self):
        return sum(len(job.orders) for job in self.jobs)

    def in_specs(self):
        return [pl.BlockSpec(memory_space=pl.ANY)] * self.n_ins()

    def out_shapes(self):
        out = [job.out_shape() for job in self.jobs]
        return out if self.trade is None else out + [jax.ShapeDtypeStruct(self.trade.shape, self.trade.dtype)]

    def out_specs(self):
        out = [pl.BlockSpec((job.rows, job.cols), lambda *_: (0, 0), pipeline_mode=pl.Buffered(1)) for job in self.jobs]
        return out if self.trade is None else out + [pl.BlockSpec(memory_space=pl.ANY)]

    def scratch(self):
        out = [x for job in self.jobs for x in job.scratch()]
        return out + [pltpu.SemaphoreType.DMA((3, self.n_parts() * self.stages)), pltpu.SemaphoreType.DMA((2,))]

    def parts(self, place, ins, outs, scratch):
        scratch = list(scratch)
        trade_sems = scratch.pop()
        sems = scratch.pop()
        found = []
        self.swap = None if self.trade is None else Trade(place, ins[-1], outs[-1], trade_sems)
        for i, job in enumerate(self.jobs):
            for at in range(len(job.orders)):
                size = job.lead + 2 + job.made
                mine, scratch = scratch[:size], scratch[size:]
                if job.made:
                    keep, send = None, mine.pop(1)
                else:
                    keep, send = ins[2 * i], ins[2 * i + 1]
                found.append(Part(place, job, at, keep, send, outs[i], mine, sems, len(found) * self.stages))
        return found

    def advance(self, parts, stage):
        for part in parts:
            if stage > 0:
                part.end(stage - 1)
            if stage < self.stages:
                part.begin(stage)
        if self.swap is not None:
            if stage == self.trade_at:
                self.swap.copy().start()
            if stage == self.stages:
                self.swap.copy().wait()


def attend_back_kernel(*refs, chunk, sums, slots):
    n_in, n_out = 6 + sums.n_ins(), 3 + sums.n_outs()
    q, kv, kvo, up, out, lse = refs[:6]
    dq, dkv, dkvi = refs[n_in : n_in + 3]
    outbox, box_sems = refs[n_in + n_out : n_in + n_out + 2]
    place = Place(sums.count)
    parts = sums.parts(place, refs[6:n_in], refs[n_in + 3 : n_in + n_out], refs[n_in + n_out + 2 :])
    t = q.shape[0]
    scale = HEAD**-0.5
    c = LOG2E * scale
    pair, pairs = pl.program_id(0), len(slots) // 2

    def parcel(at):
        return pltpu.make_async_remote_copy(
            src_ref=outbox.at[at % 2],
            dst_ref=dkvi.at[at],
            send_sem=box_sems.at[0, at],
            recv_sem=box_sems.at[1, at],
            device_id=place.partner(0),
            device_id_type=pl.DeviceIdType.MESH,
        )

    def advance(at):
        for stage in slots[at]:
            sums.advance(parts, stage)

    pl.when(pair == 0)(place.greet)
    for at in range(2, pairs):
        pl.when(pair == at)(lambda at=at: parcel(at - 2).wait_send())
    box = outbox.at[lax.rem(pair, 2)]
    for head in range(2):
        for at in range(pairs):
            if slots[2 * at + head]:
                pl.when(pair == at)(functools.partial(advance, 2 * at + head))
        ls = slice(HEAD * head, HEAD * head + HEAD)
        qh = q[:, ls]
        uh = up[:, ls]
        q_t = qh.astype(F32).T.astype(BF)
        u_t = uh.astype(F32).T.astype(BF)
        level = lse[0].T[:, head : head + 1]
        inner = jnp.sum(uh.astype(F32) * out[:, ls].astype(F32), axis=1, keepdims=True)
        blocks = [
            (src, dst, slice(i * chunk, (i + 1) * chunk))
            for src, dst in ((kvo, box), (kv, dkv))
            for i in range(t // chunk)
        ]

        def products(block):
            src, _, rows = block
            return dot(qh, src[0, rows, ls], NT), dot(uh, src[1, rows, ls], NT)

        total = None
        ahead = products(blocks[0])
        for at, (src, dst, rows) in enumerate(blocks):
            s, dp = ahead
            if at + 1 < len(blocks):
                ahead = products(blocks[at + 1])
            p = jnp.exp2(s * c - level)
            ds = (p * (dp - inner)).astype(BF)
            dst[1, rows, ls] = dot(u_t, p.astype(BF), NN).T.astype(BF)
            dst[0, rows, ls] = (dot(q_t, ds, NN).T * scale).astype(BF)
            part = dot(ds, src[0, rows, ls], NN)
            total = part if total is None else total + part
        dq[:, ls] = (total * scale).astype(BF)

    for at in range(pairs):

        @pl.when(pair == at)
        def _(at=at):
            parcel(at).start()
            if at == pairs - 1:
                advance(2 * pairs)
                for last in range(max(0, pairs - 2), pairs):
                    parcel(last).wait_send()
                for each in range(pairs):
                    parcel(each).wait_recv()


def attend_back_call(q, kv, kvo, up, out, lse, sums, collective_id):
    t, d = q.shape
    pairs = d // 128
    both = pl.BlockSpec((2, t, 128), lambda h: (0, 0, h))
    one = pl.BlockSpec((t, 128), lambda h: (0, h))
    slots = [[] for _ in range(2 * pairs + 1)]
    for stage in range(sums.stages + 1):
        slots[SLOTS[stage] if stage < min(len(SLOTS), sums.stages) else 2 * pairs].append(stage)
    return pl.pallas_call(
        functools.partial(attend_back_kernel, chunk=min(256, t), sums=sums, slots=slots),
        grid=(pairs,),
        in_specs=[one, both, both, one, one, pl.BlockSpec((1, 8, t), lambda h: (h, 0, 0))] + sums.in_specs(),
        out_specs=[one, both, pl.BlockSpec(memory_space=pl.ANY)] + sums.out_specs(),
        out_shape=[
            jax.ShapeDtypeStruct((t, d), BF),
            jax.ShapeDtypeStruct((2, t, d), BF),
            jax.ShapeDtypeStruct((pairs, 2, t, 128), BF),
        ]
        + sums.out_shapes(),
        scratch_shapes=[pltpu.VMEM((2, 2, t, 128), BF), pltpu.SemaphoreType.DMA((2, pairs))] + sums.scratch(),
        compiler_params=pltpu.CompilerParams(
            vmem_limit_bytes=60 << 20, collective_id=collective_id, has_side_effects=True
        ),
        cost_estimate=cost(37e9),
        name=N.attend_back,
    )(q, kv, kvo, up, out, lse, *sums.inputs())


def split_rows(out, rows):
    n = out.shape[0]
    even = jnp.concatenate([out[i : i + rows] for i in range(0, n, 2 * rows)], axis=0).astype(BF)
    odd = jnp.concatenate([out[i + rows : i + 2 * rows] for i in range(0, n, 2 * rows)], axis=0).astype(BF)
    return even, odd


def deliver(core, out, rows, keep, send):
    even, odd = split_rows(out, rows)

    @pl.when(core == 0)
    def _():
        keep[...] = even
        send[...] = odd

    @pl.when(core == 1)
    def _():
        keep[...] = odd
        send[...] = even


def grad_dot(a, b):
    return lax.dot_general(a, b, (((0,), (0,)), ((), ())), preferred_element_type=F32)


class Names:
    def __init__(self):
        self.names, self.specs, self.shapes = [], [], []

    def add(self, name, spec, shape=None):
        self.names.append(name)
        self.specs.append(spec)
        self.shapes.append(shape)


class Copies:
    def __init__(self, sems):
        self.sems, self.made = sems, {}

    def add(self, key, src, dst):
        self.made[key] = pltpu.make_async_copy(src, dst, self.sems.at[len(self.made)])

    def start(self, *key):
        self.made[key].start()

    def wait(self, *key):
        self.made[key].wait()


def ffn_kernel(*refs, names, forward, backward, block, chunks, sums):
    r = dict(zip(names, refs))
    if sums is not None:
        place = Place(sums.count)
        parts = sums.parts(
            place, *[[ref for name, ref in r.items() if name.startswith(kind)] for kind in (N.sum_i, N.sum_o, N.sum_s)]
        )
    layer = r[N.layer]
    row = slice(layer, layer + 1)
    j = pl.program_id(0)
    t, d = r[N.att_v].shape
    cut = r[N.wu_v].shape[2]
    count = r[N.wu_v].shape[0]
    first, final = j == 0, j == count - 1
    spans = [slice(i, i + block) for i in range(0, t, block)]
    every = range(len(spans))
    copies = Copies(r[N.sems])
    copies.add((N.wo,), r[N.wo].at[layer], r[N.wo_v])
    for i, at in enumerate(spans):
        copies.add((N.att, i), r[N.att].at[at], r[N.att_v].at[at])
        if forward:
            copies.add((N.x, i), r[N.x].at[at], r[N.x_v].at[at])
            if not backward:
                copies.add((N.next, i), r[N.next_v].at[at], r[N.next].at[at])
            elif at.start < r[N.next].shape[0]:
                copies.add((N.next, i), r[N.next_v].at[at], r[N.next].at[at])
            else:
                low = slice(at.start - r[N.next].shape[0], at.stop - r[N.next].shape[0])
                copies.add((N.next, i), r[N.dz_low].at[low], r[N.next_low].at[low])
            if not backward:
                copies.add((N.middle_o, i), r[N.middle_v].at[at], r[N.middle].at[at])
                copies.add((N.n2_o, i), r[N.n2_v].at[at], r[N.n2].at[at])
        else:
            copies.add((N.middle, i), r[N.middle].at[at], r[N.middle_v].at[at])
            copies.add((N.n2, i), r[N.n2].at[at], r[N.n2_v].at[at])
            copies.add((N.g, i), r[N.g].at[at], r[N.dm_v].at[at])
        if backward:
            copies.add((N.dm, i), r[N.dm_v].at[at], r[N.dm].at[at])
            copies.add((N.da, i), r[N.da_v].at[at], r[N.da].at[at])
    if backward:
        half = r[N.dza].shape[0]
        copies.add((N.dza,), r[N.dza], r[N.dz_v].at[:half])
        if half < t:
            copies.add((N.dzb,), r[N.dzb], r[N.dz_v].at[half:])
    for c in range(count):
        cols = slice(c * cut, (c + 1) * cut)
        copies.add((N.wu, c), r[N.wu].at[layer, :, cols], r[N.wu_v].at[c])
        copies.add((N.wd, c), r[N.wd].at[layer, cols, :], r[N.wd_v].at[c])
        if not (forward and backward):
            for name in (N.act, N.slope):
                for i, at in enumerate(spans):
                    ends = r[name].at[at, cols], r[name + N._v].at[c % 2, at]
                    copies.add((name, c, i), *(ends if backward else ends[::-1]))

    def per_chunk(act):
        for c in range(count):
            pl.when(j == c)(functools.partial(act, c))

    def feed(c):
        for i in every:
            for name in (N.act, N.slope):
                copies.start(name, c, i)

    if sums is not None:
        pl.when(first)(place.greet)

    @pl.when(first)
    def _():
        if forward:
            copies.start(N.wo)
            for i in every:
                copies.start(N.att, i)
                copies.start(N.x, i)
        if backward:
            copies.start(N.dza)
            if half < t:
                copies.start(N.dzb)
        for c in range(count):
            copies.start(N.wu, c)
            copies.start(N.wd, c)
            if c == 0 and not forward:
                feed(0)
                for i in every:
                    copies.start(N.n2, i)
        if not forward:
            for i in every:
                copies.start(N.middle, i)
                copies.start(N.g, i)
                copies.start(N.att, i)
            copies.start(N.wo)
        if forward:
            copies.wait(N.wo)
            for i, at in enumerate(spans):
                copies.wait(N.att, i)
                copies.wait(N.x, i)
                middle = r[N.x_v][at].astype(F32) + (dot(r[N.att_v][at], r[N.wo_v][...], NN) + r[N.bo][row, :])
                unit, _ = normalise(middle)
                r[N.n2_v][at] = (unit * r[N.g2][row, :] + r[N.b2][row, :]).astype(BF)
                r[N.middle_v][at] = middle
                r[N.next_v][at] = middle + r[N.bd][row, :]
                if not backward:
                    copies.start(N.middle_o, i)
                    copies.start(N.n2_o, i)
        if backward:
            r[N.dn_v][...] = jnp.zeros(r[N.dn_v].shape, F32)
            r[N.sums][...] = jnp.zeros(r[N.sums].shape, F32)
            copies.wait(N.dza)
            if half < t:
                copies.wait(N.dzb)
            r[N.sums][0:1, :] = column_sum(r[N.dz_v][...].astype(F32))
            if not forward:
                for i in every:
                    copies.wait(N.n2, i)

    @per_chunk
    def _(c):
        if sums is not None:
            sums.advance(parts, c)
        copies.wait(N.wu, c)
        copies.wait(N.wd, c)
        if not forward:
            if c + 1 < count:
                feed(c + 1)
            for i in every:
                for name in (N.act, N.slope):
                    copies.wait(name, c, i)
        elif not backward and c >= 2:
            for i in every:
                for name in (N.act, N.slope):
                    copies.wait(name, c - 2, i)

    wu, wd = r[N.wu_v].at[j], r[N.wd_v].at[j]
    slot = lax.rem(j, 2)

    def lead(at):
        return (
            dot(r[N.n2_v][at], wu[...], NN) if forward else None,
            dot(r[N.dz_v][at], wd[...], NT) if backward else None,
        )

    ff_sum = 0.0
    ahead = lead(spans[0])
    for i, at in enumerate(spans):
        hidden, da = ahead
        if i + 1 < len(spans):
            ahead = lead(spans[i + 1])
        if forward:
            act, slope = gelu_pair(hidden + r[N.bu][row, :])
            act = act.astype(BF)
            r[N.act_v][slot, at] = act
            if not backward:
                r[N.slope_v][slot, at] = slope.astype(BF)
        else:
            slope = r[N.slope_v][slot, at].astype(F32)
        if backward:
            dh = (da * slope).astype(BF)
            r[N.dh_v][at] = dh
            ff_sum = ff_sum + column_sum(dh.astype(F32))
        if forward:
            r[N.next_v][at] += dot(act, wd[...], NN)
        if backward:
            r[N.dn_v][at] += dot(dh, wu[...], NT)

    if forward:

        @per_chunk
        def _(c):
            for i in every:
                if not backward:
                    copies.start(N.act, c, i)
                    copies.start(N.slope, c, i)
                if c == count - 1:
                    if backward and spans[i].start >= r[N.next].shape[0]:
                        low = slice(spans[i].start - r[N.next].shape[0], spans[i].stop - r[N.next].shape[0])
                        r[N.dz_low][low] = r[N.next_v][spans[i]].astype(BF)
                    copies.start(N.next, i)

    if backward:
        core = r[N.core][0] if sums is None else place.bit(0)
        r[N.sums_ff][0:1, :] = ff_sum
        deliver(core, grad_dot(r[N.act_v][slot], r[N.dz_v][...]), chunks[1], r[N.wd_keep], r[N.wd_send])
        deliver(core, grad_dot(r[N.n2_v][...], r[N.dh_v][...]), chunks[0], r[N.wu_keep], r[N.wu_send])

    @pl.when(final)
    def _():
        if sums is not None:
            for stage in range(count, sums.stages):
                sums.advance(parts, stage)
        if backward:
            if not forward:
                copies.wait(N.wo)
            for i, at in enumerate(spans):
                if not forward:
                    copies.wait(N.middle, i)
                    copies.wait(N.g, i)
                    copies.wait(N.att, i)
                g = r[N.dz_v][at].astype(F32) if forward else r[N.dm_v][at]
                unit, inverse = normalise(r[N.middle_v][at])
                up = r[N.dn_v][at]
                r[N.sums][1:2, :] += column_sum(up * unit)
                r[N.sums][2:3, :] += column_sum(up)
                dm = g + norm_back(up, r[N.g2][row, :], unit, inverse)
                r[N.dm_v][at] = dm
                copies.start(N.dm, i)
                dy = dm.astype(BF)
                r[N.dh_v][at] = dy
                r[N.sums][3:4, :] += column_sum(dy.astype(F32))
                r[N.da_v][at] = dot(dy, r[N.wo_v][...], NT).astype(BF)
                copies.start(N.da, i)
            deliver(core, grad_dot(r[N.att_v][...], r[N.dh_v][...]), chunks[0], r[N.wo_keep], r[N.wo_send])
        for i in every:
            if forward:
                copies.wait(N.next, i)
                if not backward:
                    copies.wait(N.middle_o, i)
                    copies.wait(N.n2_o, i)
                    for c in range(max(0, count - 2), count):
                        copies.wait(N.act, c, i)
                        copies.wait(N.slope, c, i)
            if backward:
                copies.wait(N.dm, i)
                copies.wait(N.da, i)
        if sums is not None:
            sums.advance(parts, sums.stages)


def ffn_call(layer, devices, arrays, weights, forward, backward, sums=None, collective_id=0):
    t, d = arrays[N.att].shape
    ff = weights[N.wu].shape[2]
    cut, count = d, ff // d
    block = min(BLOCK, t)
    once = pl.Buffered(1)
    ins, outs, scratch = Names(), Names(), Names()
    hbm = pl.BlockSpec(memory_space=pl.ANY)

    def whole(shape):
        return pl.BlockSpec(shape, lambda j: (0,) * len(shape), pipeline_mode=once)

    vec = pl.BlockSpec(memory_space=pltpu.VMEM)
    ins.add(N.core, pl.BlockSpec(memory_space=pltpu.SMEM))
    for name in (N.att, N.wo, N.wu, N.wd):
        ins.add(name, hbm)
    ins.add(N.g2, vec)
    scratch.add(N.att_v, pltpu.VMEM((t, d), BF))
    scratch.add(N.wo_v, pltpu.VMEM((d, d), BF))
    scratch.add(N.wu_v, pltpu.VMEM((count, d, cut), BF))
    scratch.add(N.wd_v, pltpu.VMEM((count, cut, d), BF))
    scratch.add(N.middle_v, pltpu.VMEM((t, d), F32))
    scratch.add(N.n2_v, pltpu.VMEM((t, d), BF))
    scratch.add(N.act_v, pltpu.VMEM((2, t, cut), BF))
    if not (forward and backward):
        scratch.add(N.slope_v, pltpu.VMEM((2, t, cut), BF))
    if forward:
        ins.add(N.x, hbm)
        for name in (N.bo, N.b2, N.bd):
            ins.add(name, vec)
        ins.add(N.bu, pl.BlockSpec((weights[N.bu].shape[0], cut), lambda j: (0, j)))
        outs.add(N.next, hbm, ((t // 2 if backward else t, d), F32))
        if backward:
            outs.add(N.next_low, hbm, ((t // 2, d), BF))
            scratch.add(N.dz_low, pltpu.VMEM((t // 2, d), BF))
        scratch.add(N.x_v, pltpu.VMEM((t, d), arrays[N.x].dtype))
        scratch.add(N.next_v, pltpu.VMEM((t, d), F32))
    if backward:
        for name in (N.dza, N.dzb) if N.dzb in arrays else (N.dza,):
            ins.add(name, hbm)
        if not forward:
            for name in (N.g, N.middle, N.n2, N.act, N.slope):
                ins.add(name, hbm)
        outs.add(N.dm, hbm, ((t, d), F32))
        outs.add(N.da, hbm, ((t, d), BF))
        outs.add(N.sums, whole((8, d)), ((8, d), F32))
        outs.add(N.sums_ff, pl.BlockSpec((8, cut), lambda j: (0, j)), ((8, ff), F32))
        for kind in (N.keep, N.send):
            outs.add(N.wo_ + kind, whole((d // 2, d)), ((d // 2, d), BF))
            outs.add(N.wu_ + kind, pl.BlockSpec((d // 2, cut), lambda j: (0, j)), ((d // 2, ff), BF))
            outs.add(N.wd_ + kind, pl.BlockSpec((cut // 2, d), lambda j: (j, 0)), ((ff // 2, d), BF))
        scratch.add(N.dz_v, pltpu.VMEM((t, d), BF))
        scratch.add(N.dn_v, pltpu.VMEM((t, d), F32))
        scratch.add(N.dh_v, pltpu.VMEM((t, d), BF))
        scratch.add(N.dm_v, pltpu.VMEM((t, d), F32))
        scratch.add(N.da_v, pltpu.VMEM((t, d), BF))
    else:
        outs.add(N.middle, hbm, ((t, d), F32))
        outs.add(N.n2, hbm, ((t, d), BF))
        outs.add(N.act, hbm, ((t, ff), BF))
        outs.add(N.slope, hbm, ((t, ff), BF))
    scratch.add(N.sems, pltpu.SemaphoreType.DMA((3 + 2 * count + (t // block) * (6 + 2 * count),)))
    everything = {**weights, **arrays}
    if sums is not None:
        for i, (array, spec) in enumerate(zip(sums.inputs(), sums.in_specs())):
            ins.add(tag(N.sum_i, i), spec)
            everything[tag(N.sum_i, i)] = array
        for i, (shape, spec) in enumerate(zip(sums.out_shapes(), sums.out_specs())):
            outs.add(tag(N.sum_o, i), spec, (shape.shape, shape.dtype))
        for i, shape in enumerate(sums.scratch()):
            scratch.add(tag(N.sum_s, i), shape)
    if sums is None:
        compiler_params = params(62)
    else:
        compiler_params = pltpu.CompilerParams(
            vmem_limit_bytes=62 << 20, collective_id=collective_id, has_side_effects=True
        )

    def kernel(*refs, names):
        ffn_kernel(
            layer,
            *refs,
            names=[N.layer] + names,
            forward=forward,
            backward=backward,
            block=block,
            chunks=(d // devices, ff // devices),
            sums=sums,
        )

    found = pl.pallas_call(
        functools.partial(kernel, names=ins.names + outs.names + scratch.names),
        grid=(count,),
        in_specs=ins.specs,
        out_specs=outs.specs,
        out_shape=[jax.ShapeDtypeStruct(*shape) for shape in outs.shapes],
        scratch_shapes=scratch.specs,
        compiler_params=compiler_params,
        cost_estimate=cost((10e9 if forward else 0) + (18e9 if backward else 0)),
        name=N.feed_forward + (N._both if forward and backward else N._back if backward else ""),
    )(*[everything[name] for name in ins.names])
    return dict(zip(outs.names, found))


N_VECTORS = 12


def joined_back_kernel(*refs, names, layer, rows, block, sums):
    r = dict(zip(names, refs))
    last = sums is not None
    t, d = r[N.x_v].shape
    spans = [slice(i, i + block) for i in range(0, t, block)]
    half = len(spans) // 2
    order = list(range(half, len(spans))) + list(range(half)) if last else list(range(len(spans)))
    copies = Copies(r[N.sems])
    copies.add((N.weight,), r[N.weight].at[layer], r[N.weight_v])
    for i, at in enumerate(spans):
        for name in (N.dq, N.x, N.dm, N.normed):
            copies.add((name, i), r[name].at[at], r[name + N._v].at[at])
        copies.add((N.dkv, i), r[N.dkv].at[:, at], r[N.dkv_v].at[:, at])
        copies.add((N.dkvi, i), r[N.dkvi].at[:, :, at], r[N.dkvi_v].at[:, :, at])
        if not last or i < half:
            copies.add((N.g, i), r[N.dm_v].at[at], r[N.g].at[at])
        if not last:
            copies.add((N.low, i), r[N.low_v].at[at], r[N.low].at[at])
    for i in order:
        for name in (N.dq, N.dkv, N.dkvi):
            copies.start(name, i)
        if not last:
            if i == order[0]:
                copies.start(N.weight)
            for name in (N.x, N.dm):
                copies.start(name, i)
    if last:
        copies.start(N.weight)
        for i in order:
            for name in (N.x, N.dm):
                copies.start(name, i)
            if i == order[half - 1]:
                for j in order:
                    copies.start(N.normed, j)
        place = Place(sums.count)
        parts = sums.parts(
            place, [], [ref for name, ref in r.items() if name.startswith(N.sum_o)], [ref for name, ref in r.items() if name.startswith(N.sum_s)]
        )
        trade = Trade(place, r[N.low_v].at[t // 2 :], r[N.got], r[N.trade_sems])
    else:
        for i in order:
            copies.start(N.normed, i)
    totals = [0.0] * 4

    def gather(i):
        at = spans[i]
        for name in (N.dq, N.dkv, N.dkvi):
            copies.wait(name, i)
        r[N.df_v][at, :d] = r[N.dq_v][at]
        for k in range(2):
            got = jnp.concatenate([r[N.dkvi_v][h, k, at] for h in range(d // 128)], axis=1)
            cols = slice((k + 1) * d, (k + 2) * d)
            r[N.df_v][at, cols] = (r[N.dkv_v][k, at].astype(F32) + got.astype(F32)).astype(BF)

    def back(i):
        at = spans[i]
        up = dot(r[N.df_v][at], r[N.weight_v][...], NT)
        copies.wait(N.x, i)
        copies.wait(N.dm, i)
        unit, inverse = normalise(r[N.x_v][at].astype(F32))
        found = (up * unit, up, r[N.df_v][at, :d].astype(F32), r[N.df_v][at, 2 * d :].astype(F32))
        for k in range(4):
            totals[k] = totals[k] + column_sum(found[k])
        g = r[N.dm_v][at] + norm_back(up, r[N.gain][layer : layer + 1, :], unit, inverse)
        r[N.dm_v][at] = g
        r[N.low_v][at] = g.astype(BF)
        if not last or i < half:
            copies.start(N.g, i)
        if not last:
            copies.start(N.low, i)

    def product(k):
        return grad_dot(r[N.normed_v][...], r[N.df_v][:, k * d : (k + 1) * d])

    if not last:
        copies.wait(N.weight)
        for i in order:
            gather(i)
            back(i)
        for i in order:
            copies.wait(N.normed, i)
        for k, total in enumerate(totals):
            r[N.sums][k : k + 1, :] = total
        core = r[N.core][0]
        for k in range(3):
            cols = slice(k * d, (k + 1) * d)
            deliver(core, product(k), rows, r[N.keep].at[:, cols], r[N.send].at[:, cols])
    else:
        vectors = r[N.vectors]

        def swap(stage):
            return pltpu.make_async_remote_copy(
                src_ref=r[N.vectors_s].at[stage],
                dst_ref=r[N.vectors_v].at[stage],
                send_sem=r[N.vector_sems].at[0, stage],
                recv_sem=r[N.vector_sems].at[1, stage],
                device_id=place.partner(path[stage]),
                device_id_type=pl.DeviceIdType.MESH,
            )

        path = [0] + list(range(2, sums.stages)) + [1]

        def send_vectors(stage):
            if stage > 0:
                swap(stage - 1).wait()
                vectors[...] += r[N.vectors_v][stage - 1]
            if stage < sums.stages:
                r[N.vectors_s][stage] = vectors[...]
                swap(stage).start()

        for i in order:
            gather(i)
        copies.wait(N.weight)
        for i in order[:half]:
            back(i)
        place.greet()
        trade.copy().start()
        for i in order:
            copies.wait(N.normed, i)
        each = len(parts) // 3
        for k in range(3):
            made = product(k)
            for n in range(each):
                parts[each * k + n].fill(made[:, n * (d // each) : (n + 1) * (d // each)], rows)
                parts[each * k + n].begin(0)
        for i in order[half:]:
            back(i)
        for k, total in enumerate(totals):
            vectors[k : k + 1, :] = total
        for l in range(2):
            base = N_VECTORS * l
            if l > 0:
                vectors[base : base + 4, :] = r[N.sums_in][0:4, :]
            vectors[base + 4 : base + 8, :] = r[tag(N.sums, l)][0:4, :]
            for k in range(4):
                vectors[base + 8 + k : base + 9 + k, :] = r[tag(N.sums_ff, l)][0:1, k * d : (k + 1) * d]
        send_vectors(0)
        for stage in range(1, sums.stages + 1):
            sums.advance(parts, stage)
            send_vectors(stage)
        trade.copy().wait()
    for i in order:
        if not last or i < half:
            copies.wait(N.g, i)
        if not last:
            copies.wait(N.low, i)


def joined_back_call(arrays, layer, devices, sums=None, collective_id=0):
    t, d = arrays[N.x].shape
    last = sums is not None
    block = min(BLOCK, t // 2)
    ins, outs, scratch = Names(), Names(), Names()
    hbm = pl.BlockSpec(memory_space=pl.ANY)
    vmem = pl.BlockSpec(memory_space=pltpu.VMEM)
    ins.add(N.core, pl.BlockSpec(memory_space=pltpu.SMEM))
    for name in (N.dq, N.dkv, N.dkvi, N.x, N.dm, N.normed, N.weight):
        ins.add(name, hbm)
        shape = arrays[name].shape
        scratch.add(name + N._v, pltpu.VMEM(shape[1:] if name == N.weight else shape, arrays[name].dtype))
    ins.add(N.gain, vmem)
    scratch.add(N.df_v, pltpu.VMEM((t, 3 * d), BF))
    scratch.add(N.low_v, pltpu.VMEM((t, d), BF))
    outs.add(N.g, hbm, ((t // 2 if last else t, d), F32))
    if last:
        for name in (N.sums_in, *(tag(x, l) for x in (N.sums, N.sums_ff) for l in range(2))):
            ins.add(name, vmem)
        outs.add(N.got, hbm, ((t // 2, d), BF))
        outs.add(N.vectors, vmem, ((2 * N_VECTORS, d), F32))
        for i, (shape, spec) in enumerate(zip(sums.out_shapes(), sums.out_specs())):
            outs.add(tag(N.sum_o, i), vmem, (shape.shape, shape.dtype))
        for i, shape in enumerate(sums.scratch()):
            scratch.add(tag(N.sum_s, i), shape)
        for name in (N.vectors_s, N.vectors_v):
            scratch.add(name, pltpu.VMEM((sums.stages, 2 * N_VECTORS, d), F32))
        scratch.add(N.vector_sems, pltpu.SemaphoreType.DMA((2, sums.stages)))
        scratch.add(N.trade_sems, pltpu.SemaphoreType.DMA((2,)))
        compiler_params = pltpu.CompilerParams(
            vmem_limit_bytes=62 << 20, collective_id=collective_id, has_side_effects=True
        )
    else:
        outs.add(N.low, hbm, ((t, d), BF))
        outs.add(N.sums, vmem, ((8, d), F32))
        for kind in (N.keep, N.send):
            outs.add(kind, vmem, ((d // 2, 3 * d), BF))
        compiler_params = params(62)
    scratch.add(N.sems, pltpu.SemaphoreType.DMA((1 + (t // block) * 8,)))
    found = pl.pallas_call(
        functools.partial(
            joined_back_kernel,
            names=ins.names + outs.names + scratch.names,
            layer=layer,
            rows=d // devices,
            block=block,
            sums=sums,
        ),
        grid=(1,),
        in_specs=ins.specs,
        out_specs=outs.specs,
        out_shape=[jax.ShapeDtypeStruct(*shape) for shape in outs.shapes],
        scratch_shapes=scratch.specs,
        compiler_params=compiler_params,
        cost_estimate=cost(18e9 if last else 8e9),
        name=N.joined_back + (N._sums if last else ""),
    )(*[arrays[name] for name in ins.names])
    return dict(zip(outs.names, found))


def finish_kernel(place, *refs, names, devices):
    r = dict(zip(names, refs))
    chip, index = place[0], place[1]
    sems = r[N.sems]
    plain = []
    for cells in (N.block, N.input):
        plain.append((r[cells + N._own], r[cells + N._out].at[chip]))
    for m in range(4):
        for l in range(2):
            plain.append((r[tag(N.m, m, l)], r[tag(N.mat, m)].at[l]))
    copies = [pltpu.make_async_copy(src, dst, sems.at[i]) for i, (src, dst) in enumerate(plain)]
    n = len(copies)
    for copy in copies:
        copy.start()
    outs = []
    for i, cells in enumerate((N.block, N.input)):
        r[cells + N._wide][...] = r[cells + N._got][...].astype(F32)
        copy = pltpu.make_async_copy(r[cells + N._wide], r[cells + N._out].at[1 - chip], sems.at[n + i])
        copy.start()
        outs.append(copy)
    v = r[N.vectors]
    d = v.shape[1]
    piece = d // devices

    def cut(x, start, width):
        return pltpu.roll(x, lax.rem(d - start, d), 1)[:, :width]

    for l in range(2):
        mine = v[N_VECTORS * l : N_VECTORS * l + 8, :]
        ff = v[N_VECTORS * l + 8 : N_VECTORS * l + 12, :]
        rows = cut(mine, index * piece, piece)
        for name, k in ((N.v0, 0), (N.v1, 1), (N.v4, 7), (N.v5, 5), (N.v6, 6), (N.v8, 4)):
            r[name][l : l + 1, :] = rows[k : k + 1]
        per = devices // 2
        qv = cut(mine, lax.rem(index, per) * (2 * piece), 2 * piece)
        r[N.qv][l : l + 1, :] = jnp.where(index < per, qv[2:3], qv[3:4])
        per = devices // 4
        up = cut(ff, lax.rem(index, per) * (4 * piece), 4 * piece)
        at = index // per
        r[N.up][l : l + 1, :] = jnp.where(
            at < 2, jnp.where(at == 0, up[0:1], up[1:2]), jnp.where(at == 2, up[2:3], up[3:4])
        )
    for copy in copies + outs:
        copy.wait()


def finish_call(place, arrays, devices, genes, ff):
    d = arrays[N.vectors].shape[1]
    piece = d // devices
    ins, outs, scratch = Names(), Names(), Names()
    hbm = pl.BlockSpec(memory_space=pl.ANY)
    vmem = pl.BlockSpec(memory_space=pltpu.VMEM)
    for name in arrays:
        ins.add(name, vmem)
    for cells in (N.block, N.input):
        outs.add(cells + N._out, hbm, ((2, genes, d), F32))
        scratch.add(cells + N._wide, pltpu.VMEM((genes, d), F32))
    for m in range(4):
        outs.add(tag(N.mat, m), hbm, ((2,) + arrays[tag(N.m, m, 0)].shape, F32))
    for name in (N.v0, N.v1, N.v4, N.v5, N.v6, N.v8):
        outs.add(name, vmem, ((2, piece), F32))
    outs.add(N.qv, vmem, ((2, 2 * piece), F32))
    outs.add(N.up, vmem, ((2, ff // devices), F32))
    scratch.add(N.sems, pltpu.SemaphoreType.DMA((12,)))
    found = pl.pallas_call(
        functools.partial(finish_kernel, names=ins.names + outs.names + scratch.names, devices=devices),
        grid=(1,),
        in_specs=[pl.BlockSpec(memory_space=pltpu.SMEM)] + ins.specs,
        out_specs=outs.specs,
        out_shape=[jax.ShapeDtypeStruct(*shape) for shape in outs.shapes],
        scratch_shapes=scratch.specs,
        compiler_params=params(62),
        cost_estimate=cost(2e9),
        name=N.finish,
    )(place, *[arrays[name] for name in ins.names])
    return dict(zip(outs.names, found))


def on_device(
    device_count,
    cell_tokens,
    first_gain,
    first_bias,
    joined_weight,
    query_value_bias,
    output_weight,
    output_bias,
    second_gain,
    second_bias,
    up_weight,
    up_bias,
    down_weight,
    down_bias,
    cotangent,
    gene_mask,
):
    _, genes, d = cell_tokens.shape
    layers = joined_weight.shape[0]
    seq = lax.axis_index(N.seq)
    index = lax.axis_index(N.dp) * 4 + seq
    chip, core = seq // 2, seq % 2
    core_ref = core.astype(jnp.int32).reshape(1)
    across = [(0, 2), (1, 3), (2, 0), (3, 1)]

    x = cell_tokens
    weights = dict(
        core=core_ref,
        wo=output_weight,
        wu=up_weight,
        wd=down_weight,
        bo=output_bias,
        g2=second_gain,
        b2=second_bias,
        bu=up_bias,
        bd=down_bias,
    )
    chunks = device_count
    saved = []
    for layer in range(layers):
        top = layer == layers - 1
        seeds = (cotangent, gene_mask) if layer == 0 else ()
        joined = qkv_call(x, layer, chunks, first_gain, first_bias, joined_weight, query_value_bias, 2 * layers + 1 + layer, seeds)
        if seeds:
            g = joined[N.seed_own], lax.ppermute(joined[N.seed_send], N.seq, across)
        normed, q, kv, kvo = (joined[name] for name in (N.normed, N.q, N.kv, N.kvo))
        x = joined.get(N.held, x)
        att, lse = attend_call(q, kv, kvo)
        arrays = dict(att=att, x=x)
        if top:
            arrays.update(dza=g[0], dzb=g[1])
        found = ffn_call(layer, chunks, arrays, weights, True, top)
        saved.append((x, normed, q, kv, kvo, att, lse, found))
        x = found[N.next]

    dp_bits = list(range(2, device_count.bit_length() - 1))
    orders = (
        [1] + dp_bits,
        dp_bits[:1] + dp_bits[1:-1] + [1] + dp_bits[-1:],
        dp_bits[1:-1] + [1] + dp_bits[:1] + dp_bits[-1:],
    )

    def job(keep, send):
        split = (chunks // 2, 2 * keep.shape[0] // chunks, keep.shape[1])
        return Job(keep.reshape(split), send.reshape(split), device_count, orders)

    final = {}
    waiting, back = None, None
    for layer in reversed(range(layers)):
        x, normed, q, kv, kvo, att, lse, found = saved[layer]
        top, bottom = layer == layers - 1, layer == 0
        if not top:
            arrays = dict(att=att, g=back[N.g], dza=back[N.low], **{k: found[k] for k in (N.middle, N.n2, N.act, N.slope)})
            found = ffn_call(layer, chunks, arrays, weights, False, True, Sums([waiting], device_count), layers + layer)
            final[tag(N.m, 0, layer + 1)] = found[tag(N.sum_o, 0)]
        jobs = [job(found[w + N._keep], found[w + N._send]) for w in (N.wo, N.wu, N.wd)]
        trade_out = found[N.next_low] if top else None
        dq, dkv, dkvi, *done = attend_back_call(
            q, kv, kvo, found[N.da], att, lse, Sums(jobs, device_count, trade_out, 3), layer
        )
        if top:
            final[N.block_own], final[N.block_got] = found[N.next], done.pop()
        for i in range(3):
            final[tag(N.m, i + 1, layer)] = done[i]
        final[tag(N.sums, layer)], final[tag(N.sums_ff, layer)] = found[N.sums], found[N.sums_ff]
        arrays = dict(
            core=core_ref, dq=dq, dkv=dkv, dkvi=dkvi, x=x, dm=found[N.dm], normed=normed, weight=joined_weight, gain=first_gain
        )
        if bottom:
            arrays.update(sums_in=back[N.sums])
            for l in range(2):
                arrays.update({tag(N.sums, l): final.pop(tag(N.sums, l)), tag(N.sums_ff, l): final.pop(tag(N.sums_ff, l))})
            late = (orders[1], dp_bits[1:-1] + dp_bits[:1] + [1] + dp_bits[-1:]) * 3
            made = Job(None, None, device_count, late, (d // chunks, 3 * d))
            back = joined_back_call(arrays, layer, chunks, Sums([made], device_count), 2 * layers)
        else:
            back = joined_back_call(arrays, layer, chunks)
            waiting = job(back[N.keep], back[N.send])
    final.update(
        **{tag(N.m, 0, 0): back[tag(N.sum_o, 0)]}, input_own=back[N.g], input_got=back[N.got], vectors=back[N.vectors]
    )
    place = jnp.stack([chip, index]).astype(jnp.int32)
    out = finish_call(place, final, device_count, genes, up_bias.shape[1])
    return tuple(
        out[name]
        for name in (
            N.block_out,
            N.input_out,
            N.v0,
            N.v1,
            tag(N.mat, 0),
            N.qv,
            tag(N.mat, 1),
            N.v4,
            N.v5,
            N.v6,
            tag(N.mat, 2),
            N.up,
            tag(N.mat, 3),
            N.v8,
        )
    )


def solution(mesh):
    split = P(None, (N.dp, N.seq))
    split_rows = P(None, (N.dp, N.seq), None)
    tokens = P(N.dp, N.seq, None)
    return jax.shard_map(
        functools.partial(on_device, mesh.size),
        mesh=mesh,
        in_specs=(tokens,) + (P(),) * 12 + (tokens, P(N.dp, N.seq)),
        out_specs=(
            tokens,
            tokens,
            split,
            split,
            split_rows,
            split,
            split_rows,
            split,
            split,
            split,
            split_rows,
            split,
            split_rows,
            split,
        ),
        check_vma=False,
    )
```

```python
import functools

import jax
import jax.numpy as jnp
from jax import lax
from jax.experimental import pallas as pl
from jax.experimental.pallas import tpu as pltpu
from jax.sharding import PartitionSpec as P

HEAD = 64
LOG2E = 1.4426950408889634
BF = jnp.bfloat16
F32 = jnp.float32
NN = ((1,), (0,))
NT = ((1,), (1,))
SAFE = 60
BLOCK = 256
SLOTS = (0, 2, 6, 8, 10)


class _Names:
    def __getattr__(self, word):
        return word


N = _Names()


def tag(word, *numbers):
    return N._.join([word, *map(str, numbers)])


def dot(a, b, dims):
    return lax.dot_general(a, b, (dims, ((), ())), preferred_element_type=F32)


def params(mib):
    return pltpu.CompilerParams(vmem_limit_bytes=mib << 20)


def cost(products, nbytes=0):
    return pl.CostEstimate(flops=int(2 * products), bytes_accessed=int(nbytes), transcendentals=0)


def normalise(x):
    n = x.shape[-1]
    centred = x - jnp.sum(x, axis=-1, keepdims=True) * (1.0 / n)
    inverse = lax.rsqrt(jnp.sum(centred * centred, axis=-1, keepdims=True) * (1.0 / n) + 1e-05)
    return centred * inverse, inverse


def norm_back(upstream, gain, unit, inverse):
    n = unit.shape[-1]
    e = upstream * gain
    mean_e = jnp.sum(e, axis=-1, keepdims=True) * (1.0 / n)
    mean_eu = jnp.sum(e * unit, axis=-1, keepdims=True) * (1.0 / n)
    return inverse * (e - mean_e - unit * mean_eu)


def column_sum(x):
    return jnp.sum(x, axis=0, keepdims=True)


def gelu_pair(x):
    cdf = 0.5 + 0.5 * lax.erf(x * 0.7071067811865476)
    slope = jnp.exp2(x * x * (-0.5 * LOG2E)) * 0.3989422804014327
    return x * cdf, cdf + x * slope


def kernel_call(kernel, ins, in_specs, after=(), **kwargs):
    n = len(ins)
    extra = [pl.BlockSpec(memory_space=pl.ANY)] * len(after)

    def body(*refs):
        kernel(*refs[:n], *refs[n + len(after) :])

    return pl.pallas_call(body, in_specs=list(in_specs) + extra, **kwargs)(*ins, *after)


def qkv_kernel(*refs, names, layer, block, count, trading):
    r = dict(zip(names, refs))
    t, d = r[N.x_v].shape
    spans = [slice(i, i + block) for i in range(0, t, block)]
    half = len(spans) // 2
    place = Place(count)
    row = slice(layer, layer + 1)
    copies = Copies(r[N.sems])
    for k in range(3):
        cols = slice(k * d, (k + 1) * d)
        copies.add((N.weight, k), r[N.weight].at[layer, :, cols], r[N.weight_v].at[k])
    chip = place.bit(1)
    for i, at in enumerate(spans):
        if not trading:
            copies.add((N.x, i), r[N.x].at[at], r[N.x_v].at[at])
        elif i < half:
            copies.add((N.x, i), r[N.x].at[chip, at], r[N.x_v].at[at])
        if trading:
            copies.add((N.held, i), r[N.x_v].at[at], r[N.held].at[at])
        copies.add((N.normed, i), r[N.normed_v].at[at], r[N.normed].at[at])
        copies.add((N.q, i), r[N.q_v].at[at], r[N.q].at[at])
        copies.add((N.kv, i), r[N.kv_v].at[:, at], r[N.kv].at[:, at])

    def remote(src, dst, i, bit):
        return pltpu.make_async_remote_copy(
            src_ref=src,
            dst_ref=dst,
            send_sem=r[N.far_sems].at[0, i],
            recv_sem=r[N.far_sems].at[1, i],
            device_id=place.partner(bit),
            device_id_type=pl.DeviceIdType.MESH,
        )

    if trading:
        for i, cell in enumerate((chip, 1 - chip)):
            copies.add((N.seed, i), r[N.cotangent].at[cell], r[N.seed_v].at[i])
            copies.add((N.seeded, i), r[N.seed_v].at[i], r[N.seed_own if i == 0 else N.seed_send])

    def parcel(i):
        return remote(r[N.kv_v].at[:, spans[i]], r[N.kvo].at[:, spans[i]], i, 0)

    def trade(i):
        there = spans[half + i]
        return remote(r[N.x].at[1 - chip, spans[i]], r[N.x_v].at[there], len(spans) + i, 1)

    for i in range(half if trading else len(spans)):
        copies.start(N.x, i)
        if i == 0:
            for k in (1, 2, 0):
                copies.start(N.weight, k)
    place.greet(2)
    if trading:
        for i in range(half):
            trade(i).start()
        for i in range(2):
            copies.start(N.seed, i)
    waited = set()

    def weight(k):
        if k not in waited:
            copies.wait(N.weight, k)
            waited.add(k)
        return r[N.weight_v][k]

    for group in (range(half), range(half, len(spans))):
        if trading and group.start:
            masks = jnp.broadcast_to(r[N.mask][...].astype(F32)[:, None, :], (2, 8, t // 2))
            for i in range(2):
                mask = jnp.where(chip == i, masks[0], masks[1])
                copies.wait(N.seed, i)
                r[N.seed_v][i] = r[N.seed_v][i] * mask.T[:, :1].astype(BF)
                copies.start(N.seeded, i)
        for i in group:
            at = spans[i]
            if not trading or i < half:
                copies.wait(N.x, i)
            else:
                trade(i - half).wait()
            if trading:
                copies.start(N.held, i)
            unit, _ = normalise(r[N.x_v][at].astype(F32))
            normed = (unit * r[N.gain][row, :] + r[N.bias][row, :]).astype(BF)
            r[N.normed_v][at] = normed
            copies.start(N.normed, i)
            r[N.kv_v][0, at] = dot(normed, weight(1), NN).astype(BF)
            r[N.kv_v][1, at] = (dot(normed, weight(2), NN) + r[N.qv_bias][row, d:]).astype(BF)
            parcel(i).start()
            copies.start(N.kv, i)
        if trading or group.start:
            for i in group if trading else range(len(spans)):
                at = spans[i]
                r[N.q_v][at] = (dot(r[N.normed_v][at], weight(0), NN) + r[N.qv_bias][row, :d]).astype(BF)
                copies.start(N.q, i)
    if trading:
        for i in range(2):
            copies.wait(N.seeded, i)
    for i in range(len(spans)):
        for name in (N.held, N.normed, N.q, N.kv) if trading else (N.normed, N.q, N.kv):
            copies.wait(name, i)
        parcel(i).wait()


def qkv_call(x, layer, devices, gain, bias, weight, qv_bias, collective_id, seeds=()):
    trading = x.ndim == 3
    d = x.shape[-1]
    t = x.size // d
    block = min(BLOCK, t // 2)
    blocks = t // block
    ins, outs, scratch = Names(), Names(), Names()
    hbm = pl.BlockSpec(memory_space=pl.ANY)
    ins.add(N.x, hbm)
    ins.add(N.weight, hbm)
    for name in (N.gain, N.bias, N.qv_bias):
        ins.add(name, pl.BlockSpec(memory_space=pltpu.VMEM))
    if trading:
        ins.add(N.cotangent, hbm)
        ins.add(N.mask, pl.BlockSpec(memory_space=pltpu.VMEM))
        outs.add(N.held, hbm, ((t, d), x.dtype))
        for name in (N.seed_own, N.seed_send):
            outs.add(name, hbm, ((t // 2, d), BF))
        scratch.add(N.seed_v, pltpu.VMEM((2, t // 2, d), BF))
    outs.add(N.normed, hbm, ((t, d), BF))
    outs.add(N.q, hbm, ((t, d), BF))
    outs.add(N.kv, hbm, ((2, t, d), BF))
    outs.add(N.kvo, hbm, ((2, t, d), BF))
    scratch.add(N.x_v, pltpu.VMEM((t, d), x.dtype))
    scratch.add(N.normed_v, pltpu.VMEM((t, d), BF))
    scratch.add(N.q_v, pltpu.VMEM((t, d), BF))
    scratch.add(N.kv_v, pltpu.VMEM((2, t, d), BF))
    scratch.add(N.weight_v, pltpu.VMEM((3, d, d), BF))
    scratch.add(N.sems, pltpu.SemaphoreType.DMA((7 + 5 * blocks,)))
    scratch.add(N.far_sems, pltpu.SemaphoreType.DMA((2, 2 * blocks)))
    found = pl.pallas_call(
        functools.partial(
            qkv_kernel,
            names=ins.names + outs.names + scratch.names,
            layer=layer,
            block=block,
            count=devices,
            trading=trading,
        ),
        grid=(1,),
        in_specs=ins.specs,
        out_specs=outs.specs,
        out_shape=[jax.ShapeDtypeStruct(*shape) for shape in outs.shapes],
        scratch_shapes=scratch.specs,
        compiler_params=pltpu.CompilerParams(
            vmem_limit_bytes=62 << 20, collective_id=collective_id, has_side_effects=True
        ),
        cost_estimate=cost(12e9 if trading else 5e9),
        name=N.norm_qkv,
    )(x, weight, gain, bias, qv_bias, *seeds)
    return dict(zip(outs.names, found))


def attend_kernel(q, kv, kvo, out, lse, *, chunk):
    t = q.shape[0]
    c = LOG2E * HEAD**-0.5
    lows, highs = [], []

    def run(stable):
        for head in range(2):
            ls = slice(HEAD * head, HEAD * head + HEAD)
            values = []
            for ref in (kv, kvo):
                v = ref[1, :, ls].astype(F32).T.astype(BF)
                values.append(jnp.concatenate([v, jnp.ones((16, t), BF)], axis=0))

            def score(j):
                block = q[j * chunk : (j + 1) * chunk, ls]
                return [dot(ref[0, :, ls], block, NT) for ref in (kv, kvo)]

            ahead = score(0)
            for j in range(t // chunk):
                s = ahead
                if j + 1 < t // chunk:
                    ahead = score(j + 1)
                if stable:
                    shift = c * jnp.maximum(
                        jnp.max(s[0], axis=0, keepdims=True), jnp.max(s[1], axis=0, keepdims=True)
                    )
                    p = [jnp.exp2(x * c - shift).astype(BF) for x in s]
                else:
                    shift = 0.0
                    p = [jnp.exp2(x * c).astype(BF) for x in s]
                total = dot(values[0], p[0], NN) + dot(values[1], p[1], NN)
                level = total[HEAD : HEAD + 1]
                if not stable:
                    lows.append(level)
                    highs.append(level)
                cols = slice(j * chunk, (j + 1) * chunk)
                out[cols, ls] = (total[:HEAD] / level).T.astype(BF)
                lse[0, head : head + 1, cols] = shift + jnp.log2(level)

    run(False)
    low = jnp.min(functools.reduce(jnp.minimum, lows))
    high = jnp.max(functools.reduce(jnp.maximum, highs))
    fine = jnp.logical_and(low >= 2.0**-SAFE, high <= 2.0**SAFE)
    pl.when(jnp.logical_not(fine))(lambda: run(True))


def attend_call(q, kv, kvo):
    t, d = q.shape
    pairs = d // 128
    both = pl.BlockSpec((2, t, 128), lambda h: (0, 0, h))
    one = pl.BlockSpec((t, 128), lambda h: (0, h))
    return pl.pallas_call(
        functools.partial(attend_kernel, chunk=min(256, t)),
        grid=(pairs,),
        in_specs=[one, both, both],
        out_specs=[one, pl.BlockSpec((1, 8, t), lambda h: (h, 0, 0))],
        out_shape=[jax.ShapeDtypeStruct((t, d), BF), jax.ShapeDtypeStruct((pairs, 8, t), F32)],
        compiler_params=params(62),
        cost_estimate=cost(16e9),
        name=N.attend,
    )(q, kv, kvo)


class Place:
    def __init__(self, count):
        self.count = count
        self.bits = count.bit_length() - 1
        self.dp, self.seq = lax.axis_index(N.dp), lax.axis_index(N.seq)

    def bit(self, b):
        return (self.seq // (1 << b)) % 2 if b < 2 else (self.dp // (1 << (b - 2))) % 2

    def partner(self, b):
        step = 1 - 2 * self.bit(b)
        if b < 2:
            return {N.dp: self.dp, N.seq: self.seq + step * (1 << b)}
        return {N.dp: self.dp + step * (1 << (b - 2)), N.seq: self.seq}

    def greet(self, bits=None):
        bits = self.bits if bits is None else bits
        barrier = pltpu.get_barrier_semaphore()
        for b in range(bits):
            pl.semaphore_signal(barrier, inc=1, device_id=self.partner(b), device_id_type=pl.DeviceIdType.MESH)
        pl.semaphore_wait(barrier, bits)


class Job:
    def __init__(self, keep, send, count, orders, shape=None):
        self.lead = count.bit_length() - 2
        self.made = keep is None
        if not self.made:
            self.keep = keep.reshape((2,) * self.lead + keep.shape[1:])
            self.send = send.reshape((2,) * self.lead + send.shape[1:])
        self.rows, self.cols = shape or keep.shape[1:]
        self.orders = orders
        self.wide = self.cols // len(orders)
        self.dtype = BF

    def scratch(self):
        out = []
        for _ in self.orders:
            block = (self.rows, self.wide)
            out.append(pltpu.VMEM((2,) * self.lead + block, self.dtype))
            if self.made:
                out.append(pltpu.VMEM((2,) * self.lead + block, self.dtype))
            for left in range(self.lead, -1, -1):
                out.append(pltpu.VMEM((2,) * left + block, self.dtype))
        return out

    def out_shape(self):
        return jax.ShapeDtypeStruct((self.rows, self.cols), F32)


class Part:
    def __init__(self, place, job, at, keep, send, out, scratch, sems, first_sem):
        self.place, self.job, self.keep, self.send, self.out = place, job, keep, send, out
        self.order = job.orders[at]
        self.cols = slice(at * job.wide, (at + 1) * job.wide)
        self.total, self.got = scratch[0], scratch[1:]
        self.sems, self.first = sems, first_sem

    def fill(self, out, rows):
        lead = self.job.lead
        for core in range(2):

            @pl.when(self.place.bit(0) == core)
            def _(core=core):
                for at in range(2 << lead):
                    index = tuple((at >> (b + 1)) & 1 for b in reversed(range(lead)))
                    into = self.total if at % 2 == core else self.send
                    into[index] = out[at * rows : (at + 1) * rows].astype(BF)

    def own(self):
        return pltpu.make_async_copy(
            self.keep.at[(slice(None),) * (self.job.lead + 1) + (self.cols,)], self.total, self.sems.at[0, self.first]
        )

    def index(self, stage, away):
        out = []
        for b in range(self.job.lead, 0, -1):
            at = self.order.index(b) + 1
            if at < stage or (at == stage and not away):
                out.append(self.place.bit(b))
            elif at == stage:
                out.append(1 - self.place.bit(b))
            else:
                out.append(slice(None))
        return tuple(out)

    def copy(self, stage):
        if stage == 0 and self.keep is None:
            bit, src = 0, self.send
        elif stage == 0:
            bit, src = 0, self.send.at[(slice(None),) * (self.job.lead + 1) + (self.cols,)]
        else:
            bit, src = self.order[stage - 1], self.total.at[self.index(stage, True)]
        return pltpu.make_async_remote_copy(
            src_ref=src,
            dst_ref=self.got[stage],
            send_sem=self.sems.at[1, self.first + stage],
            recv_sem=self.sems.at[2, self.first + stage],
            device_id=self.place.partner(bit),
            device_id_type=pl.DeviceIdType.MESH,
        )

    def begin(self, stage):
        if stage == 0 and self.keep is not None:
            self.own().start()
        self.copy(stage).start()

    def end(self, stage):
        if stage == 0 and self.keep is not None:
            self.own().wait()
        self.copy(stage).wait()
        index = self.index(stage, False)
        if stage == len(self.order):
            self.out[:, self.cols] = self.total[index].astype(F32) + self.got[stage][...].astype(F32)
        elif stage == 0:
            self.total[...] = self.total[...] + self.got[0][...]
        else:
            self.total[index] = self.total[index] + self.got[stage][...]


class Trade:
    def __init__(self, place, src, dst, sems):
        self.ends = dict(src_ref=src, dst_ref=dst, send_sem=sems.at[0], recv_sem=sems.at[1])
        self.place = place

    def copy(self):
        return pltpu.make_async_remote_copy(
            **self.ends, device_id=self.place.partner(1), device_id_type=pl.DeviceIdType.MESH
        )


class Sums:
    def __init__(self, jobs, count, trade=None, trade_at=0):
        self.jobs, self.count, self.trade, self.trade_at = jobs, count, trade, trade_at
        self.stages = count.bit_length() - 1

    def n_ins(self):
        return 2 * sum(not job.made for job in self.jobs) + (self.trade is not None)

    def n_outs(self):
        return len(self.jobs) + (self.trade is not None)

    def inputs(self):
        return [x for job in self.jobs if not job.made for x in (job.keep, job.send)] + ([] if self.trade is None else [self.trade])

    def n_parts(self):
        return sum(len(job.orders) for job in self.jobs)

    def in_specs(self):
        return [pl.BlockSpec(memory_space=pl.ANY)] * self.n_ins()

    def out_shapes(self):
        out = [job.out_shape() for job in self.jobs]
        return out if self.trade is None else out + [jax.ShapeDtypeStruct(self.trade.shape, self.trade.dtype)]

    def out_specs(self):
        out = [pl.BlockSpec((job.rows, job.cols), lambda *_: (0, 0), pipeline_mode=pl.Buffered(1)) for job in self.jobs]
        return out if self.trade is None else out + [pl.BlockSpec(memory_space=pl.ANY)]

    def scratch(self):
        out = [x for job in self.jobs for x in job.scratch()]
        return out + [pltpu.SemaphoreType.DMA((3, self.n_parts() * self.stages)), pltpu.SemaphoreType.DMA((2,))]

    def parts(self, place, ins, outs, scratch):
        scratch = list(scratch)
        trade_sems = scratch.pop()
        sems = scratch.pop()
        found = []
        self.swap = None if self.trade is None else Trade(place, ins[-1], outs[-1], trade_sems)
        for i, job in enumerate(self.jobs):
            for at in range(len(job.orders)):
                size = job.lead + 2 + job.made
                mine, scratch = scratch[:size], scratch[size:]
                if job.made:
                    keep, send = None, mine.pop(1)
                else:
                    keep, send = ins[2 * i], ins[2 * i + 1]
                found.append(Part(place, job, at, keep, send, outs[i], mine, sems, len(found) * self.stages))
        return found

    def advance(self, parts, stage):
        for part in parts:
            if stage > 0:
                part.end(stage - 1)
            if stage < self.stages:
                part.begin(stage)
        if self.swap is not None:
            if stage == self.trade_at:
                self.swap.copy().start()
            if stage == self.stages:
                self.swap.copy().wait()


def attend_back_kernel(*refs, chunk, sums, slots):
    n_in, n_out = 6 + sums.n_ins(), 3 + sums.n_outs()
    q, kv, kvo, up, out, lse = refs[:6]
    dq, dkv, dkvi = refs[n_in : n_in + 3]
    outbox, box_sems = refs[n_in + n_out : n_in + n_out + 2]
    place = Place(sums.count)
    parts = sums.parts(place, refs[6:n_in], refs[n_in + 3 : n_in + n_out], refs[n_in + n_out + 2 :])
    t = q.shape[0]
    scale = HEAD**-0.5
    c = LOG2E * scale
    pair, pairs = pl.program_id(0), len(slots) // 2

    def parcel(at):
        return pltpu.make_async_remote_copy(
            src_ref=outbox.at[at % 2],
            dst_ref=dkvi.at[at],
            send_sem=box_sems.at[0, at],
            recv_sem=box_sems.at[1, at],
            device_id=place.partner(0),
            device_id_type=pl.DeviceIdType.MESH,
        )

    def advance(at):
        for stage in slots[at]:
            sums.advance(parts, stage)

    pl.when(pair == 0)(place.greet)
    for at in range(2, pairs):
        pl.when(pair == at)(lambda at=at: parcel(at - 2).wait_send())
    box = outbox.at[lax.rem(pair, 2)]
    for head in range(2):
        for at in range(pairs):
            if slots[2 * at + head]:
                pl.when(pair == at)(functools.partial(advance, 2 * at + head))
        ls = slice(HEAD * head, HEAD * head + HEAD)
        qh = q[:, ls]
        uh = up[:, ls]
        q_t = qh.astype(F32).T.astype(BF)
        u_t = uh.astype(F32).T.astype(BF)
        level = lse[0].T[:, head : head + 1]
        inner = jnp.sum(uh.astype(F32) * out[:, ls].astype(F32), axis=1, keepdims=True)
        blocks = [
            (src, dst, slice(i * chunk, (i + 1) * chunk))
            for src, dst in ((kvo, box), (kv, dkv))
            for i in range(t // chunk)
        ]

        def products(block):
            src, _, rows = block
            return dot(qh, src[0, rows, ls], NT), dot(uh, src[1, rows, ls], NT)

        total = None
        ahead = products(blocks[0])
        for at, (src, dst, rows) in enumerate(blocks):
            s, dp = ahead
            if at + 1 < len(blocks):
                ahead = products(blocks[at + 1])
            p = jnp.exp2(s * c - level)
            ds = (p * (dp - inner)).astype(BF)
            dst[1, rows, ls] = dot(u_t, p.astype(BF), NN).T.astype(BF)
            dst[0, rows, ls] = (dot(q_t, ds, NN).T * scale).astype(BF)
            part = dot(ds, src[0, rows, ls], NN)
            total = part if total is None else total + part
        dq[:, ls] = (total * scale).astype(BF)

    for at in range(pairs):

        @pl.when(pair == at)
        def _(at=at):
            parcel(at).start()
            if at == pairs - 1:
                advance(2 * pairs)
                for last in range(max(0, pairs - 2), pairs):
                    parcel(last).wait_send()
                for each in range(pairs):
                    parcel(each).wait_recv()


def attend_back_call(q, kv, kvo, up, out, lse, sums, collective_id):
    t, d = q.shape
    pairs = d // 128
    both = pl.BlockSpec((2, t, 128), lambda h: (0, 0, h))
    one = pl.BlockSpec((t, 128), lambda h: (0, h))
    slots = [[] for _ in range(2 * pairs + 1)]
    for stage in range(sums.stages + 1):
        slots[SLOTS[stage] if stage < min(len(SLOTS), sums.stages) else 2 * pairs].append(stage)
    return pl.pallas_call(
        functools.partial(attend_back_kernel, chunk=min(256, t), sums=sums, slots=slots),
        grid=(pairs,),
        in_specs=[one, both, both, one, one, pl.BlockSpec((1, 8, t), lambda h: (h, 0, 0))] + sums.in_specs(),
        out_specs=[one, both, pl.BlockSpec(memory_space=pl.ANY)] + sums.out_specs(),
        out_shape=[
            jax.ShapeDtypeStruct((t, d), BF),
            jax.ShapeDtypeStruct((2, t, d), BF),
            jax.ShapeDtypeStruct((pairs, 2, t, 128), BF),
        ]
        + sums.out_shapes(),
        scratch_shapes=[pltpu.VMEM((2, 2, t, 128), BF), pltpu.SemaphoreType.DMA((2, pairs))] + sums.scratch(),
        compiler_params=pltpu.CompilerParams(
            vmem_limit_bytes=60 << 20, collective_id=collective_id, has_side_effects=True
        ),
        cost_estimate=cost(37e9),
        name=N.attend_back,
    )(q, kv, kvo, up, out, lse, *sums.inputs())


def split_rows(out, rows):
    n = out.shape[0]
    even = jnp.concatenate([out[i : i + rows] for i in range(0, n, 2 * rows)], axis=0).astype(BF)
    odd = jnp.concatenate([out[i + rows : i + 2 * rows] for i in range(0, n, 2 * rows)], axis=0).astype(BF)
    return even, odd


def deliver(core, out, rows, keep, send):
    even, odd = split_rows(out, rows)

    @pl.when(core == 0)
    def _():
        keep[...] = even
        send[...] = odd

    @pl.when(core == 1)
    def _():
        keep[...] = odd
        send[...] = even


def grad_dot(a, b):
    return lax.dot_general(a, b, (((0,), (0,)), ((), ())), preferred_element_type=F32)


class Names:
    def __init__(self):
        self.names, self.specs, self.shapes = [], [], []

    def add(self, name, spec, shape=None):
        self.names.append(name)
        self.specs.append(spec)
        self.shapes.append(shape)


class Copies:
    def __init__(self, sems):
        self.sems, self.made = sems, {}

    def add(self, key, src, dst):
        self.made[key] = pltpu.make_async_copy(src, dst, self.sems.at[len(self.made)])

    def start(self, *key):
        self.made[key].start()

    def wait(self, *key):
        self.made[key].wait()


def ffn_kernel(*refs, names, forward, backward, block, chunks, sums):
    r = dict(zip(names, refs))
    if sums is not None:
        place = Place(sums.count)
        parts = sums.parts(
            place, *[[ref for name, ref in r.items() if name.startswith(kind)] for kind in (N.sum_i, N.sum_o, N.sum_s)]
        )
    layer = r[N.layer]
    row = slice(layer, layer + 1)
    j = pl.program_id(0)
    t, d = r[N.att_v].shape
    cut = r[N.wu_v].shape[2]
    count = r[N.wu_v].shape[0]
    first, final = j == 0, j == count - 1
    spans = [slice(i, i + block) for i in range(0, t, block)]
    every = range(len(spans))
    copies = Copies(r[N.sems])
    copies.add((N.wo,), r[N.wo].at[layer], r[N.wo_v])
    for i, at in enumerate(spans):
        copies.add((N.att, i), r[N.att].at[at], r[N.att_v].at[at])
        if forward:
            copies.add((N.x, i), r[N.x].at[at], r[N.x_v].at[at])
            if not backward:
                copies.add((N.next, i), r[N.next_v].at[at], r[N.next].at[at])
            elif at.start < r[N.next].shape[0]:
                copies.add((N.next, i), r[N.next_v].at[at], r[N.next].at[at])
            else:
                low = slice(at.start - r[N.next].shape[0], at.stop - r[N.next].shape[0])
                copies.add((N.next, i), r[N.dz_low].at[low], r[N.next_low].at[low])
            if not backward:
                copies.add((N.middle_o, i), r[N.middle_v].at[at], r[N.middle].at[at])
                copies.add((N.n2_o, i), r[N.n2_v].at[at], r[N.n2].at[at])
        else:
            copies.add((N.middle, i), r[N.middle].at[at], r[N.middle_v].at[at])
            copies.add((N.n2, i), r[N.n2].at[at], r[N.n2_v].at[at])
            copies.add((N.g, i), r[N.g].at[at], r[N.dm_v].at[at])
        if backward:
            copies.add((N.dm, i), r[N.dm_v].at[at], r[N.dm].at[at])
            copies.add((N.da, i), r[N.da_v].at[at], r[N.da].at[at])
    if backward:
        half = r[N.dza].shape[0]
        copies.add((N.dza,), r[N.dza], r[N.dz_v].at[:half])
        if half < t:
            copies.add((N.dzb,), r[N.dzb], r[N.dz_v].at[half:])
    for c in range(count):
        cols = slice(c * cut, (c + 1) * cut)
        copies.add((N.wu, c), r[N.wu].at[layer, :, cols], r[N.wu_v].at[c])
        copies.add((N.wd, c), r[N.wd].at[layer, cols, :], r[N.wd_v].at[c])
        if not (forward and backward):
            for name in (N.act, N.slope):
                for i, at in enumerate(spans):
                    ends = r[name].at[at, cols], r[name + N._v].at[c % 2, at]
                    copies.add((name, c, i), *(ends if backward else ends[::-1]))

    def per_chunk(act):
        for c in range(count):
            pl.when(j == c)(functools.partial(act, c))

    def feed(c):
        for i in every:
            for name in (N.act, N.slope):
                copies.start(name, c, i)

    if sums is not None:
        pl.when(first)(place.greet)

    @pl.when(first)
    def _():
        if forward:
            copies.start(N.wo)
            for i in every:
                copies.start(N.att, i)
                copies.start(N.x, i)
        if backward:
            copies.start(N.dza)
            if half < t:
                copies.start(N.dzb)
        for c in range(count):
            copies.start(N.wu, c)
            copies.start(N.wd, c)
            if c == 0 and not forward:
                feed(0)
                for i in every:
                    copies.start(N.n2, i)
        if not forward:
            for i in every:
                copies.start(N.middle, i)
                copies.start(N.g, i)
                copies.start(N.att, i)
            copies.start(N.wo)
        if forward:
            copies.wait(N.wo)
            for i, at in enumerate(spans):
                copies.wait(N.att, i)
                copies.wait(N.x, i)
                middle = r[N.x_v][at].astype(F32) + (dot(r[N.att_v][at], r[N.wo_v][...], NN) + r[N.bo][row, :])
                unit, _ = normalise(middle)
                r[N.n2_v][at] = (unit * r[N.g2][row, :] + r[N.b2][row, :]).astype(BF)
                r[N.middle_v][at] = middle
                r[N.next_v][at] = middle + r[N.bd][row, :]
                if not backward:
                    copies.start(N.middle_o, i)
                    copies.start(N.n2_o, i)
        if backward:
            r[N.dn_v][...] = jnp.zeros(r[N.dn_v].shape, F32)
            r[N.sums][...] = jnp.zeros(r[N.sums].shape, F32)
            copies.wait(N.dza)
            if half < t:
                copies.wait(N.dzb)
            r[N.sums][0:1, :] = column_sum(r[N.dz_v][...].astype(F32))
            if not forward:
                for i in every:
                    copies.wait(N.n2, i)

    @per_chunk
    def _(c):
        if sums is not None:
            sums.advance(parts, c)
        copies.wait(N.wu, c)
        copies.wait(N.wd, c)
        if not forward:
            if c + 1 < count:
                feed(c + 1)
            for i in every:
                for name in (N.act, N.slope):
                    copies.wait(name, c, i)
        elif not backward and c >= 2:
            for i in every:
                for name in (N.act, N.slope):
                    copies.wait(name, c - 2, i)

    wu, wd = r[N.wu_v].at[j], r[N.wd_v].at[j]
    slot = lax.rem(j, 2)

    def lead(at):
        return (
            dot(r[N.n2_v][at], wu[...], NN) if forward else None,
            dot(r[N.dz_v][at], wd[...], NT) if backward else None,
        )

    ff_sum = 0.0
    ahead = lead(spans[0])
    for i, at in enumerate(spans):
        hidden, da = ahead
        if i + 1 < len(spans):
            ahead = lead(spans[i + 1])
        if forward:
            act, slope = gelu_pair(hidden + r[N.bu][row, :])
            act = act.astype(BF)
            r[N.act_v][slot, at] = act
            if not backward:
                r[N.slope_v][slot, at] = slope.astype(BF)
        else:
            slope = r[N.slope_v][slot, at].astype(F32)
        if backward:
            dh = (da * slope).astype(BF)
            r[N.dh_v][at] = dh
            ff_sum = ff_sum + column_sum(dh.astype(F32))
        if forward:
            r[N.next_v][at] += dot(act, wd[...], NN)
        if backward:
            r[N.dn_v][at] += dot(dh, wu[...], NT)

    if forward:

        @per_chunk
        def _(c):
            for i in every:
                if not backward:
                    copies.start(N.act, c, i)
                    copies.start(N.slope, c, i)
                if c == count - 1:
                    if backward and spans[i].start >= r[N.next].shape[0]:
                        low = slice(spans[i].start - r[N.next].shape[0], spans[i].stop - r[N.next].shape[0])
                        r[N.dz_low][low] = r[N.next_v][spans[i]].astype(BF)
                    copies.start(N.next, i)

    if backward:
        core = Place(2).bit(0)
        r[N.sums_ff][0:1, :] = ff_sum
        deliver(core, grad_dot(r[N.act_v][slot], r[N.dz_v][...]), chunks[1], r[N.wd_keep], r[N.wd_send])
        deliver(core, grad_dot(r[N.n2_v][...], r[N.dh_v][...]), chunks[0], r[N.wu_keep], r[N.wu_send])

    @pl.when(final)
    def _():
        if sums is not None:
            for stage in range(count, sums.stages):
                sums.advance(parts, stage)
        if backward:
            if not forward:
                copies.wait(N.wo)
            for i, at in enumerate(spans):
                if not forward:
                    copies.wait(N.middle, i)
                    copies.wait(N.g, i)
                    copies.wait(N.att, i)
                g = r[N.dz_v][at].astype(F32) if forward else r[N.dm_v][at]
                unit, inverse = normalise(r[N.middle_v][at])
                up = r[N.dn_v][at]
                r[N.sums][1:2, :] += column_sum(up * unit)
                r[N.sums][2:3, :] += column_sum(up)
                dm = g + norm_back(up, r[N.g2][row, :], unit, inverse)
                r[N.dm_v][at] = dm
                copies.start(N.dm, i)
                dy = dm.astype(BF)
                r[N.dh_v][at] = dy
                r[N.sums][3:4, :] += column_sum(dy.astype(F32))
                r[N.da_v][at] = dot(dy, r[N.wo_v][...], NT).astype(BF)
                copies.start(N.da, i)
            deliver(core, grad_dot(r[N.att_v][...], r[N.dh_v][...]), chunks[0], r[N.wo_keep], r[N.wo_send])
        for i in every:
            if forward:
                copies.wait(N.next, i)
                if not backward:
                    copies.wait(N.middle_o, i)
                    copies.wait(N.n2_o, i)
                    for c in range(max(0, count - 2), count):
                        copies.wait(N.act, c, i)
                        copies.wait(N.slope, c, i)
            if backward:
                copies.wait(N.dm, i)
                copies.wait(N.da, i)
        if sums is not None:
            sums.advance(parts, sums.stages)


def ffn_call(layer, devices, arrays, weights, forward, backward, sums=None, collective_id=0):
    t, d = arrays[N.att].shape
    ff = weights[N.wu].shape[2]
    cut, count = d, ff // d
    block = min(BLOCK, t)
    once = pl.Buffered(1)
    ins, outs, scratch = Names(), Names(), Names()
    hbm = pl.BlockSpec(memory_space=pl.ANY)

    def whole(shape):
        return pl.BlockSpec(shape, lambda j: (0,) * len(shape), pipeline_mode=once)

    vec = pl.BlockSpec(memory_space=pltpu.VMEM)
    for name in (N.att, N.wo, N.wu, N.wd):
        ins.add(name, hbm)
    ins.add(N.g2, vec)
    scratch.add(N.att_v, pltpu.VMEM((t, d), BF))
    scratch.add(N.wo_v, pltpu.VMEM((d, d), BF))
    scratch.add(N.wu_v, pltpu.VMEM((count, d, cut), BF))
    scratch.add(N.wd_v, pltpu.VMEM((count, cut, d), BF))
    scratch.add(N.middle_v, pltpu.VMEM((t, d), F32))
    scratch.add(N.n2_v, pltpu.VMEM((t, d), BF))
    scratch.add(N.act_v, pltpu.VMEM((2, t, cut), BF))
    if not (forward and backward):
        scratch.add(N.slope_v, pltpu.VMEM((2, t, cut), BF))
    if forward:
        ins.add(N.x, hbm)
        for name in (N.bo, N.b2, N.bd):
            ins.add(name, vec)
        ins.add(N.bu, pl.BlockSpec((weights[N.bu].shape[0], cut), lambda j: (0, j)))
        outs.add(N.next, hbm, ((t // 2 if backward else t, d), F32))
        if backward:
            outs.add(N.next_low, hbm, ((t // 2, d), BF))
            scratch.add(N.dz_low, pltpu.VMEM((t // 2, d), BF))
        scratch.add(N.x_v, pltpu.VMEM((t, d), arrays[N.x].dtype))
        scratch.add(N.next_v, pltpu.VMEM((t, d), F32))
    if backward:
        for name in (N.dza, N.dzb) if N.dzb in arrays else (N.dza,):
            ins.add(name, hbm)
        if not forward:
            for name in (N.g, N.middle, N.n2, N.act, N.slope):
                ins.add(name, hbm)
        outs.add(N.dm, hbm, ((t, d), F32))
        outs.add(N.da, hbm, ((t, d), BF))
        outs.add(N.sums, whole((8, d)), ((8, d), F32))
        outs.add(N.sums_ff, pl.BlockSpec((8, cut), lambda j: (0, j)), ((8, ff), F32))
        for kind in (N.keep, N.send):
            outs.add(N.wo_ + kind, whole((d // 2, d)), ((d // 2, d), BF))
            outs.add(N.wu_ + kind, pl.BlockSpec((d // 2, cut), lambda j: (0, j)), ((d // 2, ff), BF))
            outs.add(N.wd_ + kind, pl.BlockSpec((cut // 2, d), lambda j: (j, 0)), ((ff // 2, d), BF))
        scratch.add(N.dz_v, pltpu.VMEM((t, d), BF))
        scratch.add(N.dn_v, pltpu.VMEM((t, d), F32))
        scratch.add(N.dh_v, pltpu.VMEM((t, d), BF))
        scratch.add(N.dm_v, pltpu.VMEM((t, d), F32))
        scratch.add(N.da_v, pltpu.VMEM((t, d), BF))
    else:
        outs.add(N.middle, hbm, ((t, d), F32))
        outs.add(N.n2, hbm, ((t, d), BF))
        outs.add(N.act, hbm, ((t, ff), BF))
        outs.add(N.slope, hbm, ((t, ff), BF))
    scratch.add(N.sems, pltpu.SemaphoreType.DMA((3 + 2 * count + (t // block) * (6 + 2 * count),)))
    everything = {**weights, **arrays}
    if sums is not None:
        for i, (array, spec) in enumerate(zip(sums.inputs(), sums.in_specs())):
            ins.add(tag(N.sum_i, i), spec)
            everything[tag(N.sum_i, i)] = array
        for i, (shape, spec) in enumerate(zip(sums.out_shapes(), sums.out_specs())):
            outs.add(tag(N.sum_o, i), spec, (shape.shape, shape.dtype))
        for i, shape in enumerate(sums.scratch()):
            scratch.add(tag(N.sum_s, i), shape)
    if sums is None:
        compiler_params = params(62)
    else:
        compiler_params = pltpu.CompilerParams(
            vmem_limit_bytes=62 << 20, collective_id=collective_id, has_side_effects=True
        )

    def kernel(*refs, names):
        ffn_kernel(
            layer,
            *refs,
            names=[N.layer] + names,
            forward=forward,
            backward=backward,
            block=block,
            chunks=(d // devices, ff // devices),
            sums=sums,
        )

    found = pl.pallas_call(
        functools.partial(kernel, names=ins.names + outs.names + scratch.names),
        grid=(count,),
        in_specs=ins.specs,
        out_specs=outs.specs,
        out_shape=[jax.ShapeDtypeStruct(*shape) for shape in outs.shapes],
        scratch_shapes=scratch.specs,
        compiler_params=compiler_params,
        cost_estimate=cost((10e9 if forward else 0) + (18e9 if backward else 0)),
        name=N.feed_forward + (N._both if forward and backward else N._back if backward else ""),
    )(*[everything[name] for name in ins.names])
    return dict(zip(outs.names, found))


N_VECTORS = 12


def joined_back_kernel(*refs, names, layer, rows, block, sums):
    r = dict(zip(names, refs))
    last = sums is not None
    t, d = r[N.x_v].shape
    spans = [slice(i, i + block) for i in range(0, t, block)]
    half = len(spans) // 2
    order = list(range(half, len(spans))) + list(range(half)) if last else list(range(len(spans)))
    copies = Copies(r[N.sems])
    copies.add((N.weight,), r[N.weight].at[layer], r[N.weight_v])
    for i, at in enumerate(spans):
        for name in (N.dq, N.x, N.dm, N.normed):
            copies.add((name, i), r[name].at[at], r[name + N._v].at[at])
        copies.add((N.dkv, i), r[N.dkv].at[:, at], r[N.dkv_v].at[:, at])
        copies.add((N.dkvi, i), r[N.dkvi].at[:, :, at], r[N.dkvi_v].at[:, :, at])
        if not last or i < half:
            copies.add((N.g, i), r[N.dm_v].at[at], r[N.g].at[at])
        if not last:
            copies.add((N.low, i), r[N.low_v].at[at], r[N.low].at[at])
    for i in order:
        for name in (N.dq, N.dkv, N.dkvi):
            copies.start(name, i)
        if not last:
            if i == order[0]:
                copies.start(N.weight)
            for name in (N.x, N.dm):
                copies.start(name, i)
    if last:
        for i in order:
            copies.start(N.normed, i)
        copies.start(N.weight)
        for i in order:
            for name in (N.x, N.dm):
                copies.start(name, i)
        place = Place(sums.count)
        parts = sums.parts(
            place, [], [ref for name, ref in r.items() if name.startswith(N.sum_o)], [ref for name, ref in r.items() if name.startswith(N.sum_s)]
        )
        trade = Trade(place, r[N.low_v].at[t // 2 :], r[N.got], r[N.trade_sems])
    else:
        for i in order:
            copies.start(N.normed, i)
    totals = [0.0] * 4

    def gather(i):
        at = spans[i]
        for name in (N.dq, N.dkv, N.dkvi):
            copies.wait(name, i)
        r[N.df_v][at, :d] = r[N.dq_v][at]
        for k in range(2):
            got = jnp.concatenate([r[N.dkvi_v][h, k, at] for h in range(d // 128)], axis=1)
            cols = slice((k + 1) * d, (k + 2) * d)
            r[N.df_v][at, cols] = (r[N.dkv_v][k, at].astype(F32) + got.astype(F32)).astype(BF)

    def back(i):
        at = spans[i]
        up = dot(r[N.df_v][at], r[N.weight_v][...], NT)
        copies.wait(N.x, i)
        copies.wait(N.dm, i)
        unit, inverse = normalise(r[N.x_v][at].astype(F32))
        found = (up * unit, up, r[N.df_v][at, :d].astype(F32), r[N.df_v][at, 2 * d :].astype(F32))
        for k in range(4):
            totals[k] = totals[k] + column_sum(found[k])
        g = r[N.dm_v][at] + norm_back(up, r[N.gain][layer : layer + 1, :], unit, inverse)
        r[N.dm_v][at] = g
        r[N.low_v][at] = g.astype(BF)
        if not last or i < half:
            copies.start(N.g, i)
        if not last:
            copies.start(N.low, i)

    def product(k):
        return grad_dot(r[N.normed_v][...], r[N.df_v][:, k * d : (k + 1) * d])

    if not last:
        copies.wait(N.weight)
        for i in order:
            gather(i)
            back(i)
        for i in order:
            copies.wait(N.normed, i)
        for k, total in enumerate(totals):
            r[N.sums][k : k + 1, :] = total
        core = Place(2).bit(0)
        for k in range(3):
            cols = slice(k * d, (k + 1) * d)
            deliver(core, product(k), rows, r[N.keep].at[:, cols], r[N.send].at[:, cols])
    else:
        vectors = r[N.vectors]

        def swap(stage):
            return pltpu.make_async_remote_copy(
                src_ref=r[N.vectors_s].at[stage],
                dst_ref=r[N.vectors_v].at[stage],
                send_sem=r[N.vector_sems].at[0, stage],
                recv_sem=r[N.vector_sems].at[1, stage],
                device_id=place.partner(path[stage]),
                device_id_type=pl.DeviceIdType.MESH,
            )

        path = [0] + list(range(2, sums.stages)) + [1]

        def send_vectors(stage):
            if stage > 0:
                swap(stage - 1).wait()
                vectors[...] += r[N.vectors_v][stage - 1]
            if stage < sums.stages:
                r[N.vectors_s][stage] = vectors[...]
                swap(stage).start()

        for i in order:
            gather(i)
        for i in order:
            copies.wait(N.normed, i)
        each = len(parts) // 3
        for k in range(3):
            made = product(k)
            for n in range(each):
                parts[each * k + n].fill(made[:, n * (d // each) : (n + 1) * (d // each)], rows)
                if k == n == 0:
                    place.greet()
                parts[each * k + n].begin(0)
        copies.wait(N.weight)
        for i in order[:half]:
            back(i)
        trade.copy().start()
        sums.advance(parts, 1)
        for i in order[half:]:
            back(i)
        for k, total in enumerate(totals):
            vectors[k : k + 1, :] = total
        for l in range(2):
            base = N_VECTORS * l
            if l > 0:
                vectors[base : base + 4, :] = r[N.sums_in][0:4, :]
            vectors[base + 4 : base + 8, :] = r[tag(N.sums, l)][0:4, :]
            for k in range(4):
                vectors[base + 8 + k : base + 9 + k, :] = r[tag(N.sums_ff, l)][0:1, k * d : (k + 1) * d]
        send_vectors(0)
        for stage in range(1, sums.stages + 1):
            if stage > 1:
                sums.advance(parts, stage)
            send_vectors(stage)
        trade.copy().wait()
    for i in order:
        if not last or i < half:
            copies.wait(N.g, i)
        if not last:
            copies.wait(N.low, i)


def joined_back_call(arrays, layer, devices, sums=None, collective_id=0):
    t, d = arrays[N.x].shape
    last = sums is not None
    block = min(BLOCK, t // 2)
    ins, outs, scratch = Names(), Names(), Names()
    hbm = pl.BlockSpec(memory_space=pl.ANY)
    vmem = pl.BlockSpec(memory_space=pltpu.VMEM)
    for name in (N.dq, N.dkv, N.dkvi, N.x, N.dm, N.normed, N.weight):
        ins.add(name, hbm)
        shape = arrays[name].shape
        scratch.add(name + N._v, pltpu.VMEM(shape[1:] if name == N.weight else shape, arrays[name].dtype))
    ins.add(N.gain, vmem)
    scratch.add(N.df_v, pltpu.VMEM((t, 3 * d), BF))
    scratch.add(N.low_v, pltpu.VMEM((t, d), BF))
    outs.add(N.g, hbm, ((t // 2 if last else t, d), F32))
    if last:
        for name in (N.sums_in, *(tag(x, l) for x in (N.sums, N.sums_ff) for l in range(2))):
            ins.add(name, vmem)
        outs.add(N.got, hbm, ((t // 2, d), BF))
        outs.add(N.vectors, vmem, ((2 * N_VECTORS, d), F32))
        for i, (shape, spec) in enumerate(zip(sums.out_shapes(), sums.out_specs())):
            outs.add(tag(N.sum_o, i), vmem, (shape.shape, shape.dtype))
        for i, shape in enumerate(sums.scratch()):
            scratch.add(tag(N.sum_s, i), shape)
        for name in (N.vectors_s, N.vectors_v):
            scratch.add(name, pltpu.VMEM((sums.stages, 2 * N_VECTORS, d), F32))
        scratch.add(N.vector_sems, pltpu.SemaphoreType.DMA((2, sums.stages)))
        scratch.add(N.trade_sems, pltpu.SemaphoreType.DMA((2,)))
        compiler_params = pltpu.CompilerParams(
            vmem_limit_bytes=62 << 20, collective_id=collective_id, has_side_effects=True
        )
    else:
        outs.add(N.low, hbm, ((t, d), BF))
        outs.add(N.sums, vmem, ((8, d), F32))
        for kind in (N.keep, N.send):
            outs.add(kind, vmem, ((d // 2, 3 * d), BF))
        compiler_params = params(62)
    scratch.add(N.sems, pltpu.SemaphoreType.DMA((1 + (t // block) * 8,)))
    found = pl.pallas_call(
        functools.partial(
            joined_back_kernel,
            names=ins.names + outs.names + scratch.names,
            layer=layer,
            rows=d // devices,
            block=block,
            sums=sums,
        ),
        grid=(1,),
        in_specs=ins.specs,
        out_specs=outs.specs,
        out_shape=[jax.ShapeDtypeStruct(*shape) for shape in outs.shapes],
        scratch_shapes=scratch.specs,
        compiler_params=compiler_params,
        cost_estimate=cost(18e9 if last else 8e9),
        name=N.joined_back + (N._sums if last else ""),
    )(*[arrays[name] for name in ins.names])
    return dict(zip(outs.names, found))


def finish_kernel(*refs, names, devices):
    r = dict(zip(names, refs))
    place = Place(devices)
    chip, index = place.bit(1), place.dp * 4 + place.seq
    copies, moves = Copies(r[N.sems]), []
    for cells in (N.block, N.input):
        moves.append((cells + N._got, None, None))
        moves.append((cells + N._own, cells + N._out, chip))
    for m in range(4):
        for l in range(2):
            moves.append((tag(N.m, m, l), tag(N.mat, m), l))
    for name, out, at in moves:
        copies.add((name, 0), r[name], r[name + N._v])
        if out is not None:
            copies.add((name, 1), r[name + N._v], r[out].at[at])
    for cells in (N.block, N.input):
        copies.add((cells,), r[cells + N._wide], r[cells + N._out].at[1 - chip])
    for name, _, _ in moves:
        copies.start(name, 0)
    for name, out, _ in moves:
        copies.wait(name, 0)
        if out is not None:
            copies.start(name, 1)
        else:
            cells = N.block if name == N.block_got else N.input
            r[cells + N._wide][...] = r[name + N._v][...].astype(F32)
            copies.start(cells)
    v = r[N.vectors]
    d = v.shape[1]
    piece = d // devices

    def cut(x, start, width):
        return pltpu.roll(x, lax.rem(d - start, d), 1)[:, :width]

    for l in range(2):
        mine = v[N_VECTORS * l : N_VECTORS * l + 8, :]
        ff = v[N_VECTORS * l + 8 : N_VECTORS * l + 12, :]
        rows = cut(mine, index * piece, piece)
        for name, k in ((N.v0, 0), (N.v1, 1), (N.v4, 7), (N.v5, 5), (N.v6, 6), (N.v8, 4)):
            r[name][l : l + 1, :] = rows[k : k + 1]
        per = devices // 2
        qv = cut(mine, lax.rem(index, per) * (2 * piece), 2 * piece)
        r[N.qv][l : l + 1, :] = jnp.where(index < per, qv[2:3], qv[3:4])
        per = devices // 4
        up = cut(ff, lax.rem(index, per) * (4 * piece), 4 * piece)
        at = index // per
        r[N.up][l : l + 1, :] = jnp.where(
            at < 2, jnp.where(at == 0, up[0:1], up[1:2]), jnp.where(at == 2, up[2:3], up[3:4])
        )
    for name, out, _ in moves:
        if out is not None:
            copies.wait(name, 1)
    copies.wait(N.block)
    copies.wait(N.input)


def finish_call(arrays, devices, genes, ff):
    d = arrays[N.vectors].shape[1]
    piece = d // devices
    ins, outs, scratch = Names(), Names(), Names()
    hbm = pl.BlockSpec(memory_space=pl.ANY)
    vmem = pl.BlockSpec(memory_space=pltpu.VMEM)
    for name, array in arrays.items():
        ins.add(name, vmem if name == N.vectors else hbm)
        if name != N.vectors:
            scratch.add(name + N._v, pltpu.VMEM(array.shape, array.dtype))
    for cells in (N.block, N.input):
        outs.add(cells + N._out, hbm, ((2, genes, d), F32))
        scratch.add(cells + N._wide, pltpu.VMEM((genes, d), F32))
    for m in range(4):
        outs.add(tag(N.mat, m), hbm, ((2,) + arrays[tag(N.m, m, 0)].shape, F32))
    for name in (N.v0, N.v1, N.v4, N.v5, N.v6, N.v8):
        outs.add(name, vmem, ((2, piece), F32))
    outs.add(N.qv, vmem, ((2, 2 * piece), F32))
    outs.add(N.up, vmem, ((2, ff // devices), F32))
    scratch.add(N.sems, pltpu.SemaphoreType.DMA((24,)))
    found = pl.pallas_call(
        functools.partial(finish_kernel, names=ins.names + outs.names + scratch.names, devices=devices),
        grid=(1,),
        in_specs=ins.specs,
        out_specs=outs.specs,
        out_shape=[jax.ShapeDtypeStruct(*shape) for shape in outs.shapes],
        scratch_shapes=scratch.specs,
        compiler_params=params(62),
        cost_estimate=cost(2e9),
        name=N.finish,
    )(*[arrays[name] for name in ins.names])
    return dict(zip(outs.names, found))


def on_device(
    device_count,
    cell_tokens,
    first_gain,
    first_bias,
    joined_weight,
    query_value_bias,
    output_weight,
    output_bias,
    second_gain,
    second_bias,
    up_weight,
    up_bias,
    down_weight,
    down_bias,
    cotangent,
    gene_mask,
):
    _, genes, d = cell_tokens.shape
    layers = joined_weight.shape[0]
    seq = lax.axis_index(N.seq)
    across = [(0, 2), (1, 3), (2, 0), (3, 1)]

    x = cell_tokens
    weights = dict(
        wo=output_weight,
        wu=up_weight,
        wd=down_weight,
        bo=output_bias,
        g2=second_gain,
        b2=second_bias,
        bu=up_bias,
        bd=down_bias,
    )
    chunks = device_count
    saved = []
    for layer in range(layers):
        top = layer == layers - 1
        seeds = (cotangent, gene_mask) if layer == 0 else ()
        joined = qkv_call(x, layer, chunks, first_gain, first_bias, joined_weight, query_value_bias, 2 * layers + 1 + layer, seeds)
        if seeds:
            g = joined[N.seed_own], lax.ppermute(joined[N.seed_send], N.seq, across)
        normed, q, kv, kvo = (joined[name] for name in (N.normed, N.q, N.kv, N.kvo))
        x = joined.get(N.held, x)
        att, lse = attend_call(q, kv, kvo)
        arrays = dict(att=att, x=x)
        if top:
            arrays.update(dza=g[0], dzb=g[1])
        found = ffn_call(layer, chunks, arrays, weights, True, top)
        saved.append((x, normed, q, kv, kvo, att, lse, found))
        x = found[N.next]

    dp_bits = list(range(2, device_count.bit_length() - 1))
    orders = (
        [1] + dp_bits,
        dp_bits[:1] + dp_bits[1:-1] + [1] + dp_bits[-1:],
        dp_bits[1:-1] + [1] + dp_bits[:1] + dp_bits[-1:],
    )

    def job(keep, send):
        split = (chunks // 2, 2 * keep.shape[0] // chunks, keep.shape[1])
        return Job(keep.reshape(split), send.reshape(split), device_count, orders)

    final = {}
    waiting, back = None, None
    for layer in reversed(range(layers)):
        x, normed, q, kv, kvo, att, lse, found = saved[layer]
        top, bottom = layer == layers - 1, layer == 0
        if not top:
            arrays = dict(att=att, g=back[N.g], dza=back[N.low], **{k: found[k] for k in (N.middle, N.n2, N.act, N.slope)})
            found = ffn_call(layer, chunks, arrays, weights, False, True, Sums([waiting], device_count), layers + layer)
            final[tag(N.m, 0, layer + 1)] = found[tag(N.sum_o, 0)]
        jobs = [job(found[w + N._keep], found[w + N._send]) for w in (N.wo, N.wu, N.wd)]
        trade_out = found[N.next_low] if top else None
        dq, dkv, dkvi, *done = attend_back_call(
            q, kv, kvo, found[N.da], att, lse, Sums(jobs, device_count, trade_out, 3), layer
        )
        if top:
            final[N.block_own], final[N.block_got] = found[N.next], done.pop()
        for i in range(3):
            final[tag(N.m, i + 1, layer)] = done[i]
        final[tag(N.sums, layer)], final[tag(N.sums_ff, layer)] = found[N.sums], found[N.sums_ff]
        arrays = dict(
            dq=dq, dkv=dkv, dkvi=dkvi, x=x, dm=found[N.dm], normed=normed, weight=joined_weight, gain=first_gain
        )
        if bottom:
            arrays.update(sums_in=back[N.sums])
            for l in range(2):
                arrays.update({tag(N.sums, l): final.pop(tag(N.sums, l)), tag(N.sums_ff, l): final.pop(tag(N.sums_ff, l))})
            late = (orders[1], dp_bits[1:-1] + dp_bits[:1] + [1] + dp_bits[-1:]) * 3
            made = Job(None, None, device_count, late, (d // chunks, 3 * d))
            back = joined_back_call(arrays, layer, chunks, Sums([made], device_count), 2 * layers)
        else:
            back = joined_back_call(arrays, layer, chunks)
            waiting = job(back[N.keep], back[N.send])
    final.update(
        **{tag(N.m, 0, 0): back[tag(N.sum_o, 0)]}, input_own=back[N.g], input_got=back[N.got], vectors=back[N.vectors]
    )
    out = finish_call(final, device_count, genes, up_bias.shape[1])
    return tuple(
        out[name]
        for name in (
            N.block_out,
            N.input_out,
            N.v0,
            N.v1,
            tag(N.mat, 0),
            N.qv,
            tag(N.mat, 1),
            N.v4,
            N.v5,
            N.v6,
            tag(N.mat, 2),
            N.up,
            tag(N.mat, 3),
            N.v8,
        )
    )


def solution(mesh):
    split = P(None, (N.dp, N.seq))
    split_rows = P(None, (N.dp, N.seq), None)
    tokens = P(N.dp, N.seq, None)
    return jax.shard_map(
        functools.partial(on_device, mesh.size),
        mesh=mesh,
        in_specs=(tokens,) + (P(),) * 12 + (tokens, P(N.dp, N.seq)),
        out_specs=(
            tokens,
            tokens,
            split,
            split,
            split_rows,
            split,
            split_rows,
            split,
            split,
            split,
            split_rows,
            split,
            split_rows,
            split,
        ),
        check_vma=False,
    )
```

```python
import functools

import jax
import jax.numpy as jnp
from jax import lax
from jax.experimental import pallas as pl
from jax.experimental.pallas import tpu as pltpu
from jax.sharding import PartitionSpec as P

HEAD = 64
LOG2E = 1.4426950408889634
BF = jnp.bfloat16
F32 = jnp.float32
NN = ((1,), (0,))
NT = ((1,), (1,))
SAFE = 60
BLOCK = 256
SLOTS = (0, 2, 6, 8, 10)


class _Names:
    def __getattr__(self, word):
        return word


N = _Names()


def tag(word, *numbers):
    return N._.join([word, *map(str, numbers)])


def dot(a, b, dims):
    return lax.dot_general(a, b, (dims, ((), ())), preferred_element_type=F32)


def params(mib):
    return pltpu.CompilerParams(vmem_limit_bytes=mib << 20)


def cost(products, nbytes=0):
    return pl.CostEstimate(flops=int(2 * products), bytes_accessed=int(nbytes), transcendentals=0)


def normalise(x):
    n = x.shape[-1]
    centred = x - jnp.sum(x, axis=-1, keepdims=True) * (1.0 / n)
    inverse = lax.rsqrt(jnp.sum(centred * centred, axis=-1, keepdims=True) * (1.0 / n) + 1e-05)
    return centred * inverse, inverse


def norm_back(upstream, gain, unit, inverse):
    n = unit.shape[-1]
    e = upstream * gain
    mean_e = jnp.sum(e, axis=-1, keepdims=True) * (1.0 / n)
    mean_eu = jnp.sum(e * unit, axis=-1, keepdims=True) * (1.0 / n)
    return inverse * (e - mean_e - unit * mean_eu)


def column_sum(x):
    return jnp.sum(x, axis=0, keepdims=True)


def gelu_pair(x):
    cdf = 0.5 + 0.5 * lax.erf(x * 0.7071067811865476)
    slope = jnp.exp2(x * x * (-0.5 * LOG2E)) * 0.3989422804014327
    return x * cdf, cdf + x * slope


def kernel_call(kernel, ins, in_specs, after=(), **kwargs):
    n = len(ins)
    extra = [pl.BlockSpec(memory_space=pl.ANY)] * len(after)

    def body(*refs):
        kernel(*refs[:n], *refs[n + len(after) :])

    return pl.pallas_call(body, in_specs=list(in_specs) + extra, **kwargs)(*ins, *after)


def qkv_kernel(*refs, names, layer, block, count, trading):
    r = dict(zip(names, refs))
    t, d = r[N.x_v].shape
    spans = [slice(i, i + block) for i in range(0, t, block)]
    half = len(spans) // 2
    place = Place(count)
    row = slice(layer, layer + 1)
    copies = Copies(r[N.sems])
    for k in range(3):
        cols = slice(k * d, (k + 1) * d)
        copies.add((N.weight, k), r[N.weight].at[layer, :, cols], r[N.weight_v].at[k])
    chip = place.bit(1)
    for i, at in enumerate(spans):
        if not trading:
            copies.add((N.x, i), r[N.x].at[at], r[N.x_v].at[at])
        elif i < half:
            copies.add((N.x, i), r[N.x].at[chip, at], r[N.x_v].at[at])
        if trading:
            copies.add((N.held, i), r[N.x_v].at[at], r[N.held].at[at])
        copies.add((N.normed, i), r[N.normed_v].at[at], r[N.normed].at[at])
        copies.add((N.q, i), r[N.q_v].at[at], r[N.q].at[at])
        copies.add((N.kv, i), r[N.kv_v].at[:, at], r[N.kv].at[:, at])

    def remote(src, dst, i, bit):
        return pltpu.make_async_remote_copy(
            src_ref=src,
            dst_ref=dst,
            send_sem=r[N.far_sems].at[0, i],
            recv_sem=r[N.far_sems].at[1, i],
            device_id=place.partner(bit),
            device_id_type=pl.DeviceIdType.MESH,
        )

    if trading:
        for i, cell in enumerate((chip, 1 - chip)):
            copies.add((N.seed, i), r[N.cotangent].at[cell], r[N.seed_v].at[i])
            copies.add((N.seeded, i), r[N.seed_v].at[i], r[N.seed_own if i == 0 else N.seed_send])

    def parcel(i):
        return remote(r[N.kv_v].at[:, spans[i]], r[N.kvo].at[:, spans[i]], i, 0)

    def trade(i):
        there = spans[half + i]
        return remote(r[N.x].at[1 - chip, spans[i]], r[N.x_v].at[there], len(spans) + i, 1)

    for i in range(half if trading else len(spans)):
        copies.start(N.x, i)
        if i == 0:
            for k in (1, 2, 0):
                copies.start(N.weight, k)
    place.greet(2)
    if trading:
        for i in range(half):
            trade(i).start()
        for i in range(2):
            copies.start(N.seed, i)
    waited = set()

    def weight(k):
        if k not in waited:
            copies.wait(N.weight, k)
            waited.add(k)
        return r[N.weight_v][k]

    for group in (range(half), range(half, len(spans))):
        if trading and group.start:
            masks = jnp.broadcast_to(r[N.mask][...].astype(F32)[:, None, :], (2, 8, t // 2))
            for i in range(2):
                mask = jnp.where(chip == i, masks[0], masks[1])
                copies.wait(N.seed, i)
                r[N.seed_v][i] = r[N.seed_v][i] * mask.T[:, :1].astype(BF)
                copies.start(N.seeded, i)
        for i in group:
            at = spans[i]
            if not trading or i < half:
                copies.wait(N.x, i)
            else:
                trade(i - half).wait()
            if trading:
                copies.start(N.held, i)
            unit, _ = normalise(r[N.x_v][at].astype(F32))
            normed = (unit * r[N.gain][row, :] + r[N.bias][row, :]).astype(BF)
            r[N.normed_v][at] = normed
            copies.start(N.normed, i)
            r[N.kv_v][0, at] = dot(normed, weight(1), NN).astype(BF)
            r[N.kv_v][1, at] = (dot(normed, weight(2), NN) + r[N.qv_bias][row, d:]).astype(BF)
            parcel(i).start()
            copies.start(N.kv, i)
        if trading or group.start:
            for i in group if trading else range(len(spans)):
                at = spans[i]
                r[N.q_v][at] = (dot(r[N.normed_v][at], weight(0), NN) + r[N.qv_bias][row, :d]).astype(BF)
                copies.start(N.q, i)
    if trading:
        for i in range(2):
            copies.wait(N.seeded, i)
    for i in range(len(spans)):
        for name in (N.held, N.normed, N.q, N.kv) if trading else (N.normed, N.q, N.kv):
            copies.wait(name, i)
        parcel(i).wait()


def qkv_call(x, layer, devices, gain, bias, weight, qv_bias, collective_id, seeds=()):
    trading = x.ndim == 3
    d = x.shape[-1]
    t = x.size // d
    block = min(BLOCK, t // 2)
    blocks = t // block
    ins, outs, scratch = Names(), Names(), Names()
    hbm = pl.BlockSpec(memory_space=pl.ANY)
    ins.add(N.x, hbm)
    ins.add(N.weight, hbm)
    for name in (N.gain, N.bias, N.qv_bias):
        ins.add(name, pl.BlockSpec(memory_space=pltpu.VMEM))
    if trading:
        ins.add(N.cotangent, hbm)
        ins.add(N.mask, pl.BlockSpec(memory_space=pltpu.VMEM))
        outs.add(N.held, hbm, ((t, d), x.dtype))
        for name in (N.seed_own, N.seed_send):
            outs.add(name, hbm, ((t // 2, d), BF))
        scratch.add(N.seed_v, pltpu.VMEM((2, t // 2, d), BF))
    outs.add(N.normed, hbm, ((t, d), BF))
    outs.add(N.q, hbm, ((t, d), BF))
    outs.add(N.kv, hbm, ((2, t, d), BF))
    outs.add(N.kvo, hbm, ((2, t, d), BF))
    scratch.add(N.x_v, pltpu.VMEM((t, d), x.dtype))
    scratch.add(N.normed_v, pltpu.VMEM((t, d), BF))
    scratch.add(N.q_v, pltpu.VMEM((t, d), BF))
    scratch.add(N.kv_v, pltpu.VMEM((2, t, d), BF))
    scratch.add(N.weight_v, pltpu.VMEM((3, d, d), BF))
    scratch.add(N.sems, pltpu.SemaphoreType.DMA((7 + 5 * blocks,)))
    scratch.add(N.far_sems, pltpu.SemaphoreType.DMA((2, 2 * blocks)))
    found = pl.pallas_call(
        functools.partial(
            qkv_kernel,
            names=ins.names + outs.names + scratch.names,
            layer=layer,
            block=block,
            count=devices,
            trading=trading,
        ),
        grid=(1,),
        in_specs=ins.specs,
        out_specs=outs.specs,
        out_shape=[jax.ShapeDtypeStruct(*shape) for shape in outs.shapes],
        scratch_shapes=scratch.specs,
        compiler_params=pltpu.CompilerParams(
            vmem_limit_bytes=62 << 20, collective_id=collective_id, has_side_effects=True
        ),
        cost_estimate=cost(12e9 if trading else 5e9),
        name=N.norm_qkv,
    )(x, weight, gain, bias, qv_bias, *seeds)
    return dict(zip(outs.names, found))


def attend_kernel(q, kv, kvo, out, lse, *, chunk):
    t = q.shape[0]
    c = LOG2E * HEAD**-0.5
    lows, highs = [], []

    def run(stable):
        for head in range(2):
            ls = slice(HEAD * head, HEAD * head + HEAD)
            values = []
            for ref in (kv, kvo):
                v = ref[1, :, ls].astype(F32).T.astype(BF)
                values.append(jnp.concatenate([v, jnp.ones((16, t), BF)], axis=0))

            def score(j):
                block = q[j * chunk : (j + 1) * chunk, ls]
                return [dot(ref[0, :, ls], block, NT) for ref in (kv, kvo)]

            ahead = score(0)
            for j in range(t // chunk):
                s = ahead
                if j + 1 < t // chunk:
                    ahead = score(j + 1)
                if stable:
                    shift = c * jnp.maximum(
                        jnp.max(s[0], axis=0, keepdims=True), jnp.max(s[1], axis=0, keepdims=True)
                    )
                    p = [jnp.exp2(x * c - shift).astype(BF) for x in s]
                else:
                    shift = 0.0
                    p = [jnp.exp2(x * c).astype(BF) for x in s]
                total = dot(values[0], p[0], NN) + dot(values[1], p[1], NN)
                level = total[HEAD : HEAD + 1]
                if not stable:
                    lows.append(level)
                    highs.append(level)
                cols = slice(j * chunk, (j + 1) * chunk)
                out[cols, ls] = (total[:HEAD] / level).T.astype(BF)
                lse[0, head : head + 1, cols] = shift + jnp.log2(level)

    run(False)
    low = jnp.min(functools.reduce(jnp.minimum, lows))
    high = jnp.max(functools.reduce(jnp.maximum, highs))
    fine = jnp.logical_and(low >= 2.0**-SAFE, high <= 2.0**SAFE)
    pl.when(jnp.logical_not(fine))(lambda: run(True))


def attend_call(q, kv, kvo):
    t, d = q.shape
    pairs = d // 128
    both = pl.BlockSpec((2, t, 128), lambda h: (0, 0, h))
    one = pl.BlockSpec((t, 128), lambda h: (0, h))
    return pl.pallas_call(
        functools.partial(attend_kernel, chunk=min(256, t)),
        grid=(pairs,),
        in_specs=[one, both, both],
        out_specs=[one, pl.BlockSpec((1, 8, t), lambda h: (h, 0, 0))],
        out_shape=[jax.ShapeDtypeStruct((t, d), BF), jax.ShapeDtypeStruct((pairs, 8, t), F32)],
        compiler_params=params(62),
        cost_estimate=cost(16e9),
        name=N.attend,
    )(q, kv, kvo)


class Place:
    def __init__(self, count):
        self.count = count
        self.bits = count.bit_length() - 1
        self.dp, self.seq = lax.axis_index(N.dp), lax.axis_index(N.seq)

    def bit(self, b):
        return (self.seq // (1 << b)) % 2 if b < 2 else (self.dp // (1 << (b - 2))) % 2

    def partner(self, b):
        step = 1 - 2 * self.bit(b)
        if b < 2:
            return {N.dp: self.dp, N.seq: self.seq + step * (1 << b)}
        return {N.dp: self.dp + step * (1 << (b - 2)), N.seq: self.seq}

    def greet(self, bits=None):
        bits = self.bits if bits is None else bits
        barrier = pltpu.get_barrier_semaphore()
        for b in range(bits):
            pl.semaphore_signal(barrier, inc=1, device_id=self.partner(b), device_id_type=pl.DeviceIdType.MESH)
        pl.semaphore_wait(barrier, bits)


class Job:
    def __init__(self, both, count, orders, shape=None):
        self.lead = count.bit_length() - 2
        self.made = both is None
        if not self.made:
            self.both = both.reshape((2,) * (self.lead + 1) + both.shape[2:])
        self.rows, self.cols = shape or both.shape[2:]
        self.orders = orders
        self.wide = self.cols // len(orders)
        self.dtype = BF

    def scratch(self):
        out = []
        for _ in self.orders:
            block = (self.rows, self.wide)
            out.append(pltpu.VMEM((2,) * (self.lead + self.made) + block, self.dtype))
            for left in range(self.lead, -1, -1):
                out.append(pltpu.VMEM((2,) * left + block, self.dtype))
        return out

    def out_shape(self):
        return jax.ShapeDtypeStruct((self.rows, self.cols), F32)


class Part:
    def __init__(self, place, job, at, both, out, scratch, sems, first_sem):
        self.place, self.job, self.both, self.out = place, job, both, out
        self.order = job.orders[at]
        self.cols = slice(at * job.wide, (at + 1) * job.wide)
        self.total, self.got = scratch[0], scratch[1:]
        self.sems, self.first = sems, first_sem
        self.every = (slice(None),) * (job.lead + 1)
        self.pre = (place.bit(0),) if job.made else ()

    def fill(self, out, rows):
        lead = self.job.lead
        for at in range(2 << lead):
            index = (at % 2,) + tuple((at >> (b + 1)) & 1 for b in reversed(range(lead)))
            self.total[index] = out[at * rows : (at + 1) * rows].astype(BF)

    def own(self):
        return pltpu.make_async_copy(
            self.both.at[(self.place.bit(0),) + self.every + (self.cols,)], self.total, self.sems.at[0, self.first]
        )

    def index(self, stage, away):
        out = []
        for b in range(self.job.lead, 0, -1):
            at = self.order.index(b) + 1
            if at < stage or (at == stage and not away):
                out.append(self.place.bit(b))
            elif at == stage:
                out.append(1 - self.place.bit(b))
            else:
                out.append(slice(None))
        return tuple(out)

    def copy(self, stage):
        if stage == 0 and self.job.made:
            bit, src = 0, self.total.at[1 - self.place.bit(0)]
        elif stage == 0:
            bit, src = 0, self.both.at[(1 - self.place.bit(0),) + self.every + (self.cols,)]
        else:
            bit, src = self.order[stage - 1], self.total.at[self.pre + self.index(stage, True)]
        return pltpu.make_async_remote_copy(
            src_ref=src,
            dst_ref=self.got[stage],
            send_sem=self.sems.at[1, self.first + stage],
            recv_sem=self.sems.at[2, self.first + stage],
            device_id=self.place.partner(bit),
            device_id_type=pl.DeviceIdType.MESH,
        )

    def begin(self, stage):
        if stage == 0 and not self.job.made:
            self.own().start()
        self.copy(stage).start()

    def end(self, stage):
        if stage == 0 and not self.job.made:
            self.own().wait()
        self.copy(stage).wait()
        index = self.pre + self.index(stage, False)
        if stage == len(self.order):
            self.out[:, self.cols] = self.total[index].astype(F32) + self.got[stage][...].astype(F32)
        elif stage == 0:
            index = self.pre + self.every
            self.total[index] = self.total[index] + self.got[0][...]
        else:
            self.total[index] = self.total[index] + self.got[stage][...]


class Trade:
    def __init__(self, place, src, dst, sems):
        self.ends = dict(src_ref=src, dst_ref=dst, send_sem=sems.at[0], recv_sem=sems.at[1])
        self.place = place

    def copy(self):
        return pltpu.make_async_remote_copy(
            **self.ends, device_id=self.place.partner(1), device_id_type=pl.DeviceIdType.MESH
        )


class Sums:
    def __init__(self, jobs, count, trade=None, trade_at=0):
        self.jobs, self.count, self.trade, self.trade_at = jobs, count, trade, trade_at
        self.stages = count.bit_length() - 1

    def n_ins(self):
        return sum(not job.made for job in self.jobs) + (self.trade is not None)

    def n_outs(self):
        return len(self.jobs) + (self.trade is not None)

    def inputs(self):
        return [job.both for job in self.jobs if not job.made] + ([] if self.trade is None else [self.trade])

    def n_parts(self):
        return sum(len(job.orders) for job in self.jobs)

    def in_specs(self):
        return [pl.BlockSpec(memory_space=pl.ANY)] * self.n_ins()

    def out_shapes(self):
        out = [job.out_shape() for job in self.jobs]
        return out if self.trade is None else out + [jax.ShapeDtypeStruct(self.trade.shape, self.trade.dtype)]

    def out_specs(self):
        out = [pl.BlockSpec((job.rows, job.cols), lambda *_: (0, 0), pipeline_mode=pl.Buffered(1)) for job in self.jobs]
        return out if self.trade is None else out + [pl.BlockSpec(memory_space=pl.ANY)]

    def scratch(self):
        out = [x for job in self.jobs for x in job.scratch()]
        return out + [pltpu.SemaphoreType.DMA((3, self.n_parts() * self.stages)), pltpu.SemaphoreType.DMA((2,))]

    def parts(self, place, ins, outs, scratch):
        scratch = list(scratch)
        trade_sems = scratch.pop()
        sems = scratch.pop()
        found = []
        self.swap = None if self.trade is None else Trade(place, ins[-1], outs[-1], trade_sems)
        for i, job in enumerate(self.jobs):
            for at in range(len(job.orders)):
                mine, scratch = scratch[: job.lead + 2], scratch[job.lead + 2 :]
                both = None if job.made else ins[i]
                found.append(Part(place, job, at, both, outs[i], mine, sems, len(found) * self.stages))
        return found

    def advance(self, parts, stage):
        for part in parts:
            if stage > 0:
                part.end(stage - 1)
            if stage < self.stages:
                part.begin(stage)
        if self.swap is not None:
            if stage == self.trade_at:
                self.swap.copy().start()
            if stage == self.stages:
                self.swap.copy().wait()


def attend_back_kernel(*refs, chunk, sums, slots):
    n_in, n_out = 6 + sums.n_ins(), 3 + sums.n_outs()
    q, kv, kvo, up, out, lse = refs[:6]
    dq, dkv, dkvi = refs[n_in : n_in + 3]
    outbox, box_sems = refs[n_in + n_out : n_in + n_out + 2]
    place = Place(sums.count)
    parts = sums.parts(place, refs[6:n_in], refs[n_in + 3 : n_in + n_out], refs[n_in + n_out + 2 :])
    t = q.shape[0]
    scale = HEAD**-0.5
    c = LOG2E * scale
    pair, pairs = pl.program_id(0), len(slots) // 2

    def parcel(at):
        return pltpu.make_async_remote_copy(
            src_ref=outbox.at[at % 2],
            dst_ref=dkvi.at[at],
            send_sem=box_sems.at[0, at],
            recv_sem=box_sems.at[1, at],
            device_id=place.partner(0),
            device_id_type=pl.DeviceIdType.MESH,
        )

    def advance(at):
        for stage in slots[at]:
            sums.advance(parts, stage)

    pl.when(pair == 0)(place.greet)
    for at in range(2, pairs):
        pl.when(pair == at)(lambda at=at: parcel(at - 2).wait_send())
    box = outbox.at[lax.rem(pair, 2)]
    for head in range(2):
        for at in range(pairs):
            if slots[2 * at + head]:
                pl.when(pair == at)(functools.partial(advance, 2 * at + head))
        ls = slice(HEAD * head, HEAD * head + HEAD)
        qh = q[:, ls]
        uh = up[:, ls]
        q_t = qh.astype(F32).T.astype(BF)
        u_t = uh.astype(F32).T.astype(BF)
        level = lse[0].T[:, head : head + 1]
        inner = jnp.sum(uh.astype(F32) * out[:, ls].astype(F32), axis=1, keepdims=True)
        blocks = [
            (src, dst, slice(i * chunk, (i + 1) * chunk))
            for src, dst in ((kvo, box), (kv, dkv))
            for i in range(t // chunk)
        ]

        def products(block):
            src, _, rows = block
            return dot(qh, src[0, rows, ls], NT), dot(uh, src[1, rows, ls], NT)

        total = None
        ahead = products(blocks[0])
        for at, (src, dst, rows) in enumerate(blocks):
            s, dp = ahead
            if at + 1 < len(blocks):
                ahead = products(blocks[at + 1])
            p = jnp.exp2(s * c - level)
            ds = (p * (dp - inner)).astype(BF)
            dst[1, rows, ls] = dot(u_t, p.astype(BF), NN).T.astype(BF)
            dst[0, rows, ls] = (dot(q_t, ds, NN).T * scale).astype(BF)
            part = dot(ds, src[0, rows, ls], NN)
            total = part if total is None else total + part
        dq[:, ls] = (total * scale).astype(BF)

    for at in range(pairs):

        @pl.when(pair == at)
        def _(at=at):
            parcel(at).start()
            if at == pairs - 1:
                advance(2 * pairs)
                for last in range(max(0, pairs - 2), pairs):
                    parcel(last).wait_send()
                for each in range(pairs):
                    parcel(each).wait_recv()


def attend_back_call(q, kv, kvo, up, out, lse, sums, collective_id):
    t, d = q.shape
    pairs = d // 128
    both = pl.BlockSpec((2, t, 128), lambda h: (0, 0, h))
    one = pl.BlockSpec((t, 128), lambda h: (0, h))
    slots = [[] for _ in range(2 * pairs + 1)]
    for stage in range(sums.stages + 1):
        slots[SLOTS[stage] if stage < min(len(SLOTS), sums.stages) else 2 * pairs].append(stage)
    return pl.pallas_call(
        functools.partial(attend_back_kernel, chunk=min(256, t), sums=sums, slots=slots),
        grid=(pairs,),
        in_specs=[one, both, both, one, one, pl.BlockSpec((1, 8, t), lambda h: (h, 0, 0))] + sums.in_specs(),
        out_specs=[one, both, pl.BlockSpec(memory_space=pl.ANY)] + sums.out_specs(),
        out_shape=[
            jax.ShapeDtypeStruct((t, d), BF),
            jax.ShapeDtypeStruct((2, t, d), BF),
            jax.ShapeDtypeStruct((pairs, 2, t, 128), BF),
        ]
        + sums.out_shapes(),
        scratch_shapes=[pltpu.VMEM((2, 2, t, 128), BF), pltpu.SemaphoreType.DMA((2, pairs))] + sums.scratch(),
        compiler_params=pltpu.CompilerParams(
            vmem_limit_bytes=60 << 20, collective_id=collective_id, has_side_effects=True
        ),
        cost_estimate=cost(37e9),
        name=N.attend_back,
    )(q, kv, kvo, up, out, lse, *sums.inputs())


def split_rows(out, rows):
    n = out.shape[0]
    even = jnp.concatenate([out[i : i + rows] for i in range(0, n, 2 * rows)], axis=0).astype(BF)
    odd = jnp.concatenate([out[i + rows : i + 2 * rows] for i in range(0, n, 2 * rows)], axis=0).astype(BF)
    return even, odd


def deliver(out, rows, both):
    both[0], both[1] = split_rows(out, rows)


def grad_dot(a, b):
    return lax.dot_general(a, b, (((0,), (0,)), ((), ())), preferred_element_type=F32)


class Names:
    def __init__(self):
        self.names, self.specs, self.shapes = [], [], []

    def add(self, name, spec, shape=None):
        self.names.append(name)
        self.specs.append(spec)
        self.shapes.append(shape)


class Copies:
    def __init__(self, sems):
        self.sems, self.made = sems, {}

    def add(self, key, src, dst):
        self.made[key] = pltpu.make_async_copy(src, dst, self.sems.at[len(self.made)])

    def start(self, *key):
        self.made[key].start()

    def wait(self, *key):
        self.made[key].wait()


def ffn_kernel(*refs, names, forward, backward, block, chunks, sums):
    r = dict(zip(names, refs))
    if sums is not None:
        place = Place(sums.count)
        parts = sums.parts(
            place, *[[ref for name, ref in r.items() if name.startswith(kind)] for kind in (N.sum_i, N.sum_o, N.sum_s)]
        )
    layer = r[N.layer]
    row = slice(layer, layer + 1)
    j = pl.program_id(0)
    t, d = r[N.att_v].shape
    cut = r[N.wu_v].shape[2]
    count = r[N.wu_v].shape[0]
    first, final = j == 0, j == count - 1
    spans = [slice(i, i + block) for i in range(0, t, block)]
    every = range(len(spans))
    copies = Copies(r[N.sems])
    copies.add((N.wo,), r[N.wo].at[layer], r[N.wo_v])
    for i, at in enumerate(spans):
        copies.add((N.att, i), r[N.att].at[at], r[N.att_v].at[at])
        if forward:
            copies.add((N.x, i), r[N.x].at[at], r[N.x_v].at[at])
            if not backward:
                copies.add((N.next, i), r[N.next_v].at[at], r[N.next].at[at])
            elif at.start < r[N.next].shape[0]:
                copies.add((N.next, i), r[N.next_v].at[at], r[N.next].at[at])
            else:
                low = slice(at.start - r[N.next].shape[0], at.stop - r[N.next].shape[0])
                copies.add((N.next, i), r[N.dz_low].at[low], r[N.next_low].at[low])
            if not backward:
                copies.add((N.middle_o, i), r[N.middle_v].at[at], r[N.middle].at[at])
                copies.add((N.n2_o, i), r[N.n2_v].at[at], r[N.n2].at[at])
        else:
            copies.add((N.middle, i), r[N.middle].at[at], r[N.middle_v].at[at])
            copies.add((N.n2, i), r[N.n2].at[at], r[N.n2_v].at[at])
            copies.add((N.g, i), r[N.g].at[at], r[N.dm_v].at[at])
        if backward:
            copies.add((N.dm, i), r[N.dm_v].at[at], r[N.dm].at[at])
            copies.add((N.da, i), r[N.da_v].at[at], r[N.da].at[at])
    if backward:
        half = r[N.dza].shape[0]
        copies.add((N.dza,), r[N.dza], r[N.dz_v].at[:half])
        if half < t:
            copies.add((N.dzb,), r[N.dzb], r[N.dz_v].at[half:])
    for c in range(count):
        cols = slice(c * cut, (c + 1) * cut)
        copies.add((N.wu, c), r[N.wu].at[layer, :, cols], r[N.wu_v].at[c])
        copies.add((N.wd, c), r[N.wd].at[layer, cols, :], r[N.wd_v].at[c])
        if not (forward and backward):
            for name in (N.act, N.slope):
                for i, at in enumerate(spans):
                    ends = r[name].at[at, cols], r[name + N._v].at[c % 2, at]
                    copies.add((name, c, i), *(ends if backward else ends[::-1]))

    def per_chunk(act):
        for c in range(count):
            pl.when(j == c)(functools.partial(act, c))

    def feed(c):
        for i in every:
            for name in (N.act, N.slope):
                copies.start(name, c, i)

    if sums is not None:
        pl.when(first)(place.greet)

    @pl.when(first)
    def _():
        if forward:
            copies.start(N.wo)
            for i in every:
                copies.start(N.att, i)
                copies.start(N.x, i)
        if backward:
            copies.start(N.dza)
            if half < t:
                copies.start(N.dzb)
        for c in range(count):
            copies.start(N.wu, c)
            copies.start(N.wd, c)
            if c == 0 and not forward:
                feed(0)
                for i in every:
                    copies.start(N.n2, i)
        if not forward:
            for i in every:
                copies.start(N.middle, i)
                copies.start(N.g, i)
                copies.start(N.att, i)
            copies.start(N.wo)
        if forward:
            copies.wait(N.wo)
            for i, at in enumerate(spans):
                copies.wait(N.att, i)
                copies.wait(N.x, i)
                middle = r[N.x_v][at].astype(F32) + (dot(r[N.att_v][at], r[N.wo_v][...], NN) + r[N.bo][row, :])
                unit, _ = normalise(middle)
                r[N.n2_v][at] = (unit * r[N.g2][row, :] + r[N.b2][row, :]).astype(BF)
                r[N.middle_v][at] = middle
                r[N.next_v][at] = middle + r[N.bd][row, :]
                if not backward:
                    copies.start(N.middle_o, i)
                    copies.start(N.n2_o, i)
        if backward:
            r[N.dn_v][...] = jnp.zeros(r[N.dn_v].shape, F32)
            r[N.sums][...] = jnp.zeros(r[N.sums].shape, F32)
            copies.wait(N.dza)
            if half < t:
                copies.wait(N.dzb)
            r[N.sums][0:1, :] = column_sum(r[N.dz_v][...].astype(F32))
            if not forward:
                for i in every:
                    copies.wait(N.n2, i)

    @per_chunk
    def _(c):
        if sums is not None:
            sums.advance(parts, c)
        copies.wait(N.wu, c)
        copies.wait(N.wd, c)
        if not forward:
            if c + 1 < count:
                feed(c + 1)
            for i in every:
                for name in (N.act, N.slope):
                    copies.wait(name, c, i)
        elif not backward and c >= 2:
            for i in every:
                for name in (N.act, N.slope):
                    copies.wait(name, c - 2, i)

    wu, wd = r[N.wu_v].at[j], r[N.wd_v].at[j]
    slot = lax.rem(j, 2)

    def lead(at):
        return (
            dot(r[N.n2_v][at], wu[...], NN) if forward else None,
            dot(r[N.dz_v][at], wd[...], NT) if backward else None,
        )

    ff_sum = 0.0
    ahead = lead(spans[0])
    for i, at in enumerate(spans):
        hidden, da = ahead
        if i + 1 < len(spans):
            ahead = lead(spans[i + 1])
        if forward:
            act, slope = gelu_pair(hidden + r[N.bu][row, :])
            act = act.astype(BF)
            r[N.act_v][slot, at] = act
            if not backward:
                r[N.slope_v][slot, at] = slope.astype(BF)
        else:
            slope = r[N.slope_v][slot, at].astype(F32)
        if backward:
            dh = (da * slope).astype(BF)
            r[N.dh_v][at] = dh
            ff_sum = ff_sum + column_sum(dh.astype(F32))
        if forward:
            r[N.next_v][at] += dot(act, wd[...], NN)
        if backward:
            r[N.dn_v][at] += dot(dh, wu[...], NT)

    if forward:

        @per_chunk
        def _(c):
            for i in every:
                if not backward:
                    copies.start(N.act, c, i)
                    copies.start(N.slope, c, i)
                if c == count - 1:
                    if backward and spans[i].start >= r[N.next].shape[0]:
                        low = slice(spans[i].start - r[N.next].shape[0], spans[i].stop - r[N.next].shape[0])
                        r[N.dz_low][low] = r[N.next_v][spans[i]].astype(BF)
                    copies.start(N.next, i)

    if backward:
        r[N.sums_ff][0:1, :] = ff_sum
        deliver(grad_dot(r[N.act_v][slot], r[N.dz_v][...]), chunks[1], r[N.wd_both])
        deliver(grad_dot(r[N.n2_v][...], r[N.dh_v][...]), chunks[0], r[N.wu_both])

    @pl.when(final)
    def _():
        if sums is not None:
            for stage in range(count, sums.stages):
                sums.advance(parts, stage)
        if backward:
            if not forward:
                copies.wait(N.wo)
            for i, at in enumerate(spans):
                if not forward:
                    copies.wait(N.middle, i)
                    copies.wait(N.g, i)
                    copies.wait(N.att, i)
                g = r[N.dz_v][at].astype(F32) if forward else r[N.dm_v][at]
                unit, inverse = normalise(r[N.middle_v][at])
                up = r[N.dn_v][at]
                r[N.sums][1:2, :] += column_sum(up * unit)
                r[N.sums][2:3, :] += column_sum(up)
                dm = g + norm_back(up, r[N.g2][row, :], unit, inverse)
                r[N.dm_v][at] = dm
                copies.start(N.dm, i)
                dy = dm.astype(BF)
                r[N.dh_v][at] = dy
                r[N.sums][3:4, :] += column_sum(dy.astype(F32))
                r[N.da_v][at] = dot(dy, r[N.wo_v][...], NT).astype(BF)
                copies.start(N.da, i)
            deliver(grad_dot(r[N.att_v][...], r[N.dh_v][...]), chunks[0], r[N.wo_both])
        for i in every:
            if forward:
                copies.wait(N.next, i)
                if not backward:
                    copies.wait(N.middle_o, i)
                    copies.wait(N.n2_o, i)
                    for c in range(max(0, count - 2), count):
                        copies.wait(N.act, c, i)
                        copies.wait(N.slope, c, i)
            if backward:
                copies.wait(N.dm, i)
                copies.wait(N.da, i)
        if sums is not None:
            sums.advance(parts, sums.stages)


def ffn_call(layer, devices, arrays, weights, forward, backward, sums=None, collective_id=0):
    t, d = arrays[N.att].shape
    ff = weights[N.wu].shape[2]
    cut, count = d, ff // d
    block = min(BLOCK, t)
    once = pl.Buffered(1)
    ins, outs, scratch = Names(), Names(), Names()
    hbm = pl.BlockSpec(memory_space=pl.ANY)

    def whole(shape):
        return pl.BlockSpec(shape, lambda j: (0,) * len(shape), pipeline_mode=once)

    vec = pl.BlockSpec(memory_space=pltpu.VMEM)
    for name in (N.att, N.wo, N.wu, N.wd):
        ins.add(name, hbm)
    ins.add(N.g2, vec)
    scratch.add(N.att_v, pltpu.VMEM((t, d), BF))
    scratch.add(N.wo_v, pltpu.VMEM((d, d), BF))
    scratch.add(N.wu_v, pltpu.VMEM((count, d, cut), BF))
    scratch.add(N.wd_v, pltpu.VMEM((count, cut, d), BF))
    scratch.add(N.middle_v, pltpu.VMEM((t, d), F32))
    scratch.add(N.n2_v, pltpu.VMEM((t, d), BF))
    scratch.add(N.act_v, pltpu.VMEM((2, t, cut), BF))
    if not (forward and backward):
        scratch.add(N.slope_v, pltpu.VMEM((2, t, cut), BF))
    if forward:
        ins.add(N.x, hbm)
        for name in (N.bo, N.b2, N.bd):
            ins.add(name, vec)
        ins.add(N.bu, pl.BlockSpec((weights[N.bu].shape[0], cut), lambda j: (0, j)))
        outs.add(N.next, hbm, ((t // 2 if backward else t, d), F32))
        if backward:
            outs.add(N.next_low, hbm, ((t // 2, d), BF))
            scratch.add(N.dz_low, pltpu.VMEM((t // 2, d), BF))
        scratch.add(N.x_v, pltpu.VMEM((t, d), arrays[N.x].dtype))
        scratch.add(N.next_v, pltpu.VMEM((t, d), F32))
    if backward:
        for name in (N.dza, N.dzb) if N.dzb in arrays else (N.dza,):
            ins.add(name, hbm)
        if not forward:
            for name in (N.g, N.middle, N.n2, N.act, N.slope):
                ins.add(name, hbm)
        outs.add(N.dm, hbm, ((t, d), F32))
        outs.add(N.da, hbm, ((t, d), BF))
        outs.add(N.sums, whole((8, d)), ((8, d), F32))
        outs.add(N.sums_ff, pl.BlockSpec((8, cut), lambda j: (0, j)), ((8, ff), F32))
        outs.add(N.wo_both, whole((2, d // 2, d)), ((2, d // 2, d), BF))
        outs.add(N.wu_both, pl.BlockSpec((2, d // 2, cut), lambda j: (0, 0, j)), ((2, d // 2, ff), BF))
        outs.add(N.wd_both, pl.BlockSpec((2, cut // 2, d), lambda j: (0, j, 0)), ((2, ff // 2, d), BF))
        scratch.add(N.dz_v, pltpu.VMEM((t, d), BF))
        scratch.add(N.dn_v, pltpu.VMEM((t, d), F32))
        scratch.add(N.dh_v, pltpu.VMEM((t, d), BF))
        scratch.add(N.dm_v, pltpu.VMEM((t, d), F32))
        scratch.add(N.da_v, pltpu.VMEM((t, d), BF))
    else:
        outs.add(N.middle, hbm, ((t, d), F32))
        outs.add(N.n2, hbm, ((t, d), BF))
        outs.add(N.act, hbm, ((t, ff), BF))
        outs.add(N.slope, hbm, ((t, ff), BF))
    scratch.add(N.sems, pltpu.SemaphoreType.DMA((3 + 2 * count + (t // block) * (6 + 2 * count),)))
    everything = {**weights, **arrays}
    if sums is not None:
        for i, (array, spec) in enumerate(zip(sums.inputs(), sums.in_specs())):
            ins.add(tag(N.sum_i, i), spec)
            everything[tag(N.sum_i, i)] = array
        for i, (shape, spec) in enumerate(zip(sums.out_shapes(), sums.out_specs())):
            outs.add(tag(N.sum_o, i), spec, (shape.shape, shape.dtype))
        for i, shape in enumerate(sums.scratch()):
            scratch.add(tag(N.sum_s, i), shape)
    if sums is None:
        compiler_params = params(62)
    else:
        compiler_params = pltpu.CompilerParams(
            vmem_limit_bytes=62 << 20, collective_id=collective_id, has_side_effects=True
        )

    def kernel(*refs, names):
        ffn_kernel(
            layer,
            *refs,
            names=[N.layer] + names,
            forward=forward,
            backward=backward,
            block=block,
            chunks=(d // devices, ff // devices),
            sums=sums,
        )

    found = pl.pallas_call(
        functools.partial(kernel, names=ins.names + outs.names + scratch.names),
        grid=(count,),
        in_specs=ins.specs,
        out_specs=outs.specs,
        out_shape=[jax.ShapeDtypeStruct(*shape) for shape in outs.shapes],
        scratch_shapes=scratch.specs,
        compiler_params=compiler_params,
        cost_estimate=cost((10e9 if forward else 0) + (18e9 if backward else 0)),
        name=N.feed_forward + (N._both if forward and backward else N._back if backward else ""),
    )(*[everything[name] for name in ins.names])
    return dict(zip(outs.names, found))


N_VECTORS = 12


def joined_back_kernel(*refs, names, layer, rows, block, sums):
    r = dict(zip(names, refs))
    last = sums is not None
    t, d = r[N.x_v].shape
    spans = [slice(i, i + block) for i in range(0, t, block)]
    half = len(spans) // 2
    order = list(range(half, len(spans))) + list(range(half)) if last else list(range(len(spans)))
    copies = Copies(r[N.sems])
    copies.add((N.weight,), r[N.weight].at[layer], r[N.weight_v])
    for i, at in enumerate(spans):
        for name in (N.dq, N.x, N.dm, N.normed):
            copies.add((name, i), r[name].at[at], r[name + N._v].at[at])
        copies.add((N.dkv, i), r[N.dkv].at[:, at], r[N.dkv_v].at[:, at])
        copies.add((N.dkvi, i), r[N.dkvi].at[:, :, at], r[N.dkvi_v].at[:, :, at])
        if not last or i < half:
            copies.add((N.g, i), r[N.dm_v].at[at], r[N.g].at[at])
        if not last:
            copies.add((N.low, i), r[N.low_v].at[at], r[N.low].at[at])
    for i in order:
        for name in (N.dq, N.dkv, N.dkvi):
            copies.start(name, i)
        if not last:
            if i == order[0]:
                copies.start(N.weight)
            for name in (N.x, N.dm):
                copies.start(name, i)
    if last:
        for i in order:
            copies.start(N.normed, i)
        copies.start(N.weight)
        for i in order:
            for name in (N.x, N.dm):
                copies.start(name, i)
        place = Place(sums.count)
        parts = sums.parts(
            place, [], [ref for name, ref in r.items() if name.startswith(N.sum_o)], [ref for name, ref in r.items() if name.startswith(N.sum_s)]
        )
        trade = Trade(place, r[N.low_v].at[t // 2 :], r[N.got], r[N.trade_sems])
    else:
        for i in order:
            copies.start(N.normed, i)
    totals = [0.0] * 4

    def gather(i):
        at = spans[i]
        for name in (N.dq, N.dkv, N.dkvi):
            copies.wait(name, i)
        r[N.df_v][at, :d] = r[N.dq_v][at]
        for k in range(2):
            got = jnp.concatenate([r[N.dkvi_v][h, k, at] for h in range(d // 128)], axis=1)
            cols = slice((k + 1) * d, (k + 2) * d)
            r[N.df_v][at, cols] = (r[N.dkv_v][k, at].astype(F32) + got.astype(F32)).astype(BF)

    def back(i):
        at = spans[i]
        up = dot(r[N.df_v][at], r[N.weight_v][...], NT)
        copies.wait(N.x, i)
        copies.wait(N.dm, i)
        unit, inverse = normalise(r[N.x_v][at].astype(F32))
        found = (up * unit, up, r[N.df_v][at, :d].astype(F32), r[N.df_v][at, 2 * d :].astype(F32))
        for k in range(4):
            totals[k] = totals[k] + column_sum(found[k])
        g = r[N.dm_v][at] + norm_back(up, r[N.gain][layer : layer + 1, :], unit, inverse)
        r[N.dm_v][at] = g
        r[N.low_v][at] = g.astype(BF)
        if not last or i < half:
            copies.start(N.g, i)
        if not last:
            copies.start(N.low, i)

    def product(k):
        return grad_dot(r[N.normed_v][...], r[N.df_v][:, k * d : (k + 1) * d])

    if not last:
        copies.wait(N.weight)
        for i in order:
            gather(i)
            back(i)
        for i in order:
            copies.wait(N.normed, i)
        for k, total in enumerate(totals):
            r[N.sums][k : k + 1, :] = total
        for k in range(3):
            deliver(product(k), rows, r[N.both].at[:, :, k * d : (k + 1) * d])
    else:
        vectors = r[N.vectors]

        def swap(stage):
            return pltpu.make_async_remote_copy(
                src_ref=r[N.vectors_s].at[stage],
                dst_ref=r[N.vectors_v].at[stage],
                send_sem=r[N.vector_sems].at[0, stage],
                recv_sem=r[N.vector_sems].at[1, stage],
                device_id=place.partner(path[stage]),
                device_id_type=pl.DeviceIdType.MESH,
            )

        path = [0] + list(range(2, sums.stages)) + [1]

        def send_vectors(stage):
            if stage > 0:
                swap(stage - 1).wait()
                vectors[...] += r[N.vectors_v][stage - 1]
            if stage < sums.stages:
                r[N.vectors_s][stage] = vectors[...]
                swap(stage).start()

        for i in order:
            gather(i)
        for i in order:
            copies.wait(N.normed, i)
        each = len(parts) // 3
        for k in range(3):
            made = product(k)
            for n in range(each):
                parts[each * k + n].fill(made[:, n * (d // each) : (n + 1) * (d // each)], rows)
                if k == n == 0:
                    place.greet()
                parts[each * k + n].begin(0)
        copies.wait(N.weight)
        for i in order[:half]:
            back(i)
        trade.copy().start()
        sums.advance(parts, 1)
        for i in order[half:]:
            back(i)
        for k, total in enumerate(totals):
            vectors[k : k + 1, :] = total
        for l in range(2):
            base = N_VECTORS * l
            if l > 0:
                vectors[base : base + 4, :] = r[N.sums_in][0:4, :]
            vectors[base + 4 : base + 8, :] = r[tag(N.sums, l)][0:4, :]
            for k in range(4):
                vectors[base + 8 + k : base + 9 + k, :] = r[tag(N.sums_ff, l)][0:1, k * d : (k + 1) * d]
        send_vectors(0)
        for stage in range(1, sums.stages + 1):
            if stage > 1:
                sums.advance(parts, stage)
            send_vectors(stage)
        trade.copy().wait()
    for i in order:
        if not last or i < half:
            copies.wait(N.g, i)
        if not last:
            copies.wait(N.low, i)


def joined_back_call(arrays, layer, devices, sums=None, collective_id=0):
    t, d = arrays[N.x].shape
    last = sums is not None
    block = min(BLOCK, t // 2)
    ins, outs, scratch = Names(), Names(), Names()
    hbm = pl.BlockSpec(memory_space=pl.ANY)
    vmem = pl.BlockSpec(memory_space=pltpu.VMEM)
    for name in (N.dq, N.dkv, N.dkvi, N.x, N.dm, N.normed, N.weight):
        ins.add(name, hbm)
        shape = arrays[name].shape
        scratch.add(name + N._v, pltpu.VMEM(shape[1:] if name == N.weight else shape, arrays[name].dtype))
    ins.add(N.gain, vmem)
    scratch.add(N.df_v, pltpu.VMEM((t, 3 * d), BF))
    scratch.add(N.low_v, pltpu.VMEM((t, d), BF))
    outs.add(N.g, hbm, ((t // 2 if last else t, d), F32))
    if last:
        for name in (N.sums_in, *(tag(x, l) for x in (N.sums, N.sums_ff) for l in range(2))):
            ins.add(name, vmem)
        outs.add(N.got, hbm, ((t // 2, d), BF))
        outs.add(N.vectors, vmem, ((2 * N_VECTORS, d), F32))
        for i, (shape, spec) in enumerate(zip(sums.out_shapes(), sums.out_specs())):
            outs.add(tag(N.sum_o, i), vmem, (shape.shape, shape.dtype))
        for i, shape in enumerate(sums.scratch()):
            scratch.add(tag(N.sum_s, i), shape)
        for name in (N.vectors_s, N.vectors_v):
            scratch.add(name, pltpu.VMEM((sums.stages, 2 * N_VECTORS, d), F32))
        scratch.add(N.vector_sems, pltpu.SemaphoreType.DMA((2, sums.stages)))
        scratch.add(N.trade_sems, pltpu.SemaphoreType.DMA((2,)))
        compiler_params = pltpu.CompilerParams(
            vmem_limit_bytes=62 << 20, collective_id=collective_id, has_side_effects=True
        )
    else:
        outs.add(N.low, hbm, ((t, d), BF))
        outs.add(N.sums, vmem, ((8, d), F32))
        outs.add(N.both, vmem, ((2, d // 2, 3 * d), BF))
        compiler_params = params(62)
    scratch.add(N.sems, pltpu.SemaphoreType.DMA((1 + (t // block) * 8,)))
    found = pl.pallas_call(
        functools.partial(
            joined_back_kernel,
            names=ins.names + outs.names + scratch.names,
            layer=layer,
            rows=d // devices,
            block=block,
            sums=sums,
        ),
        grid=(1,),
        in_specs=ins.specs,
        out_specs=outs.specs,
        out_shape=[jax.ShapeDtypeStruct(*shape) for shape in outs.shapes],
        scratch_shapes=scratch.specs,
        compiler_params=compiler_params,
        cost_estimate=cost(18e9 if last else 8e9),
        name=N.joined_back + (N._sums if last else ""),
    )(*[arrays[name] for name in ins.names])
    return dict(zip(outs.names, found))


def finish_kernel(*refs, names, devices):
    r = dict(zip(names, refs))
    place = Place(devices)
    chip, index = place.bit(1), place.dp * 4 + place.seq
    copies, moves = Copies(r[N.sems]), []
    for cells in (N.block, N.input):
        moves.append((cells + N._got, None, None))
        moves.append((cells + N._own, cells + N._out, chip))
    for m in range(4):
        for l in range(2):
            moves.append((tag(N.m, m, l), tag(N.mat, m), l))
    for name, out, at in moves:
        copies.add((name, 0), r[name], r[name + N._v])
        if out is not None:
            copies.add((name, 1), r[name + N._v], r[out].at[at])
    for cells in (N.block, N.input):
        copies.add((cells,), r[cells + N._wide], r[cells + N._out].at[1 - chip])
    for name, _, _ in moves:
        copies.start(name, 0)
    for name, out, _ in moves:
        copies.wait(name, 0)
        if out is not None:
            copies.start(name, 1)
        else:
            cells = N.block if name == N.block_got else N.input
            r[cells + N._wide][...] = r[name + N._v][...].astype(F32)
            copies.start(cells)
    v = r[N.vectors]
    d = v.shape[1]
    piece = d // devices

    def cut(x, start, width):
        return pltpu.roll(x, lax.rem(d - start, d), 1)[:, :width]

    for l in range(2):
        mine = v[N_VECTORS * l : N_VECTORS * l + 8, :]
        ff = v[N_VECTORS * l + 8 : N_VECTORS * l + 12, :]
        rows = cut(mine, index * piece, piece)
        for name, k in ((N.v0, 0), (N.v1, 1), (N.v4, 7), (N.v5, 5), (N.v6, 6), (N.v8, 4)):
            r[name][l : l + 1, :] = rows[k : k + 1]
        per = devices // 2
        qv = cut(mine, lax.rem(index, per) * (2 * piece), 2 * piece)
        r[N.qv][l : l + 1, :] = jnp.where(index < per, qv[2:3], qv[3:4])
        per = devices // 4
        up = cut(ff, lax.rem(index, per) * (4 * piece), 4 * piece)
        at = index // per
        r[N.up][l : l + 1, :] = jnp.where(
            at < 2, jnp.where(at == 0, up[0:1], up[1:2]), jnp.where(at == 2, up[2:3], up[3:4])
        )
    for name, out, _ in moves:
        if out is not None:
            copies.wait(name, 1)
    copies.wait(N.block)
    copies.wait(N.input)


def finish_call(arrays, devices, genes, ff):
    d = arrays[N.vectors].shape[1]
    piece = d // devices
    ins, outs, scratch = Names(), Names(), Names()
    hbm = pl.BlockSpec(memory_space=pl.ANY)
    vmem = pl.BlockSpec(memory_space=pltpu.VMEM)
    for name, array in arrays.items():
        ins.add(name, vmem if name == N.vectors else hbm)
        if name != N.vectors:
            scratch.add(name + N._v, pltpu.VMEM(array.shape, array.dtype))
    for cells in (N.block, N.input):
        outs.add(cells + N._out, hbm, ((2, genes, d), F32))
        scratch.add(cells + N._wide, pltpu.VMEM((genes, d), F32))
    for m in range(4):
        outs.add(tag(N.mat, m), hbm, ((2,) + arrays[tag(N.m, m, 0)].shape, F32))
    for name in (N.v0, N.v1, N.v4, N.v5, N.v6, N.v8):
        outs.add(name, vmem, ((2, piece), F32))
    outs.add(N.qv, vmem, ((2, 2 * piece), F32))
    outs.add(N.up, vmem, ((2, ff // devices), F32))
    scratch.add(N.sems, pltpu.SemaphoreType.DMA((24,)))
    found = pl.pallas_call(
        functools.partial(finish_kernel, names=ins.names + outs.names + scratch.names, devices=devices),
        grid=(1,),
        in_specs=ins.specs,
        out_specs=outs.specs,
        out_shape=[jax.ShapeDtypeStruct(*shape) for shape in outs.shapes],
        scratch_shapes=scratch.specs,
        compiler_params=params(62),
        cost_estimate=cost(2e9),
        name=N.finish,
    )(*[arrays[name] for name in ins.names])
    return dict(zip(outs.names, found))


def on_device(
    device_count,
    cell_tokens,
    first_gain,
    first_bias,
    joined_weight,
    query_value_bias,
    output_weight,
    output_bias,
    second_gain,
    second_bias,
    up_weight,
    up_bias,
    down_weight,
    down_bias,
    cotangent,
    gene_mask,
):
    _, genes, d = cell_tokens.shape
    layers = joined_weight.shape[0]
    seq = lax.axis_index(N.seq)
    across = [(0, 2), (1, 3), (2, 0), (3, 1)]

    x = cell_tokens
    weights = dict(
        wo=output_weight,
        wu=up_weight,
        wd=down_weight,
        bo=output_bias,
        g2=second_gain,
        b2=second_bias,
        bu=up_bias,
        bd=down_bias,
    )
    chunks = device_count
    saved = []
    for layer in range(layers):
        top = layer == layers - 1
        seeds = (cotangent, gene_mask) if layer == 0 else ()
        joined = qkv_call(x, layer, chunks, first_gain, first_bias, joined_weight, query_value_bias, 2 * layers + 1 + layer, seeds)
        if seeds:
            g = joined[N.seed_own], lax.ppermute(joined[N.seed_send], N.seq, across)
        normed, q, kv, kvo = (joined[name] for name in (N.normed, N.q, N.kv, N.kvo))
        x = joined.get(N.held, x)
        att, lse = attend_call(q, kv, kvo)
        arrays = dict(att=att, x=x)
        if top:
            arrays.update(dza=g[0], dzb=g[1])
        found = ffn_call(layer, chunks, arrays, weights, True, top)
        saved.append((x, normed, q, kv, kvo, att, lse, found))
        x = found[N.next]

    dp_bits = list(range(2, device_count.bit_length() - 1))
    orders = (
        [1] + dp_bits,
        dp_bits[:1] + dp_bits[1:-1] + [1] + dp_bits[-1:],
        dp_bits[1:-1] + [1] + dp_bits[:1] + dp_bits[-1:],
    )

    def job(both):
        split = (2, chunks // 2, 2 * both.shape[1] // chunks, both.shape[2])
        return Job(both.reshape(split), device_count, orders)

    final = {}
    waiting, back = None, None
    for layer in reversed(range(layers)):
        x, normed, q, kv, kvo, att, lse, found = saved[layer]
        top, bottom = layer == layers - 1, layer == 0
        if not top:
            arrays = dict(att=att, g=back[N.g], dza=back[N.low], **{k: found[k] for k in (N.middle, N.n2, N.act, N.slope)})
            found = ffn_call(layer, chunks, arrays, weights, False, True, Sums([waiting], device_count), layers + layer)
            final[tag(N.m, 0, layer + 1)] = found[tag(N.sum_o, 0)]
        jobs = [job(found[w + N._both]) for w in (N.wo, N.wu, N.wd)]
        trade_out = found[N.next_low] if top else None
        dq, dkv, dkvi, *done = attend_back_call(
            q, kv, kvo, found[N.da], att, lse, Sums(jobs, device_count, trade_out, 3), layer
        )
        if top:
            final[N.block_own], final[N.block_got] = found[N.next], done.pop()
        for i in range(3):
            final[tag(N.m, i + 1, layer)] = done[i]
        final[tag(N.sums, layer)], final[tag(N.sums_ff, layer)] = found[N.sums], found[N.sums_ff]
        arrays = dict(
            dq=dq, dkv=dkv, dkvi=dkvi, x=x, dm=found[N.dm], normed=normed, weight=joined_weight, gain=first_gain
        )
        if bottom:
            arrays.update(sums_in=back[N.sums])
            for l in range(2):
                arrays.update({tag(N.sums, l): final.pop(tag(N.sums, l)), tag(N.sums_ff, l): final.pop(tag(N.sums_ff, l))})
            late = (orders[1], dp_bits[1:-1] + dp_bits[:1] + [1] + dp_bits[-1:]) * 3
            made = Job(None, device_count, late, (d // chunks, 3 * d))
            back = joined_back_call(arrays, layer, chunks, Sums([made], device_count), 2 * layers)
        else:
            back = joined_back_call(arrays, layer, chunks)
            waiting = job(back[N.both])
    final.update(
        **{tag(N.m, 0, 0): back[tag(N.sum_o, 0)]}, input_own=back[N.g], input_got=back[N.got], vectors=back[N.vectors]
    )
    out = finish_call(final, device_count, genes, up_bias.shape[1])
    return tuple(
        out[name]
        for name in (
            N.block_out,
            N.input_out,
            N.v0,
            N.v1,
            tag(N.mat, 0),
            N.qv,
            tag(N.mat, 1),
            N.v4,
            N.v5,
            N.v6,
            tag(N.mat, 2),
            N.up,
            tag(N.mat, 3),
            N.v8,
        )
    )


def solution(mesh):
    split = P(None, (N.dp, N.seq))
    split_rows = P(None, (N.dp, N.seq), None)
    tokens = P(N.dp, N.seq, None)
    return jax.shard_map(
        functools.partial(on_device, mesh.size),
        mesh=mesh,
        in_specs=(tokens,) + (P(),) * 12 + (tokens, P(N.dp, N.seq)),
        out_specs=(
            tokens,
            tokens,
            split,
            split,
            split_rows,
            split,
            split_rows,
            split,
            split,
            split,
            split_rows,
            split,
            split_rows,
            split,
        ),
        check_vma=False,
    )
```

```python
import functools

import jax
import jax.numpy as jnp
from jax import lax
from jax.experimental import pallas as pl
from jax.experimental.pallas import tpu as pltpu
from jax.sharding import PartitionSpec as P

HEAD = 64
LOG2E = 1.4426950408889634
BF = jnp.bfloat16
F32 = jnp.float32
NN = ((1,), (0,))
NT = ((1,), (1,))
SAFE = 60
BLOCK = 256
SLOTS = (0, 2, 6, 8, 10)


class _Names:
    def __getattr__(self, word):
        return word


N = _Names()


def tag(word, *numbers):
    return N._.join([word, *map(str, numbers)])


def dot(a, b, dims):
    return lax.dot_general(a, b, (dims, ((), ())), preferred_element_type=F32)


def params(mib):
    return pltpu.CompilerParams(vmem_limit_bytes=mib << 20)


def cost(products, nbytes=0):
    return pl.CostEstimate(flops=int(2 * products), bytes_accessed=int(nbytes), transcendentals=0)


def normalise(x):
    n = x.shape[-1]
    centred = x - jnp.sum(x, axis=-1, keepdims=True) * (1.0 / n)
    inverse = lax.rsqrt(jnp.sum(centred * centred, axis=-1, keepdims=True) * (1.0 / n) + 1e-05)
    return centred * inverse, inverse


def norm_back(upstream, gain, unit, inverse):
    n = unit.shape[-1]
    e = upstream * gain
    mean_e = jnp.sum(e, axis=-1, keepdims=True) * (1.0 / n)
    mean_eu = jnp.sum(e * unit, axis=-1, keepdims=True) * (1.0 / n)
    return inverse * (e - mean_e - unit * mean_eu)


def column_sum(x):
    return jnp.sum(x, axis=0, keepdims=True)


def gelu_pair(x):
    cdf = 0.5 + 0.5 * lax.erf(x * 0.7071067811865476)
    slope = jnp.exp2(x * x * (-0.5 * LOG2E)) * 0.3989422804014327
    return x * cdf, cdf + x * slope


def kernel_call(kernel, ins, in_specs, after=(), **kwargs):
    n = len(ins)
    extra = [pl.BlockSpec(memory_space=pl.ANY)] * len(after)

    def body(*refs):
        kernel(*refs[:n], *refs[n + len(after) :])

    return pl.pallas_call(body, in_specs=list(in_specs) + extra, **kwargs)(*ins, *after)


def qkv_kernel(*refs, names, layer, block, count, trading):
    r = dict(zip(names, refs))
    t, d = r[N.x_v].shape
    spans = [slice(i, i + block) for i in range(0, t, block)]
    half = len(spans) // 2
    place = Place(count)
    row = slice(layer, layer + 1)
    copies = Copies(r[N.sems])
    for k in range(3):
        cols = slice(k * d, (k + 1) * d)
        copies.add((N.weight, k), r[N.weight].at[layer, :, cols], r[N.weight_v].at[k])
    chip = place.bit(1)
    for i, at in enumerate(spans):
        if not trading:
            copies.add((N.x, i), r[N.x].at[at], r[N.x_v].at[at])
        elif i < half:
            copies.add((N.x, i), r[N.x].at[chip, at], r[N.x_v].at[at])
        if trading:
            copies.add((N.held, i), r[N.x_v].at[at], r[N.held].at[at])
        copies.add((N.normed, i), r[N.normed_v].at[at], r[N.normed].at[at])
        copies.add((N.q, i), r[N.q_v].at[at], r[N.q].at[at])
        copies.add((N.kv, i), r[N.kv_v].at[:, at], r[N.kv].at[:, at])

    def remote(src, dst, i, bit):
        return pltpu.make_async_remote_copy(
            src_ref=src,
            dst_ref=dst,
            send_sem=r[N.far_sems].at[0, i],
            recv_sem=r[N.far_sems].at[1, i],
            device_id=place.partner(bit),
            device_id_type=pl.DeviceIdType.MESH,
        )

    if trading:
        for i, cell in enumerate((chip, 1 - chip)):
            copies.add((N.seed, i), r[N.cotangent].at[cell], r[N.seed_v].at[i])
            copies.add((N.seeded, i), r[N.seed_v].at[i], r[N.seed_own if i == 0 else N.seed_send])

    def parcel(i):
        return remote(r[N.kv_v].at[:, spans[i]], r[N.kvo].at[:, spans[i]], i, 0)

    def trade(i):
        there = spans[half + i]
        return remote(r[N.x].at[1 - chip, spans[i]], r[N.x_v].at[there], len(spans) + i, 1)

    for i in range(half if trading else len(spans)):
        copies.start(N.x, i)
        if i == 0:
            for k in (1, 2, 0):
                copies.start(N.weight, k)
    place.greet(2)
    if trading:
        for i in range(half):
            trade(i).start()
        for i in range(2):
            copies.start(N.seed, i)
    waited = set()

    def weight(k):
        if k not in waited:
            copies.wait(N.weight, k)
            waited.add(k)
        return r[N.weight_v][k]

    for group in (range(half), range(half, len(spans))):
        if trading and group.start:
            masks = jnp.broadcast_to(r[N.mask][...].astype(F32)[:, None, :], (2, 8, t // 2))
            for i in range(2):
                mask = jnp.where(chip == i, masks[0], masks[1])
                copies.wait(N.seed, i)
                r[N.seed_v][i] = r[N.seed_v][i] * mask.T[:, :1].astype(BF)
                copies.start(N.seeded, i)
        for i in group:
            at = spans[i]
            if not trading or i < half:
                copies.wait(N.x, i)
            else:
                trade(i - half).wait()
            if trading:
                copies.start(N.held, i)
            unit, _ = normalise(r[N.x_v][at].astype(F32))
            normed = (unit * r[N.gain][row, :] + r[N.bias][row, :]).astype(BF)
            r[N.normed_v][at] = normed
            copies.start(N.normed, i)
            r[N.kv_v][0, at] = dot(normed, weight(1), NN).astype(BF)
            r[N.kv_v][1, at] = (dot(normed, weight(2), NN) + r[N.qv_bias][row, d:]).astype(BF)
            parcel(i).start()
            copies.start(N.kv, i)
        if trading or group.start:
            for i in group if trading else range(len(spans)):
                at = spans[i]
                r[N.q_v][at] = (dot(r[N.normed_v][at], weight(0), NN) + r[N.qv_bias][row, :d]).astype(BF)
                copies.start(N.q, i)
    if trading:
        for i in range(2):
            copies.wait(N.seeded, i)
    for i in range(len(spans)):
        for name in (N.held, N.normed, N.q, N.kv) if trading else (N.normed, N.q, N.kv):
            copies.wait(name, i)
        parcel(i).wait()


def qkv_call(x, layer, devices, gain, bias, weight, qv_bias, collective_id, seeds=()):
    trading = x.ndim == 3
    d = x.shape[-1]
    t = x.size // d
    block = min(BLOCK, t // 2)
    blocks = t // block
    ins, outs, scratch = Names(), Names(), Names()
    hbm = pl.BlockSpec(memory_space=pl.ANY)
    ins.add(N.x, hbm)
    ins.add(N.weight, hbm)
    for name in (N.gain, N.bias, N.qv_bias):
        ins.add(name, pl.BlockSpec(memory_space=pltpu.VMEM))
    if trading:
        ins.add(N.cotangent, hbm)
        ins.add(N.mask, pl.BlockSpec(memory_space=pltpu.VMEM))
        outs.add(N.held, hbm, ((t, d), x.dtype))
        for name in (N.seed_own, N.seed_send):
            outs.add(name, hbm, ((t // 2, d), BF))
        scratch.add(N.seed_v, pltpu.VMEM((2, t // 2, d), BF))
    outs.add(N.normed, hbm, ((t, d), BF))
    outs.add(N.q, hbm, ((t, d), BF))
    outs.add(N.kv, hbm, ((2, t, d), BF))
    outs.add(N.kvo, hbm, ((2, t, d), BF))
    scratch.add(N.x_v, pltpu.VMEM((t, d), x.dtype))
    scratch.add(N.normed_v, pltpu.VMEM((t, d), BF))
    scratch.add(N.q_v, pltpu.VMEM((t, d), BF))
    scratch.add(N.kv_v, pltpu.VMEM((2, t, d), BF))
    scratch.add(N.weight_v, pltpu.VMEM((3, d, d), BF))
    scratch.add(N.sems, pltpu.SemaphoreType.DMA((7 + 5 * blocks,)))
    scratch.add(N.far_sems, pltpu.SemaphoreType.DMA((2, 2 * blocks)))
    found = pl.pallas_call(
        functools.partial(
            qkv_kernel,
            names=ins.names + outs.names + scratch.names,
            layer=layer,
            block=block,
            count=devices,
            trading=trading,
        ),
        grid=(1,),
        in_specs=ins.specs,
        out_specs=outs.specs,
        out_shape=[jax.ShapeDtypeStruct(*shape) for shape in outs.shapes],
        scratch_shapes=scratch.specs,
        compiler_params=pltpu.CompilerParams(
            vmem_limit_bytes=62 << 20, collective_id=collective_id, has_side_effects=True
        ),
        cost_estimate=cost(12e9 if trading else 5e9),
        name=N.norm_qkv,
    )(x, weight, gain, bias, qv_bias, *seeds)
    return dict(zip(outs.names, found))


def attend_kernel(q, kv, kvo, out, lse, *, chunk):
    t = q.shape[0]
    c = LOG2E * HEAD**-0.5
    lows, highs = [], []

    def run(stable):
        for head in range(2):
            ls = slice(HEAD * head, HEAD * head + HEAD)
            values = []
            for ref in (kv, kvo):
                v = ref[1, :, ls].astype(F32).T.astype(BF)
                values.append(jnp.concatenate([v, jnp.ones((16, t), BF)], axis=0))

            def score(j):
                block = q[j * chunk : (j + 1) * chunk, ls]
                return [dot(ref[0, :, ls], block, NT) for ref in (kv, kvo)]

            ahead = score(0)
            for j in range(t // chunk):
                s = ahead
                if j + 1 < t // chunk:
                    ahead = score(j + 1)
                if stable:
                    shift = c * jnp.maximum(
                        jnp.max(s[0], axis=0, keepdims=True), jnp.max(s[1], axis=0, keepdims=True)
                    )
                    p = [jnp.exp2(x * c - shift).astype(BF) for x in s]
                else:
                    shift = 0.0
                    p = [jnp.exp2(x * c).astype(BF) for x in s]
                total = dot(values[0], p[0], NN) + dot(values[1], p[1], NN)
                level = total[HEAD : HEAD + 1]
                if not stable:
                    lows.append(level)
                    highs.append(level)
                cols = slice(j * chunk, (j + 1) * chunk)
                out[cols, ls] = (total[:HEAD] / level).T.astype(BF)
                lse[0, head : head + 1, cols] = shift + jnp.log2(level)

    run(False)
    low = jnp.min(functools.reduce(jnp.minimum, lows))
    high = jnp.max(functools.reduce(jnp.maximum, highs))
    fine = jnp.logical_and(low >= 2.0**-SAFE, high <= 2.0**SAFE)
    pl.when(jnp.logical_not(fine))(lambda: run(True))


def attend_call(q, kv, kvo):
    t, d = q.shape
    pairs = d // 128
    both = pl.BlockSpec((2, t, 128), lambda h: (0, 0, h))
    one = pl.BlockSpec((t, 128), lambda h: (0, h))
    return pl.pallas_call(
        functools.partial(attend_kernel, chunk=min(256, t)),
        grid=(pairs,),
        in_specs=[one, both, both],
        out_specs=[one, pl.BlockSpec((1, 8, t), lambda h: (h, 0, 0))],
        out_shape=[jax.ShapeDtypeStruct((t, d), BF), jax.ShapeDtypeStruct((pairs, 8, t), F32)],
        compiler_params=params(62),
        cost_estimate=cost(16e9),
        name=N.attend,
    )(q, kv, kvo)


class Place:
    def __init__(self, count):
        self.count = count
        self.bits = count.bit_length() - 1
        self.dp, self.seq = lax.axis_index(N.dp), lax.axis_index(N.seq)

    def bit(self, b):
        return (self.seq // (1 << b)) % 2 if b < 2 else (self.dp // (1 << (b - 2))) % 2

    def partner(self, b):
        step = 1 - 2 * self.bit(b)
        if b < 2:
            return {N.dp: self.dp, N.seq: self.seq + step * (1 << b)}
        return {N.dp: self.dp + step * (1 << (b - 2)), N.seq: self.seq}

    def greet(self, bits=None):
        bits = self.bits if bits is None else bits
        barrier = pltpu.get_barrier_semaphore()
        for b in range(bits):
            pl.semaphore_signal(barrier, inc=1, device_id=self.partner(b), device_id_type=pl.DeviceIdType.MESH)
        pl.semaphore_wait(barrier, bits)


class Job:
    def __init__(self, both, count, orders, shape=None):
        self.lead = count.bit_length() - 2
        self.made = both is None
        if not self.made:
            self.both = both.reshape((2,) * (self.lead + 1) + both.shape[2:])
        self.rows, self.cols = shape or both.shape[2:]
        self.orders = orders
        self.wide = self.cols // len(orders)
        self.dtype = BF

    def scratch(self):
        out = []
        for _ in self.orders:
            block = (self.rows, self.wide)
            out.append(pltpu.VMEM((2,) * (self.lead + self.made) + block, self.dtype))
            for left in range(self.lead, -1, -1):
                out.append(pltpu.VMEM((2,) * left + block, self.dtype))
        return out

    def out_shape(self):
        return jax.ShapeDtypeStruct((self.rows, self.cols), F32)


class Part:
    def __init__(self, place, job, at, both, out, scratch, sems, first_sem):
        self.place, self.job, self.both, self.out = place, job, both, out
        self.order = job.orders[at]
        self.cols = slice(at * job.wide, (at + 1) * job.wide)
        self.total, self.got = scratch[0], scratch[1:]
        self.sems, self.first = sems, first_sem
        self.every = (slice(None),) * (job.lead + 1)
        self.pre = (place.bit(0),) if job.made else ()

    def fill(self, out, rows):
        lead = self.job.lead
        for at in range(2 << lead):
            index = (at % 2,) + tuple((at >> (b + 1)) & 1 for b in reversed(range(lead)))
            self.total[index] = out[at * rows : (at + 1) * rows].astype(BF)

    def own(self):
        return pltpu.make_async_copy(
            self.both.at[(self.place.bit(0),) + self.every + (self.cols,)], self.total, self.sems.at[0, self.first]
        )

    def index(self, stage, away):
        out = []
        for b in range(self.job.lead, 0, -1):
            at = self.order.index(b) + 1
            if at < stage or (at == stage and not away):
                out.append(self.place.bit(b))
            elif at == stage:
                out.append(1 - self.place.bit(b))
            else:
                out.append(slice(None))
        return tuple(out)

    def copy(self, stage):
        if stage == 0 and self.job.made:
            bit, src = 0, self.total.at[1 - self.place.bit(0)]
        elif stage == 0:
            bit, src = 0, self.both.at[(1 - self.place.bit(0),) + self.every + (self.cols,)]
        else:
            bit, src = self.order[stage - 1], self.total.at[self.pre + self.index(stage, True)]
        return pltpu.make_async_remote_copy(
            src_ref=src,
            dst_ref=self.got[stage],
            send_sem=self.sems.at[1, self.first + stage],
            recv_sem=self.sems.at[2, self.first + stage],
            device_id=self.place.partner(bit),
            device_id_type=pl.DeviceIdType.MESH,
        )

    def begin(self, stage):
        if stage == 0 and not self.job.made:
            self.own().start()
        self.copy(stage).start()

    def end(self, stage):
        if stage == 0 and not self.job.made:
            self.own().wait()
        self.copy(stage).wait()
        index = self.pre + self.index(stage, False)
        if stage == len(self.order):
            self.out[:, self.cols] = self.total[index].astype(F32) + self.got[stage][...].astype(F32)
        elif stage == 0:
            index = self.pre + self.every
            self.total[index] = self.total[index] + self.got[0][...]
        else:
            self.total[index] = self.total[index] + self.got[stage][...]


class Trade:
    def __init__(self, place, src, dst, sems):
        self.ends = dict(src_ref=src, dst_ref=dst, send_sem=sems.at[0], recv_sem=sems.at[1])
        self.place = place

    def copy(self):
        return pltpu.make_async_remote_copy(
            **self.ends, device_id=self.place.partner(1), device_id_type=pl.DeviceIdType.MESH
        )


class Sums:
    def __init__(self, jobs, count, trade=None, trade_at=0):
        self.jobs, self.count, self.trade, self.trade_at = jobs, count, trade, trade_at
        self.stages = count.bit_length() - 1

    def n_ins(self):
        return sum(not job.made for job in self.jobs) + (self.trade is not None)

    def n_outs(self):
        return len(self.jobs) + (self.trade is not None)

    def inputs(self):
        return [job.both for job in self.jobs if not job.made] + ([] if self.trade is None else [self.trade])

    def n_parts(self):
        return sum(len(job.orders) for job in self.jobs)

    def in_specs(self):
        return [pl.BlockSpec(memory_space=pl.ANY)] * self.n_ins()

    def out_shapes(self):
        out = [job.out_shape() for job in self.jobs]
        return out if self.trade is None else out + [jax.ShapeDtypeStruct(self.trade.shape, self.trade.dtype)]

    def out_specs(self):
        out = [pl.BlockSpec((job.rows, job.cols), lambda *_: (0, 0), pipeline_mode=pl.Buffered(1)) for job in self.jobs]
        return out if self.trade is None else out + [pl.BlockSpec(memory_space=pl.ANY)]

    def scratch(self):
        out = [x for job in self.jobs for x in job.scratch()]
        return out + [pltpu.SemaphoreType.DMA((3, self.n_parts() * self.stages)), pltpu.SemaphoreType.DMA((2,))]

    def parts(self, place, ins, outs, scratch):
        scratch = list(scratch)
        trade_sems = scratch.pop()
        sems = scratch.pop()
        found = []
        self.swap = None if self.trade is None else Trade(place, ins[-1], outs[-1], trade_sems)
        for i, job in enumerate(self.jobs):
            for at in range(len(job.orders)):
                mine, scratch = scratch[: job.lead + 2], scratch[job.lead + 2 :]
                both = None if job.made else ins[i]
                found.append(Part(place, job, at, both, outs[i], mine, sems, len(found) * self.stages))
        return found

    def advance(self, parts, stage):
        for part in parts:
            if stage > 0:
                part.end(stage - 1)
            if stage < self.stages:
                part.begin(stage)
        if self.swap is not None:
            if stage == self.trade_at:
                self.swap.copy().start()
            if stage == self.stages:
                self.swap.copy().wait()


def attend_back_kernel(*refs, chunk, sums, slots):
    n_in, n_out = 6 + sums.n_ins(), 3 + sums.n_outs()
    q, kv, kvo, up, out, lse = refs[:6]
    dq, dkv, dkvi = refs[n_in : n_in + 3]
    outbox, box_sems = refs[n_in + n_out : n_in + n_out + 2]
    place = Place(sums.count)
    parts = sums.parts(place, refs[6:n_in], refs[n_in + 3 : n_in + n_out], refs[n_in + n_out + 2 :])
    t = q.shape[0]
    scale = HEAD**-0.5
    c = LOG2E * scale
    pair, pairs = pl.program_id(0), len(slots) // 2

    def parcel(at):
        return pltpu.make_async_remote_copy(
            src_ref=outbox.at[at % 2],
            dst_ref=dkvi.at[at],
            send_sem=box_sems.at[0, at],
            recv_sem=box_sems.at[1, at],
            device_id=place.partner(0),
            device_id_type=pl.DeviceIdType.MESH,
        )

    def advance(at):
        for stage in slots[at]:
            sums.advance(parts, stage)

    pl.when(pair == 0)(place.greet)
    for at in range(2, pairs):
        pl.when(pair == at)(lambda at=at: parcel(at - 2).wait_send())
    box = outbox.at[lax.rem(pair, 2)]
    for head in range(2):
        for at in range(pairs):
            if slots[2 * at + head]:
                pl.when(pair == at)(functools.partial(advance, 2 * at + head))
        ls = slice(HEAD * head, HEAD * head + HEAD)
        qh = q[:, ls]
        uh = up[:, ls]
        q_t = qh.astype(F32).T.astype(BF)
        u_t = uh.astype(F32).T.astype(BF)
        level = lse[0].T[:, head : head + 1]
        inner = jnp.sum(uh.astype(F32) * out[:, ls].astype(F32), axis=1, keepdims=True)
        blocks = [
            (src, dst, slice(i * chunk, (i + 1) * chunk))
            for src, dst in ((kvo, box), (kv, dkv))
            for i in range(t // chunk)
        ]

        def products(block):
            src, _, rows = block
            return dot(qh, src[0, rows, ls], NT), dot(uh, src[1, rows, ls], NT)

        total = None
        ahead = products(blocks[0])
        for at, (src, dst, rows) in enumerate(blocks):
            s, dp = ahead
            if at + 1 < len(blocks):
                ahead = products(blocks[at + 1])
            p = jnp.exp2(s * c - level)
            ds = (p * (dp - inner)).astype(BF)
            dst[1, rows, ls] = dot(u_t, p.astype(BF), NN).T.astype(BF)
            dst[0, rows, ls] = (dot(q_t, ds, NN).T * scale).astype(BF)
            part = dot(ds, src[0, rows, ls], NN)
            total = part if total is None else total + part
        dq[:, ls] = (total * scale).astype(BF)

    for at in range(pairs):

        @pl.when(pair == at)
        def _(at=at):
            parcel(at).start()
            if at == pairs - 1:
                advance(2 * pairs)
                for last in range(max(0, pairs - 2), pairs):
                    parcel(last).wait_send()
                for each in range(pairs):
                    parcel(each).wait_recv()


def attend_back_call(q, kv, kvo, up, out, lse, sums, collective_id):
    t, d = q.shape
    pairs = d // 128
    both = pl.BlockSpec((2, t, 128), lambda h: (0, 0, h))
    one = pl.BlockSpec((t, 128), lambda h: (0, h))
    slots = [[] for _ in range(2 * pairs + 1)]
    for stage in range(sums.stages + 1):
        slots[SLOTS[stage] if stage < min(len(SLOTS), sums.stages) else 2 * pairs].append(stage)
    return pl.pallas_call(
        functools.partial(attend_back_kernel, chunk=min(256, t), sums=sums, slots=slots),
        grid=(pairs,),
        in_specs=[one, both, both, one, one, pl.BlockSpec((1, 8, t), lambda h: (h, 0, 0))] + sums.in_specs(),
        out_specs=[one, both, pl.BlockSpec(memory_space=pl.ANY)] + sums.out_specs(),
        out_shape=[
            jax.ShapeDtypeStruct((t, d), BF),
            jax.ShapeDtypeStruct((2, t, d), BF),
            jax.ShapeDtypeStruct((pairs, 2, t, 128), BF),
        ]
        + sums.out_shapes(),
        scratch_shapes=[pltpu.VMEM((2, 2, t, 128), BF), pltpu.SemaphoreType.DMA((2, pairs))] + sums.scratch(),
        compiler_params=pltpu.CompilerParams(
            vmem_limit_bytes=60 << 20, collective_id=collective_id, has_side_effects=True
        ),
        cost_estimate=cost(37e9),
        name=N.attend_back,
    )(q, kv, kvo, up, out, lse, *sums.inputs())


def split_rows(out, rows):
    n = out.shape[0]
    even = jnp.concatenate([out[i : i + rows] for i in range(0, n, 2 * rows)], axis=0).astype(BF)
    odd = jnp.concatenate([out[i + rows : i + 2 * rows] for i in range(0, n, 2 * rows)], axis=0).astype(BF)
    return even, odd


def deliver(out, rows, both):
    both[0], both[1] = split_rows(out, rows)


def grad_dot(a, b):
    return lax.dot_general(a, b, (((0,), (0,)), ((), ())), preferred_element_type=F32)


class Names:
    def __init__(self):
        self.names, self.specs, self.shapes = [], [], []

    def add(self, name, spec, shape=None):
        self.names.append(name)
        self.specs.append(spec)
        self.shapes.append(shape)


class Copies:
    def __init__(self, sems):
        self.sems, self.made = sems, {}

    def add(self, key, src, dst):
        self.made[key] = pltpu.make_async_copy(src, dst, self.sems.at[len(self.made)])

    def start(self, *key):
        self.made[key].start()

    def wait(self, *key):
        self.made[key].wait()


def ffn_kernel(*refs, names, forward, backward, block, chunks, sums):
    r = dict(zip(names, refs))
    if sums is not None:
        place = Place(sums.count)
        parts = sums.parts(
            place, *[[ref for name, ref in r.items() if name.startswith(kind)] for kind in (N.sum_i, N.sum_o, N.sum_s)]
        )
    layer = r[N.layer]
    row = slice(layer, layer + 1)
    j = pl.program_id(0)
    t, d = r[N.att_v].shape
    cut = r[N.wu_v].shape[2]
    count = r[N.wu_v].shape[0]
    first, final = j == 0, j == count - 1
    spans = [slice(i, i + block) for i in range(0, t, block)]
    every = range(len(spans))
    copies = Copies(r[N.sems])
    copies.add((N.wo,), r[N.wo].at[layer], r[N.wo_v])
    for i, at in enumerate(spans):
        copies.add((N.att, i), r[N.att].at[at], r[N.att_v].at[at])
        if forward:
            copies.add((N.x, i), r[N.x].at[at], r[N.x_v].at[at])
            if not backward:
                copies.add((N.next, i), r[N.next_v].at[at], r[N.next].at[at])
            elif at.start < r[N.next].shape[0]:
                copies.add((N.next, i), r[N.next_v].at[at], r[N.next].at[at])
            else:
                low = slice(at.start - r[N.next].shape[0], at.stop - r[N.next].shape[0])
                copies.add((N.next, i), r[N.dz_low].at[low], r[N.next_low].at[low])
            if not backward:
                copies.add((N.middle_o, i), r[N.middle_v].at[at], r[N.middle].at[at])
                copies.add((N.n2_o, i), r[N.n2_v].at[at], r[N.n2].at[at])
        else:
            copies.add((N.middle, i), r[N.middle].at[at], r[N.middle_v].at[at])
            copies.add((N.n2, i), r[N.n2].at[at], r[N.n2_v].at[at])
            copies.add((N.g, i), r[N.g].at[at], r[N.dm_v].at[at])
        if backward:
            copies.add((N.dm, i), r[N.dm_v].at[at], r[N.dm].at[at])
            copies.add((N.da, i), r[N.da_v].at[at], r[N.da].at[at])
    if backward:
        half = r[N.dza].shape[0]
        copies.add((N.dza,), r[N.dza], r[N.dz_v].at[:half])
        if half < t:
            copies.add((N.dzb,), r[N.dzb], r[N.dz_v].at[half:])
    for c in range(count):
        cols = slice(c * cut, (c + 1) * cut)
        copies.add((N.wu, c), r[N.wu].at[layer, :, cols], r[N.wu_v].at[c])
        copies.add((N.wd, c), r[N.wd].at[layer, cols, :], r[N.wd_v].at[c])
        if not (forward and backward):
            for name in (N.act, N.slope):
                for i, at in enumerate(spans):
                    ends = r[name].at[at, cols], r[name + N._v].at[c % 2, at]
                    copies.add((name, c, i), *(ends if backward else ends[::-1]))

    def per_chunk(act):
        for c in range(count):
            pl.when(j == c)(functools.partial(act, c))

    def feed(c):
        for i in every:
            for name in (N.act, N.slope):
                copies.start(name, c, i)

    if sums is not None:
        pl.when(first)(place.greet)

    @pl.when(first)
    def _():
        if forward:
            copies.start(N.wo)
            for i in every:
                copies.start(N.att, i)
                copies.start(N.x, i)
        if backward:
            copies.start(N.dza)
            if half < t:
                copies.start(N.dzb)
        for c in range(count):
            copies.start(N.wu, c)
            copies.start(N.wd, c)
            if c == 0 and not forward:
                feed(0)
                for i in every:
                    copies.start(N.n2, i)
        if not forward:
            for i in every:
                copies.start(N.middle, i)
                copies.start(N.g, i)
                copies.start(N.att, i)
            copies.start(N.wo)
        if forward:
            copies.wait(N.wo)
            for i, at in enumerate(spans):
                copies.wait(N.att, i)
                copies.wait(N.x, i)
                middle = r[N.x_v][at].astype(F32) + (dot(r[N.att_v][at], r[N.wo_v][...], NN) + r[N.bo][row, :])
                unit, _ = normalise(middle)
                r[N.n2_v][at] = (unit * r[N.g2][row, :] + r[N.b2][row, :]).astype(BF)
                r[N.middle_v][at] = middle
                r[N.next_v][at] = middle + r[N.bd][row, :]
                if not backward:
                    copies.start(N.middle_o, i)
                    copies.start(N.n2_o, i)
        if backward:
            r[N.dn_v][...] = jnp.zeros(r[N.dn_v].shape, F32)
            r[N.sums][...] = jnp.zeros(r[N.sums].shape, F32)
            copies.wait(N.dza)
            if half < t:
                copies.wait(N.dzb)
            r[N.sums][0:1, :] = column_sum(r[N.dz_v][...].astype(F32))
            if not forward:
                for i in every:
                    copies.wait(N.n2, i)

    @per_chunk
    def _(c):
        if sums is not None:
            sums.advance(parts, c)
        copies.wait(N.wu, c)
        copies.wait(N.wd, c)
        if not forward:
            if c + 1 < count:
                feed(c + 1)
            for i in every:
                for name in (N.act, N.slope):
                    copies.wait(name, c, i)
        elif not backward and c >= 2:
            for i in every:
                for name in (N.act, N.slope):
                    copies.wait(name, c - 2, i)

    wu, wd = r[N.wu_v].at[j], r[N.wd_v].at[j]
    slot = lax.rem(j, 2)

    def lead(at):
        return (
            dot(r[N.n2_v][at], wu[...], NN) if forward else None,
            dot(r[N.dz_v][at], wd[...], NT) if backward else None,
        )

    ff_sum = 0.0
    ahead = lead(spans[0])
    for i, at in enumerate(spans):
        hidden, da = ahead
        if i + 1 < len(spans):
            ahead = lead(spans[i + 1])
        if forward:
            act, slope = gelu_pair(hidden + r[N.bu][row, :])
            act = act.astype(BF)
            r[N.act_v][slot, at] = act
            if not backward:
                r[N.slope_v][slot, at] = slope.astype(BF)
        else:
            slope = r[N.slope_v][slot, at].astype(F32)
        if backward:
            dh = (da * slope).astype(BF)
            r[N.dh_v][at] = dh
            ff_sum = ff_sum + column_sum(dh.astype(F32))
        if forward:
            r[N.next_v][at] += dot(act, wd[...], NN)
        if backward:
            r[N.dn_v][at] += dot(dh, wu[...], NT)

    if forward:

        @per_chunk
        def _(c):
            for i in every:
                if not backward:
                    copies.start(N.act, c, i)
                    copies.start(N.slope, c, i)
                if c == count - 1:
                    if backward and spans[i].start >= r[N.next].shape[0]:
                        low = slice(spans[i].start - r[N.next].shape[0], spans[i].stop - r[N.next].shape[0])
                        r[N.dz_low][low] = r[N.next_v][spans[i]].astype(BF)
                    copies.start(N.next, i)

    if backward:
        r[N.sums_ff][0:1, :] = ff_sum
        deliver(grad_dot(r[N.act_v][slot], r[N.dz_v][...]), chunks[1], r[N.wd_both])
        deliver(grad_dot(r[N.n2_v][...], r[N.dh_v][...]), chunks[0], r[N.wu_both])

    @pl.when(final)
    def _():
        if sums is not None:
            for stage in range(count, sums.stages):
                sums.advance(parts, stage)
        if backward:
            if not forward:
                copies.wait(N.wo)
            for i, at in enumerate(spans):
                if not forward:
                    copies.wait(N.middle, i)
                    copies.wait(N.g, i)
                    copies.wait(N.att, i)
                g = r[N.dz_v][at].astype(F32) if forward else r[N.dm_v][at]
                unit, inverse = normalise(r[N.middle_v][at])
                up = r[N.dn_v][at]
                r[N.sums][1:2, :] += column_sum(up * unit)
                r[N.sums][2:3, :] += column_sum(up)
                dm = g + norm_back(up, r[N.g2][row, :], unit, inverse)
                r[N.dm_v][at] = dm
                copies.start(N.dm, i)
                dy = dm.astype(BF)
                r[N.dh_v][at] = dy
                r[N.sums][3:4, :] += column_sum(dy.astype(F32))
                r[N.da_v][at] = dot(dy, r[N.wo_v][...], NT).astype(BF)
                copies.start(N.da, i)
            deliver(grad_dot(r[N.att_v][...], r[N.dh_v][...]), chunks[0], r[N.wo_both])
        for i in every:
            if forward:
                copies.wait(N.next, i)
                if not backward:
                    copies.wait(N.middle_o, i)
                    copies.wait(N.n2_o, i)
                    for c in range(max(0, count - 2), count):
                        copies.wait(N.act, c, i)
                        copies.wait(N.slope, c, i)
            if backward:
                copies.wait(N.dm, i)
                copies.wait(N.da, i)
        if sums is not None:
            sums.advance(parts, sums.stages)


def ffn_call(layer, devices, arrays, weights, forward, backward, sums=None, collective_id=0):
    t, d = arrays[N.att].shape
    ff = weights[N.wu].shape[2]
    cut, count = d, ff // d
    block = min(2 * BLOCK, t // 2)
    once = pl.Buffered(1)
    ins, outs, scratch = Names(), Names(), Names()
    hbm = pl.BlockSpec(memory_space=pl.ANY)

    def whole(shape):
        return pl.BlockSpec(shape, lambda j: (0,) * len(shape), pipeline_mode=once)

    vec = pl.BlockSpec(memory_space=pltpu.VMEM)
    for name in (N.att, N.wo, N.wu, N.wd):
        ins.add(name, hbm)
    ins.add(N.g2, vec)
    scratch.add(N.att_v, pltpu.VMEM((t, d), BF))
    scratch.add(N.wo_v, pltpu.VMEM((d, d), BF))
    scratch.add(N.wu_v, pltpu.VMEM((count, d, cut), BF))
    scratch.add(N.wd_v, pltpu.VMEM((count, cut, d), BF))
    scratch.add(N.middle_v, pltpu.VMEM((t, d), F32))
    scratch.add(N.n2_v, pltpu.VMEM((t, d), BF))
    scratch.add(N.act_v, pltpu.VMEM((2, t, cut), BF))
    if not (forward and backward):
        scratch.add(N.slope_v, pltpu.VMEM((2, t, cut), BF))
    if forward:
        ins.add(N.x, hbm)
        for name in (N.bo, N.b2, N.bd):
            ins.add(name, vec)
        ins.add(N.bu, pl.BlockSpec((weights[N.bu].shape[0], cut), lambda j: (0, j)))
        outs.add(N.next, hbm, ((t // 2 if backward else t, d), F32))
        if backward:
            outs.add(N.next_low, hbm, ((t // 2, d), BF))
            scratch.add(N.dz_low, pltpu.VMEM((t // 2, d), BF))
        scratch.add(N.x_v, pltpu.VMEM((t, d), arrays[N.x].dtype))
        scratch.add(N.next_v, pltpu.VMEM((t, d), F32))
    if backward:
        for name in (N.dza, N.dzb) if N.dzb in arrays else (N.dza,):
            ins.add(name, hbm)
        if not forward:
            for name in (N.g, N.middle, N.n2, N.act, N.slope):
                ins.add(name, hbm)
        outs.add(N.dm, hbm, ((t, d), F32))
        outs.add(N.da, hbm, ((t, d), BF))
        outs.add(N.sums, whole((8, d)), ((8, d), F32))
        outs.add(N.sums_ff, pl.BlockSpec((8, cut), lambda j: (0, j)), ((8, ff), F32))
        outs.add(N.wo_both, whole((2, d // 2, d)), ((2, d // 2, d), BF))
        outs.add(N.wu_both, pl.BlockSpec((2, d // 2, cut), lambda j: (0, 0, j)), ((2, d // 2, ff), BF))
        outs.add(N.wd_both, pl.BlockSpec((2, cut // 2, d), lambda j: (0, j, 0)), ((2, ff // 2, d), BF))
        scratch.add(N.dz_v, pltpu.VMEM((t, d), BF))
        scratch.add(N.dn_v, pltpu.VMEM((t, d), F32))
        scratch.add(N.dh_v, pltpu.VMEM((t, d), BF))
        scratch.add(N.dm_v, pltpu.VMEM((t, d), F32))
        scratch.add(N.da_v, pltpu.VMEM((t, d), BF))
    else:
        outs.add(N.middle, hbm, ((t, d), F32))
        outs.add(N.n2, hbm, ((t, d), BF))
        outs.add(N.act, hbm, ((t, ff), BF))
        outs.add(N.slope, hbm, ((t, ff), BF))
    scratch.add(N.sems, pltpu.SemaphoreType.DMA((3 + 2 * count + (t // block) * (6 + 2 * count),)))
    everything = {**weights, **arrays}
    if sums is not None:
        for i, (array, spec) in enumerate(zip(sums.inputs(), sums.in_specs())):
            ins.add(tag(N.sum_i, i), spec)
            everything[tag(N.sum_i, i)] = array
        for i, (shape, spec) in enumerate(zip(sums.out_shapes(), sums.out_specs())):
            outs.add(tag(N.sum_o, i), spec, (shape.shape, shape.dtype))
        for i, shape in enumerate(sums.scratch()):
            scratch.add(tag(N.sum_s, i), shape)
    if sums is None:
        compiler_params = params(62)
    else:
        compiler_params = pltpu.CompilerParams(
            vmem_limit_bytes=62 << 20, collective_id=collective_id, has_side_effects=True
        )

    def kernel(*refs, names):
        ffn_kernel(
            layer,
            *refs,
            names=[N.layer] + names,
            forward=forward,
            backward=backward,
            block=block,
            chunks=(d // devices, ff // devices),
            sums=sums,
        )

    found = pl.pallas_call(
        functools.partial(kernel, names=ins.names + outs.names + scratch.names),
        grid=(count,),
        in_specs=ins.specs,
        out_specs=outs.specs,
        out_shape=[jax.ShapeDtypeStruct(*shape) for shape in outs.shapes],
        scratch_shapes=scratch.specs,
        compiler_params=compiler_params,
        cost_estimate=cost((10e9 if forward else 0) + (18e9 if backward else 0)),
        name=N.feed_forward + (N._both if forward and backward else N._back if backward else ""),
    )(*[everything[name] for name in ins.names])
    return dict(zip(outs.names, found))


N_VECTORS = 12


def joined_back_kernel(*refs, names, layer, rows, block, sums):
    r = dict(zip(names, refs))
    last = sums is not None
    t, d = r[N.x_v].shape
    spans = [slice(i, i + block) for i in range(0, t, block)]
    half = len(spans) // 2
    order = list(range(half, len(spans))) + list(range(half)) if last else list(range(len(spans)))
    copies = Copies(r[N.sems])
    copies.add((N.weight,), r[N.weight].at[layer], r[N.weight_v])
    for i, at in enumerate(spans):
        for name in (N.dq, N.x, N.dm, N.normed):
            copies.add((name, i), r[name].at[at], r[name + N._v].at[at])
        copies.add((N.dkv, i), r[N.dkv].at[:, at], r[N.dkv_v].at[:, at])
        copies.add((N.dkvi, i), r[N.dkvi].at[:, :, at], r[N.dkvi_v].at[:, :, at])
        if not last or i < half:
            copies.add((N.g, i), r[N.dm_v].at[at], r[N.g].at[at])
        if not last:
            copies.add((N.low, i), r[N.low_v].at[at], r[N.low].at[at])
    for i in order:
        for name in (N.dq, N.dkv, N.dkvi):
            copies.start(name, i)
        if not last:
            if i == order[0]:
                copies.start(N.weight)
            for name in (N.x, N.dm):
                copies.start(name, i)
    if last:
        for i in order:
            copies.start(N.normed, i)
        copies.start(N.weight)
        for i in order:
            for name in (N.x, N.dm):
                copies.start(name, i)
        place = Place(sums.count)
        parts = sums.parts(
            place, [], [ref for name, ref in r.items() if name.startswith(N.sum_o)], [ref for name, ref in r.items() if name.startswith(N.sum_s)]
        )
        trade = Trade(place, r[N.low_v].at[t // 2 :], r[N.got], r[N.trade_sems])
    else:
        for i in order:
            copies.start(N.normed, i)
    totals = [0.0] * 4

    def gather(i):
        at = spans[i]
        for name in (N.dq, N.dkv, N.dkvi):
            copies.wait(name, i)
        r[N.df_v][at, :d] = r[N.dq_v][at]
        for k in range(2):
            got = jnp.concatenate([r[N.dkvi_v][h, k, at] for h in range(d // 128)], axis=1)
            cols = slice((k + 1) * d, (k + 2) * d)
            r[N.df_v][at, cols] = (r[N.dkv_v][k, at].astype(F32) + got.astype(F32)).astype(BF)

    def back(i):
        at = spans[i]
        up = dot(r[N.df_v][at], r[N.weight_v][...], NT)
        copies.wait(N.x, i)
        copies.wait(N.dm, i)
        unit, inverse = normalise(r[N.x_v][at].astype(F32))
        found = (up * unit, up, r[N.df_v][at, :d].astype(F32), r[N.df_v][at, 2 * d :].astype(F32))
        for k in range(4):
            totals[k] = totals[k] + column_sum(found[k])
        g = r[N.dm_v][at] + norm_back(up, r[N.gain][layer : layer + 1, :], unit, inverse)
        r[N.dm_v][at] = g
        r[N.low_v][at] = g.astype(BF)
        if not last or i < half:
            copies.start(N.g, i)
        if not last:
            copies.start(N.low, i)

    def product(k):
        return grad_dot(r[N.normed_v][...], r[N.df_v][:, k * d : (k + 1) * d])

    if not last:
        copies.wait(N.weight)
        for i in order:
            gather(i)
            back(i)
        for i in order:
            copies.wait(N.normed, i)
        for k, total in enumerate(totals):
            r[N.sums][k : k + 1, :] = total
        for k in range(3):
            deliver(product(k), rows, r[N.both].at[:, :, k * d : (k + 1) * d])
    else:
        vectors = r[N.vectors]

        def swap(stage):
            return pltpu.make_async_remote_copy(
                src_ref=r[N.vectors_s].at[stage],
                dst_ref=r[N.vectors_v].at[stage],
                send_sem=r[N.vector_sems].at[0, stage],
                recv_sem=r[N.vector_sems].at[1, stage],
                device_id=place.partner(path[stage]),
                device_id_type=pl.DeviceIdType.MESH,
            )

        path = [0] + list(range(2, sums.stages)) + [1]

        def send_vectors(stage):
            if stage > 0:
                swap(stage - 1).wait()
                vectors[...] += r[N.vectors_v][stage - 1]
            if stage < sums.stages:
                r[N.vectors_s][stage] = vectors[...]
                swap(stage).start()

        for i in order:
            gather(i)
        for i in order:
            copies.wait(N.normed, i)
        each = len(parts) // 3
        for k in range(3):
            made = product(k)
            for n in range(each):
                parts[each * k + n].fill(made[:, n * (d // each) : (n + 1) * (d // each)], rows)
                if k == n == 0:
                    place.greet()
                parts[each * k + n].begin(0)
        copies.wait(N.weight)
        for i in order[:half]:
            back(i)
        trade.copy().start()
        sums.advance(parts, 1)
        for i in order[half:]:
            back(i)
        for k, total in enumerate(totals):
            vectors[k : k + 1, :] = total
        for l in range(2):
            base = N_VECTORS * l
            if l > 0:
                vectors[base : base + 4, :] = r[N.sums_in][0:4, :]
            vectors[base + 4 : base + 8, :] = r[tag(N.sums, l)][0:4, :]
            for k in range(4):
                vectors[base + 8 + k : base + 9 + k, :] = r[tag(N.sums_ff, l)][0:1, k * d : (k + 1) * d]
        send_vectors(0)
        for stage in range(1, sums.stages + 1):
            if stage > 1:
                sums.advance(parts, stage)
            send_vectors(stage)
        trade.copy().wait()
    for i in order:
        if not last or i < half:
            copies.wait(N.g, i)
        if not last:
            copies.wait(N.low, i)


def joined_back_call(arrays, layer, devices, sums=None, collective_id=0):
    t, d = arrays[N.x].shape
    last = sums is not None
    block = min(BLOCK, t // 2)
    ins, outs, scratch = Names(), Names(), Names()
    hbm = pl.BlockSpec(memory_space=pl.ANY)
    vmem = pl.BlockSpec(memory_space=pltpu.VMEM)
    for name in (N.dq, N.dkv, N.dkvi, N.x, N.dm, N.normed, N.weight):
        ins.add(name, hbm)
        shape = arrays[name].shape
        scratch.add(name + N._v, pltpu.VMEM(shape[1:] if name == N.weight else shape, arrays[name].dtype))
    ins.add(N.gain, vmem)
    scratch.add(N.df_v, pltpu.VMEM((t, 3 * d), BF))
    scratch.add(N.low_v, pltpu.VMEM((t, d), BF))
    outs.add(N.g, hbm, ((t // 2 if last else t, d), F32))
    if last:
        for name in (N.sums_in, *(tag(x, l) for x in (N.sums, N.sums_ff) for l in range(2))):
            ins.add(name, vmem)
        outs.add(N.got, hbm, ((t // 2, d), BF))
        outs.add(N.vectors, vmem, ((2 * N_VECTORS, d), F32))
        for i, (shape, spec) in enumerate(zip(sums.out_shapes(), sums.out_specs())):
            outs.add(tag(N.sum_o, i), vmem, (shape.shape, shape.dtype))
        for i, shape in enumerate(sums.scratch()):
            scratch.add(tag(N.sum_s, i), shape)
        for name in (N.vectors_s, N.vectors_v):
            scratch.add(name, pltpu.VMEM((sums.stages, 2 * N_VECTORS, d), F32))
        scratch.add(N.vector_sems, pltpu.SemaphoreType.DMA((2, sums.stages)))
        scratch.add(N.trade_sems, pltpu.SemaphoreType.DMA((2,)))
        compiler_params = pltpu.CompilerParams(
            vmem_limit_bytes=62 << 20, collective_id=collective_id, has_side_effects=True
        )
    else:
        outs.add(N.low, hbm, ((t, d), BF))
        outs.add(N.sums, vmem, ((8, d), F32))
        outs.add(N.both, vmem, ((2, d // 2, 3 * d), BF))
        compiler_params = params(62)
    scratch.add(N.sems, pltpu.SemaphoreType.DMA((1 + (t // block) * 8,)))
    found = pl.pallas_call(
        functools.partial(
            joined_back_kernel,
            names=ins.names + outs.names + scratch.names,
            layer=layer,
            rows=d // devices,
            block=block,
            sums=sums,
        ),
        grid=(1,),
        in_specs=ins.specs,
        out_specs=outs.specs,
        out_shape=[jax.ShapeDtypeStruct(*shape) for shape in outs.shapes],
        scratch_shapes=scratch.specs,
        compiler_params=compiler_params,
        cost_estimate=cost(18e9 if last else 8e9),
        name=N.joined_back + (N._sums if last else ""),
    )(*[arrays[name] for name in ins.names])
    return dict(zip(outs.names, found))


def finish_kernel(*refs, names, devices):
    r = dict(zip(names, refs))
    place = Place(devices)
    chip, index = place.bit(1), place.dp * 4 + place.seq
    copies, moves = Copies(r[N.sems]), []
    for cells in (N.block, N.input):
        moves.append((cells + N._got, None, None))
        moves.append((cells + N._own, cells + N._out, chip))
    for m in range(4):
        for l in range(2):
            moves.append((tag(N.m, m, l), tag(N.mat, m), l))
    for name, out, at in moves:
        copies.add((name, 0), r[name], r[name + N._v])
        if out is not None:
            copies.add((name, 1), r[name + N._v], r[out].at[at])
    for cells in (N.block, N.input):
        copies.add((cells,), r[cells + N._wide], r[cells + N._out].at[1 - chip])
    for name, _, _ in moves:
        copies.start(name, 0)
    for name, out, _ in moves:
        copies.wait(name, 0)
        if out is not None:
            copies.start(name, 1)
        else:
            cells = N.block if name == N.block_got else N.input
            r[cells + N._wide][...] = r[name + N._v][...].astype(F32)
            copies.start(cells)
    v = r[N.vectors]
    d = v.shape[1]
    piece = d // devices

    def cut(x, start, width):
        return pltpu.roll(x, lax.rem(d - start, d), 1)[:, :width]

    for l in range(2):
        mine = v[N_VECTORS * l : N_VECTORS * l + 8, :]
        ff = v[N_VECTORS * l + 8 : N_VECTORS * l + 12, :]
        rows = cut(mine, index * piece, piece)
        for name, k in ((N.v0, 0), (N.v1, 1), (N.v4, 7), (N.v5, 5), (N.v6, 6), (N.v8, 4)):
            r[name][l : l + 1, :] = rows[k : k + 1]
        per = devices // 2
        qv = cut(mine, lax.rem(index, per) * (2 * piece), 2 * piece)
        r[N.qv][l : l + 1, :] = jnp.where(index < per, qv[2:3], qv[3:4])
        per = devices // 4
        up = cut(ff, lax.rem(index, per) * (4 * piece), 4 * piece)
        at = index // per
        r[N.up][l : l + 1, :] = jnp.where(
            at < 2, jnp.where(at == 0, up[0:1], up[1:2]), jnp.where(at == 2, up[2:3], up[3:4])
        )
    for name, out, _ in moves:
        if out is not None:
            copies.wait(name, 1)
    copies.wait(N.block)
    copies.wait(N.input)


def finish_call(arrays, devices, genes, ff):
    d = arrays[N.vectors].shape[1]
    piece = d // devices
    ins, outs, scratch = Names(), Names(), Names()
    hbm = pl.BlockSpec(memory_space=pl.ANY)
    vmem = pl.BlockSpec(memory_space=pltpu.VMEM)
    for name, array in arrays.items():
        ins.add(name, vmem if name == N.vectors else hbm)
        if name != N.vectors:
            scratch.add(name + N._v, pltpu.VMEM(array.shape, array.dtype))
    for cells in (N.block, N.input):
        outs.add(cells + N._out, hbm, ((2, genes, d), F32))
        scratch.add(cells + N._wide, pltpu.VMEM((genes, d), F32))
    for m in range(4):
        outs.add(tag(N.mat, m), hbm, ((2,) + arrays[tag(N.m, m, 0)].shape, F32))
    for name in (N.v0, N.v1, N.v4, N.v5, N.v6, N.v8):
        outs.add(name, vmem, ((2, piece), F32))
    outs.add(N.qv, vmem, ((2, 2 * piece), F32))
    outs.add(N.up, vmem, ((2, ff // devices), F32))
    scratch.add(N.sems, pltpu.SemaphoreType.DMA((24,)))
    found = pl.pallas_call(
        functools.partial(finish_kernel, names=ins.names + outs.names + scratch.names, devices=devices),
        grid=(1,),
        in_specs=ins.specs,
        out_specs=outs.specs,
        out_shape=[jax.ShapeDtypeStruct(*shape) for shape in outs.shapes],
        scratch_shapes=scratch.specs,
        compiler_params=params(62),
        cost_estimate=cost(2e9),
        name=N.finish,
    )(*[arrays[name] for name in ins.names])
    return dict(zip(outs.names, found))


def on_device(
    device_count,
    cell_tokens,
    first_gain,
    first_bias,
    joined_weight,
    query_value_bias,
    output_weight,
    output_bias,
    second_gain,
    second_bias,
    up_weight,
    up_bias,
    down_weight,
    down_bias,
    cotangent,
    gene_mask,
):
    _, genes, d = cell_tokens.shape
    layers = joined_weight.shape[0]
    seq = lax.axis_index(N.seq)
    across = [(0, 2), (1, 3), (2, 0), (3, 1)]

    x = cell_tokens
    weights = dict(
        wo=output_weight,
        wu=up_weight,
        wd=down_weight,
        bo=output_bias,
        g2=second_gain,
        b2=second_bias,
        bu=up_bias,
        bd=down_bias,
    )
    chunks = device_count
    saved = []
    for layer in range(layers):
        top = layer == layers - 1
        seeds = (cotangent, gene_mask) if layer == 0 else ()
        joined = qkv_call(x, layer, chunks, first_gain, first_bias, joined_weight, query_value_bias, 2 * layers + 1 + layer, seeds)
        if seeds:
            g = joined[N.seed_own], lax.ppermute(joined[N.seed_send], N.seq, across)
        normed, q, kv, kvo = (joined[name] for name in (N.normed, N.q, N.kv, N.kvo))
        x = joined.get(N.held, x)
        att, lse = attend_call(q, kv, kvo)
        arrays = dict(att=att, x=x)
        if top:
            arrays.update(dza=g[0], dzb=g[1])
        found = ffn_call(layer, chunks, arrays, weights, True, top)
        saved.append((x, normed, q, kv, kvo, att, lse, found))
        x = found[N.next]

    dp_bits = list(range(2, device_count.bit_length() - 1))
    orders = (
        [1] + dp_bits,
        dp_bits + [1],
        dp_bits[1:-1] + [1] + dp_bits[:1] + dp_bits[-1:],
    )

    def job(both):
        split = (2, chunks // 2, 2 * both.shape[1] // chunks, both.shape[2])
        return Job(both.reshape(split), device_count, orders)

    final = {}
    waiting, back = None, None
    for layer in reversed(range(layers)):
        x, normed, q, kv, kvo, att, lse, found = saved[layer]
        top, bottom = layer == layers - 1, layer == 0
        if not top:
            arrays = dict(att=att, g=back[N.g], dza=back[N.low], **{k: found[k] for k in (N.middle, N.n2, N.act, N.slope)})
            found = ffn_call(layer, chunks, arrays, weights, False, True, Sums([waiting], device_count), layers + layer)
            final[tag(N.m, 0, layer + 1)] = found[tag(N.sum_o, 0)]
        jobs = [job(found[w + N._both]) for w in (N.wo, N.wu, N.wd)]
        trade_out = found[N.next_low] if top else None
        dq, dkv, dkvi, *done = attend_back_call(
            q, kv, kvo, found[N.da], att, lse, Sums(jobs, device_count, trade_out, 3), layer
        )
        if top:
            final[N.block_own], final[N.block_got] = found[N.next], done.pop()
        for i in range(3):
            final[tag(N.m, i + 1, layer)] = done[i]
        final[tag(N.sums, layer)], final[tag(N.sums_ff, layer)] = found[N.sums], found[N.sums_ff]
        arrays = dict(
            dq=dq, dkv=dkv, dkvi=dkvi, x=x, dm=found[N.dm], normed=normed, weight=joined_weight, gain=first_gain
        )
        if bottom:
            arrays.update(sums_in=back[N.sums])
            for l in range(2):
                arrays.update({tag(N.sums, l): final.pop(tag(N.sums, l)), tag(N.sums_ff, l): final.pop(tag(N.sums_ff, l))})
            late = (
                dp_bits[:-1] + [1] + dp_bits[-1:],
                dp_bits[1:-1] + dp_bits[:1] + [1] + dp_bits[-1:],
            ) * 3
            made = Job(None, device_count, late, (d // chunks, 3 * d))
            back = joined_back_call(arrays, layer, chunks, Sums([made], device_count), 2 * layers)
        else:
            back = joined_back_call(arrays, layer, chunks)
            waiting = job(back[N.both])
    final.update(
        **{tag(N.m, 0, 0): back[tag(N.sum_o, 0)]}, input_own=back[N.g], input_got=back[N.got], vectors=back[N.vectors]
    )
    out = finish_call(final, device_count, genes, up_bias.shape[1])
    return tuple(
        out[name]
        for name in (
            N.block_out,
            N.input_out,
            N.v0,
            N.v1,
            tag(N.mat, 0),
            N.qv,
            tag(N.mat, 1),
            N.v4,
            N.v5,
            N.v6,
            tag(N.mat, 2),
            N.up,
            tag(N.mat, 3),
            N.v8,
        )
    )


def solution(mesh):
    split = P(None, (N.dp, N.seq))
    split_rows = P(None, (N.dp, N.seq), None)
    tokens = P(N.dp, N.seq, None)
    return jax.shard_map(
        functools.partial(on_device, mesh.size),
        mesh=mesh,
        in_specs=(tokens,) + (P(),) * 12 + (tokens, P(N.dp, N.seq)),
        out_specs=(
            tokens,
            tokens,
            split,
            split,
            split_rows,
            split,
            split_rows,
            split,
            split,
            split,
            split_rows,
            split,
            split_rows,
            split,
        ),
        check_vma=False,
    )
```
